512 devices in a mesh: dp: 4 (over x), ctx: 16 (over z), tp: 8 (over y, core).
Axes of the slice: x: 4, y: 4, z: 16, core: 2. Of those that a mesh axis runs over, the one named last changes fastest.
Arguments:
- inputs: bfloat16 [4, 4096, 8192], P('dp', 'ctx', 'tp'), may hold values from -6 to 6
- cotangent: bfloat16 [4, 4096, 8192], P('dp', 'ctx', 'tp'), may hold values from -6 to 6
- residues: float32 [512, 16], P('tp'), may hold values from -3 to 3
- decay_rates: float32 [512, 16], P('tp'), may hold values from 4.8828125e-05 to 0.0333333333
- skip_gain: float32 [8192], P('tp'), may hold values from -1 to 1
Outputs:
- outputs: bfloat16 [4, 4096, 8192], P('dp', 'ctx', 'tp')
- grad_inputs: bfloat16 [4, 4096, 8192], P('dp', 'ctx', 'tp')
- grad_residues: float32 [512, 16], P('tp')
- grad_skip: float32 [8192], P('tp')
The draws below stay inside these ranges and needn't reach their ends.
All inputs are finite; a program needn't handle non-finite values.
Results may differ from the reference program's by a relative error of at most 0.0014.
Values sent between devices are 32-bit elements; how exact they have to be, the bound alone decides.
A program may use at most 64 MiB of HBM per device.

```python
import math
import jax
import jax.numpy as jnp
from jax import lax

D = 8192
MODES = 16
BATCH = 4
SEQ = 4096
GROUPS = 512
TOKENS = 16384


def draw_decay_rates(key, part):
    key_pick, key_slow, key_fast = jax.random.split(jax.random.fold_in(key, 17), 3)
    slow_share = 0.5
    slow_pick = jax.random.uniform(key_pick, (GROUPS, MODES), dtype=jnp.float32) < slow_share
    slow_rates = jnp.exp(jax.random.uniform(key_slow, (GROUPS, MODES), dtype=jnp.float32, minval=jnp.log(0.2 / SEQ), maxval=jnp.log(2.0 / SEQ)))
    fast_rates = jnp.exp(jax.random.uniform(key_fast, (GROUPS, MODES), dtype=jnp.float32, minval=jnp.log(2.0 / SEQ), maxval=jnp.log(1.0 / 30.0)))
    return jnp.where(slow_pick, slow_rates, fast_rates).astype(jnp.float32)


def level_of(own_key, extent, shards, low, largest):
    def one(position, shards_of):
        draws = jax.random.uniform(jax.random.fold_in(jax.random.fold_in(own_key, 6), position), (shards_of,), jnp.float32, low / len(shards), largest / len(shards))
        return jnp.repeat(jnp.exp(draws), extent[position] // shards_of).reshape((-1,) + (1,) * (len(extent) - position - 1))

    level = one(*shards[0])
    for cut in shards[1:]:
        level = level * one(*cut)
    return level


def normal_values(rng, dims, spread, limit, shards=(), kind=jnp.bfloat16):
    level = level_of(rng, dims, shards, -0.22, 0.18) if shards else 1.0
    array = jax.random.normal(rng, dims, jnp.float32) * spread * level
    return jnp.minimum(jnp.maximum(array, -limit), limit).astype(kind)


def setup_inputs(seed: int = 0) -> dict:
    splits = jax.random.split(jax.random.key(seed), 6)
    return {
        "inputs": normal_values(splits[0], (BATCH, SEQ, D), 1.0, 6.0, ((0, 4), (1, 16), (2, 8))),
        "cotangent": normal_values(splits[1], (BATCH, SEQ, D), 1.0, 6.0, ((0, 4), (1, 16), (2, 8))),
        "residues": normal_values(splits[2], (GROUPS, MODES), 0.5, 3.0, ((0, 8),), jnp.float32),
        "decay_rates": draw_decay_rates(jax.random.fold_in(splits[5], 71), 0),
        "skip_gain": jnp.clip(jax.random.uniform(splits[4], (D,), jnp.float32, -1.0, 1.0) * level_of(splits[4], (D,), ((0, 8),), -0.4, 0.0), -1.0, 1.0),
    }


highest = lax.Precision.HIGHEST

def reference(inputs, cotangent, residues, decay_rates, skip_gain):
    block_rows = math.gcd(64, SEQ)
    block_count = SEQ // block_rows
    group_count, mode_count = residues.shape
    channels = inputs.shape[2]
    group_width = channels // group_count
    weight = jnp.sqrt(1.0 - jnp.exp(-2.0 * decay_rates))
    coefficient = residues * weight
    positions = jnp.arange(block_rows, dtype=jnp.float32)
    center = (block_rows - 1) / 2.0
    rate_cube = decay_rates[:, :, None]
    decay_down = jnp.exp(-rate_cube * (positions - center))
    decay_up = jnp.exp(rate_cube * (positions - center))
    from_start = jnp.exp(-rate_cube * positions)
    to_end = jnp.exp(-rate_cube * (block_rows - 1.0 - positions))
    first_weights = coefficient[:, :, None] * jnp.exp(-rate_cube * (positions + 1.0))
    last_weights = coefficient[:, :, None] * jnp.exp(-rate_cube * (block_rows - positions))
    causal_mask = positions[:, None] >= positions[None, :]
    kernel = jnp.where(causal_mask, jnp.einsum('gm,gmt,gms->gts', coefficient, decay_down, decay_up, precision=highest), 0.0)
    block_passing = jnp.exp(-decay_rates.T[:, :, None] * float(block_rows))
    skip_wide = skip_gain.reshape(group_count, group_width)
    one_step = jnp.exp(-decay_rates)

    def one_sequence(pair):
        sequence, back_row = pair
        split_x = sequence.reshape(block_count, block_rows, group_count, group_width)
        split_d = back_row.reshape(block_count, block_rows, group_count, group_width)

        def forward_turn(carried, pieces):
            state_in, grad_total = carried
            half_x, half_d = pieces
            wide_x = half_x.astype(jnp.float32)
            wide_d = half_d.astype(jnp.float32)
            local_out = jnp.einsum('gts,sgc->tgc', kernel, wide_x, precision=highest)
            carried_out = jnp.einsum('gmt,mgc->tgc', first_weights, state_in, precision=highest)
            local_back = jnp.einsum('gts,tgc->sgc', kernel, wide_d, precision=highest)
            pairs = jnp.einsum('tgc,sgc->gts', half_d, half_x, preferred_element_type=jnp.float32)
            pairs = jnp.where(causal_mask, pairs, 0.0)
            local_grad = weight * jnp.einsum('gmt,gts,gms->gm', decay_down, pairs, decay_up, precision=highest)
            start_state = jnp.einsum('gmt,tgc->mgc', from_start, wide_d, precision=highest)
            cross_grad = weight * one_step * jnp.einsum('mgc,mgc->gm', start_state, state_in, precision=highest)
            end_state = jnp.einsum('gmt,tgc->mgc', to_end, wide_x, precision=highest)
            state_out = state_in * block_passing + end_state
            return ((state_out, grad_total + local_grad + cross_grad), (local_out + carried_out + skip_wide * wide_x, local_back + skip_wide * wide_d, start_state))
        empty_state = jnp.zeros((mode_count, group_count, group_width), jnp.float32)
        empty_grad = jnp.zeros((group_count, mode_count), jnp.float32)
        final_pair, stacked = lax.scan(forward_turn, (empty_state, empty_grad), (split_x, split_d))
        forward_out, backward_local, start_states = stacked

        def backward_turn(carried, local_start):
            return (carried * block_passing + local_start, carried)
        final_state, after_states = lax.scan(backward_turn, empty_state, start_states, reverse=True)
        carried_back = jnp.einsum('gmt,kmgc->ktgc', last_weights, after_states, precision=highest)
        result_out = forward_out.reshape(SEQ, channels).astype(jnp.bfloat16)
        result_back = (backward_local + carried_back).reshape(SEQ, channels).astype(jnp.bfloat16)
        return (result_out, result_back, final_pair[1])
    outputs, grad_inputs, grad_parts = lax.map(one_sequence, (inputs, cotangent))
    scale = 1.0 / math.sqrt(TOKENS)
    grad_residues = lax.optimization_barrier(jnp.sum(grad_parts, axis=0)) * scale
    grad_skip = jnp.einsum('btc,btc->c', inputs.astype(jnp.float32), cotangent.astype(jnp.float32), precision=highest) * scale
    return (outputs, grad_inputs, grad_residues, grad_skip)
```

```python
import functools
import math

import jax
import jax.numpy as jnp
import numpy as np
from jax import lax
from jax.experimental import pallas as pl
from jax.experimental.pallas import tpu as pltpu
from jax.sharding import PartitionSpec as P

MESH = pl.DeviceIdType.MESH
highest = lax.Precision.HIGHEST
f32 = jnp.float32
bf16 = jnp.bfloat16


def split(value):
    high = value.astype(bf16)
    return high, (value - high.astype(f32)).astype(bf16)


def times(left, right):
    total = jnp.dot(left[0], right[0], preferred_element_type=f32)
    total += jnp.dot(left[0], right[1], preferred_element_type=f32)
    return total + jnp.dot(left[1], right[0], preferred_element_type=f32)


def kernel(sizes, x_hbm, d_hbm, res_hbm, rate_hbm, skip_hbm, fwd_hbm, inv_hbm, trig_hbm,
           y_ref, z_ref, gres_ref, gskip_ref,
           x_ref, d_ref, res_ref, rate_ref, skip_ref, fwd_ref, inv_ref, trig_ref,
           wf_ref, wb_ref, h_ref, ylocal, zlocal, states, coefs, packs, e_send, e_recv, s_send, s_recv,
           g_send, g_recv, p_send, p_recv, o_send, o_recv, load_sem, send_sem, recv_sem, psend_sem, precv_sem):
    nctx, ndp, rows, channels, groups, modes, scale = sizes
    half = rows // 2
    tiles = channels // 256
    me = lax.axis_index("ctx")
    mine = lax.axis_index("dp")

    barrier = pltpu.get_barrier_semaphore()

    def greet(step, carried):
        pl.semaphore_signal(barrier, inc=1, device_id={"ctx": lax.rem(me + step, nctx)}, device_id_type=MESH)
        return carried

    lax.fori_loop(1, nctx, greet, 0)
    for step in range(1, ndp):
        pl.semaphore_signal(barrier, inc=1, device_id={"dp": lax.rem(mine + step, ndp)}, device_id_type=MESH)

    loads = [
        pltpu.make_async_copy(source, target, load_sem.at[number])
        for number, (source, target) in enumerate(
            [(rate_hbm, rate_ref), (res_hbm, res_ref), (x_hbm.at[0], x_ref), (d_hbm.at[0], d_ref), (trig_hbm, trig_ref),
             (fwd_hbm, fwd_ref), (inv_hbm, inv_ref), (skip_hbm, skip_ref)]
        )
    ]
    for load in loads:
        load.start()

    block_ones = lax.broadcasted_iota(jnp.int32, (256, 256), 0) // modes == lax.broadcasted_iota(jnp.int32, (256, 256), 1) // modes
    ones = block_ones.astype(bf16)
    lanes = lax.broadcasted_iota(jnp.int32, (8, 128), 1)
    lower = lanes < 64
    lower_row = lax.broadcasted_iota(jnp.int32, (1, 128), 1) < 64
    positions = lax.broadcasted_iota(jnp.int32, (rows, 1), 0).astype(f32)

    spread = (
        lax.broadcasted_iota(jnp.int32, (modes, channels), 1) % modes == lax.broadcasted_iota(jnp.int32, (modes, channels), 0)
    ).astype(f32)
    own_group = (
        lax.broadcasted_iota(jnp.int32, (groups, channels), 1) // modes == lax.broadcasted_iota(jnp.int32, (groups, channels), 0)
    )
    own_mode = (
        lax.broadcasted_iota(jnp.int32, (modes, channels), 1) % modes == lax.broadcasted_iota(jnp.int32, (modes, channels), 0)
    )

    def as_row(array):
        wide = jnp.dot(array, spread, precision=highest, preferred_element_type=f32)
        return jnp.sum(jnp.where(own_group, wide, 0.0), axis=0, keepdims=True)

    def by_channel(row):
        wide = jnp.where(own_mode, row, 0.0)
        return jnp.concatenate(
            [
                jnp.dot(wide[:, 256 * q : 256 * q + 256], ones.astype(f32), precision=highest, preferred_element_type=f32)
                for q in range(tiles)
            ],
            axis=1,
        )

    def pack(array, target):
        for pair in range(nctx // 2):
            low = array[0:8, 128 * pair : 128 * pair + 128]
            high = array[8:16, 128 * pair : 128 * pair + 128]
            target[2 * pair] = jnp.where(lower, low, pltpu.roll(high, 64, 1))
            target[2 * pair + 1] = jnp.where(lower, pltpu.roll(low, 64, 1), high)

    def unpack(source):
        lows, highs = [], []
        for pair in range(nctx // 2):
            first, second = source[2 * pair], source[2 * pair + 1]
            lows.append(jnp.where(lower, first, pltpu.roll(second, 64, 1)))
            highs.append(jnp.where(lower, pltpu.roll(first, 64, 1), second))
        return jnp.concatenate([jnp.concatenate(lows, axis=1), jnp.concatenate(highs, axis=1)], axis=0)

    def on_blocks(array, q):
        piece = array[:, 256 * q : 256 * q + 256]
        return jnp.where(block_ones, jnp.concatenate([piece] * (256 // modes), axis=0), 0.0)

    def off_blocks(array):
        return jnp.sum(jnp.where(block_ones, array, 0.0).reshape(256 // modes, modes, 256), axis=0)

    def transposed_dot(left, right):
        return lax.dot_general(left, right, (((0,), (0,)), ((), ())), preferred_element_type=f32)

    loads[0].wait()
    rate_row = as_row(rate_ref[...])
    for q in range(tiles):
        piece = slice(256 * q, 256 * q + 256)
        rate_piece = rate_row[:, piece]
        high, low = split(jnp.exp(-rate_piece * (rows - 1.0 - positions)))
        wb_ref[0, :, piece] = high
        wb_ref[1, :, piece] = low
    loads[2].wait()
    for q in range(tiles):
        piece = slice(256 * q, 256 * q + 256)
        full = transposed_dot(wb_ref[0, :, piece], x_ref[:, piece]) + transposed_dot(wb_ref[1, :, piece], x_ref[:, piece])
        states[0, :, piece] = off_blocks(full)
    pack(states[0], e_send)
    for q in range(tiles):
        piece = slice(256 * q, 256 * q + 256)
        high, low = split(jnp.exp(-rate_row[:, piece] * positions))
        wf_ref[0, :, piece] = high
        wf_ref[1, :, piece] = low
    loads[3].wait()
    for q in range(tiles):
        piece = slice(256 * q, 256 * q + 256)
        full = transposed_dot(wf_ref[0, :, piece], d_ref[:, piece]) + transposed_dot(wf_ref[1, :, piece], d_ref[:, piece])
        states[1, :, piece] = off_blocks(full)
    pack(states[1], s_send)

    def copy_to(step, kind, send, recv, slot_there, slot_here):
        there = lax.rem(me + step, nctx)
        return pltpu.make_async_remote_copy(
            src_ref=send.at[there] if slot_here else send,
            dst_ref=recv.at[me],
            send_sem=send_sem.at[kind, there],
            recv_sem=recv_sem.at[kind, me],
            device_id={"ctx": there},
            device_id_type=MESH,
        )

    def arrival(step, kind, send, recv, slot_here):
        origin = lax.rem(me + step, nctx)
        return pltpu.make_async_remote_copy(
            src_ref=send.at[origin] if slot_here else send,
            dst_ref=recv.at[origin],
            send_sem=send_sem.at[kind, origin],
            recv_sem=recv_sem.at[kind, origin],
            device_id={"ctx": origin},
            device_id_type=MESH,
        )

    def send_all(kind, send, recv, slot_here=True):
        def one(turn, carried):
            step = nctx // 2 + jnp.where(turn % 2 == 1, -((turn + 1) // 2), turn // 2)
            copy_to(step, kind, send, recv, None, slot_here).start()
            return carried

        lax.fori_loop(0, nctx - 1, one, 0)

    def await_all(kind, send, recv, slot_here=True):
        def one(step, carried):
            arrival(step, kind, send, recv, slot_here).wait_recv()
            return carried

        lax.fori_loop(1, nctx, one, 0)

    def await_sent(kind, send, recv, slot_here=True):
        def one(step, carried):
            arrival(step, kind, send, recv, slot_here).wait_send()
            return carried

        lax.fori_loop(1, nctx, one, 0)

    pl.semaphore_wait(barrier, nctx - 1 + ndp - 1)
    send_all(0, e_send, e_recv.at[0])
    send_all(1, s_send, s_recv.at[0])
    e_recv[0, me] = e_send[me]
    s_recv[0, me] = s_send[me]

    loads[1].wait()
    weight_row = jnp.sqrt(1.0 - jnp.exp(-2.0 * rate_row))
    step_row = jnp.exp(-rate_row)
    coef = by_channel(as_row(res_ref[...]) * weight_row)
    rate_wide = by_channel(rate_row)
    step_wide = jnp.exp(-rate_wide)
    block_wide = jnp.exp(-rate_wide * float(rows))
    inverse_wide = 1.0 / (1.0 + block_wide)
    coefs[0] = coef * step_wide
    coefs[1] = inverse_wide
    pack(block_wide, packs.at[0])
    pack(inverse_wide, packs.at[1])
    pack(step_wide, packs.at[2])
    loads[4].wait()
    loads[5].wait()
    loads[6].wait()
    loads[7].wait()
    less_cos, sine = trig_ref[:, 0:1], trig_ref[:, 1:2]
    for q in range(tiles):
        piece = slice(256 * q, 256 * q + 256)
        step_piece = step_row[:, piece]
        rest = 1.0 - step_piece
        near = step_piece * less_cos
        below = 1.0 / (rest * rest + 2.0 * near)
        real, imag = (rest + near) * below, (-step_piece * sine) * below
        h_ref[0:half] = real
        h_ref[half:rows] = imag
        response = times(split(h_ref[...]), split(on_blocks(coef, q)))
        f_re, f_im = response[0:half], response[half:rows]
        x_piece, d_piece = x_ref[:, piece], d_ref[:, piece]
        x_hat = jnp.dot(fwd_ref[0], x_piece, preferred_element_type=f32) + jnp.dot(fwd_ref[1], x_piece, preferred_element_type=f32)
        d_hat = jnp.dot(fwd_ref[0], d_piece, preferred_element_type=f32) + jnp.dot(fwd_ref[1], d_piece, preferred_element_type=f32)
        x_re, x_im, d_re, d_im = x_hat[0:half], x_hat[half:rows], d_hat[0:half], d_hat[half:rows]
        skip = skip_ref[:, piece]
        x_wide, d_wide = x_piece.astype(f32), d_piece.astype(f32)
        y_hat = jnp.concatenate([f_re * x_re - f_im * x_im, f_re * x_im + f_im * x_re], axis=0)
        ylocal[:, piece] = times((inv_ref[0], inv_ref[1]), split(y_hat)) + skip * x_wide
        z_hat = jnp.concatenate([f_re * d_re + f_im * d_im, f_re * d_im - f_im * d_re], axis=0)
        zlocal[:, piece] = times((inv_ref[0], inv_ref[1]), split(z_hat)) + skip * d_wide
        cross = jnp.concatenate([d_re * x_re + d_im * x_im, d_im * x_re - d_re * x_im], axis=0)
        cross_high, cross_low = split(cross)
        grouped = jnp.dot(cross_high, ones, preferred_element_type=f32) + jnp.dot(cross_low, ones, preferred_element_type=f32)
        grad_piece = jnp.sum(grouped * h_ref[...], axis=0, keepdims=True) * (2.0 / rows)
        skip_piece = jnp.sum(x_wide * d_wide, axis=0, keepdims=True)
        for part in range(2):
            pair = 2 * q + part
            grad_row, skip_row = grad_piece[:, 128 * part : 128 * part + 128], skip_piece[:, 128 * part : 128 * part + 128]
            g_send[2 * pair] = jnp.where(lower_row, grad_row, pltpu.roll(skip_row, 64, 1))
            g_send[2 * pair + 1] = jnp.where(lower_row, pltpu.roll(grad_row, 64, 1), skip_row)
    send_all(2, g_send, g_recv)
    g_recv[me] = g_send[me]

    block_own, inverse_own, step_own = packs[0, me], packs[1, me], packs[2, me]
    await_all(0, e_send, e_recv.at[0])
    running = jnp.zeros((8, 128), f32)
    for block in range(nctx):
        e_recv[1, block] = running
        running = running * block_own + e_recv[0, block]
    send_all(3, e_recv.at[1], p_recv.at[0])
    p_recv[0, me] = e_recv[1, me]
    await_all(1, s_send, s_recv.at[0])
    running = jnp.zeros((8, 128), f32)
    owned = jnp.zeros((8, 128), f32)
    for block in range(nctx - 1, -1, -1):
        s_recv[1, block] = running
        start = s_recv[0, block]
        running = running * block_own + start
        owned += start * (e_recv[1, block] + e_recv[0, block] * inverse_own)
    owned = owned * step_own
    lane_row = lax.broadcasted_iota(jnp.int32, (128, 128), 0)
    lane_column = lax.broadcasted_iota(jnp.int32, (128, 128), 1)
    chosen = (
        (lane_row // 64 == (lane_column % 16) // 8) & ((lane_row % 64) // 16 == lane_column // 16)
    ).astype(f32)
    summed = jnp.dot(owned, chosen, precision=highest, preferred_element_type=f32)
    right_row = lax.broadcasted_iota(jnp.int32, (8, 128), 0) == lanes % 8
    gradient = jnp.sum(jnp.where(right_row & lower, summed, 0.0), axis=0, keepdims=True)
    await_all(2, g_send, g_recv)
    for block in range(nctx):
        gradient += g_recv[block]
    p_send[...] = gradient

    def dp_copy(step, here):
        there = lax.rem(mine + step, ndp)
        return pltpu.make_async_remote_copy(
            src_ref=p_send,
            dst_ref=g_recv_dp.at[there if here else mine],
            send_sem=psend_sem.at[there],
            recv_sem=precv_sem.at[there if here else mine],
            device_id={"dp": there},
            device_id_type=MESH,
        )

    g_recv_dp = o_recv.at[1]
    for step in range(1, ndp):
        dp_copy(step, False).start()
    send_all(4, s_recv.at[1], p_recv.at[1])
    p_recv[1, me] = s_recv[1, me]
    g_recv_dp[mine] = gradient
    for step in range(1, ndp):
        dp_copy(step, True).wait_recv()
    gradient = g_recv_dp[0]
    for other in range(1, ndp):
        gradient += g_recv_dp[other]
    o_send[...] = gradient * scale
    send_all(5, o_send, o_recv.at[0], False)
    o_recv[0, me] = gradient * scale

    def finish(kind, back, number, table, local, target):
        await_all(kind, back, p_recv.at[number])
        carried = (unpack(p_recv.at[number]) + states[number] * coefs[1]) * coefs[0]
        for q in range(tiles):
            piece = slice(256 * q, 256 * q + 256)
            product = times((table[0, :, piece], table[1, :, piece]), split(on_blocks(carried, q)))
            target[0, :, piece] = (local[:, piece] + product).astype(bf16)

    finish(3, e_recv.at[1], 0, wf_ref, ylocal, y_ref)
    finish(4, s_recv.at[1], 1, wb_ref, zlocal, z_ref)
    await_all(5, o_send, o_recv.at[0], False)
    for pair in range(nctx // 2):
        first, second = o_recv[0, 2 * pair], o_recv[0, 2 * pair + 1]
        piece = slice(128 * pair, 128 * pair + 128)
        h_ref[0:1, 0:128] = jnp.where(lower_row, first, pltpu.roll(second, 64, 1))
        gskip_ref[:, piece] = jnp.where(lower_row, pltpu.roll(first, 64, 1), second)
        packs[0, pair, 0:1] = h_ref[0:1, 0:128]
    grad_row = jnp.concatenate([packs[0, pair, 0:1] for pair in range(nctx // 2)], axis=1) * weight_row
    gres_ref[...] = lax.dot_general(
        jnp.where(own_group, grad_row, 0.0), spread, (((1,), (1,)), ((), ())), precision=highest, preferred_element_type=f32
    )

    for load_kind in ((0, e_send, e_recv.at[0]), (1, s_send, s_recv.at[0]), (2, g_send, g_recv),
                      (3, e_recv.at[1], p_recv.at[0]), (4, s_recv.at[1], p_recv.at[1])):
        await_sent(*load_kind)
    await_sent(5, o_send, o_recv.at[0], False)
    for step in range(1, ndp):
        dp_copy(step, True).wait_send()


def transform(rows):
    frequency = np.pi * (2 * np.arange(rows // 2) + 1) / rows
    angle = frequency[:, None] * np.arange(rows)[None, :]
    forward = np.concatenate([np.cos(angle), -np.sin(angle)], axis=0)
    high = forward.astype(jnp.bfloat16)
    low = (forward - high.astype(np.float64)).astype(jnp.bfloat16)
    both = np.stack([high, low])
    back = (both.transpose(0, 2, 1).astype(np.float32) * (2.0 / rows)).astype(jnp.bfloat16)
    trig = np.zeros((rows // 2, 128), np.float32)
    trig[:, 0] = 2.0 * np.sin(frequency / 2.0) ** 2
    trig[:, 1] = np.sin(frequency)
    return jnp.asarray(both), jnp.asarray(back), jnp.asarray(trig)


def shards(nctx, ndp, inputs, cotangent, residues, decay_rates, skip_gain):
    _, rows, channels = inputs.shape
    groups, modes = residues.shape
    sizes = (nctx, ndp, rows, channels, groups, modes, 1.0 / math.sqrt(rows * nctx * ndp))
    forward, back, trig = transform(rows)
    anywhere = pl.BlockSpec(memory_space=pl.ANY)
    vmem = pl.BlockSpec(memory_space=pltpu.VMEM)
    wide = (1, rows, channels)
    outputs, grad_inputs, grad_residues, grad_skip = pl.pallas_call(
        functools.partial(kernel, sizes),
        out_shape=(
            jax.ShapeDtypeStruct(wide, bf16),
            jax.ShapeDtypeStruct(wide, bf16),
            jax.ShapeDtypeStruct((groups, modes), f32),
            jax.ShapeDtypeStruct((1, channels), f32),
        ),
        in_specs=[anywhere] * 8,
        out_specs=(vmem, vmem, vmem, vmem),
        scratch_shapes=[
            pltpu.VMEM((rows, channels), bf16),
            pltpu.VMEM((rows, channels), bf16),
            pltpu.VMEM((groups, modes), f32),
            pltpu.VMEM((groups, modes), f32),
            pltpu.VMEM((1, channels), f32),
            pltpu.VMEM((2, rows, rows), bf16),
            pltpu.VMEM((2, rows, rows), bf16),
            pltpu.VMEM((rows // 2, 128), f32),
            pltpu.VMEM((2, rows, channels), bf16),
            pltpu.VMEM((2, rows, channels), bf16),
            pltpu.VMEM((rows, 256), f32),
            pltpu.VMEM((rows, channels), f32),
            pltpu.VMEM((rows, channels), f32),
            pltpu.VMEM((2, modes, channels), f32),
            pltpu.VMEM((2, modes, channels), f32),
            pltpu.VMEM((3, nctx, 8, 128), f32),
            pltpu.VMEM((nctx, 8, 128), f32),
            pltpu.VMEM((2, nctx, 8, 128), f32),
            pltpu.VMEM((nctx, 8, 128), f32),
            pltpu.VMEM((2, nctx, 8, 128), f32),
            pltpu.VMEM((nctx, 1, 128), f32),
            pltpu.VMEM((nctx, 1, 128), f32),
            pltpu.VMEM((1, 128), f32),
            pltpu.VMEM((2, nctx, 8, 128), f32),
            pltpu.VMEM((1, 128), f32),
            pltpu.VMEM((2, nctx, 1, 128), f32),
            pltpu.SemaphoreType.DMA((8,)),
            pltpu.SemaphoreType.DMA((6, nctx)),
            pltpu.SemaphoreType.DMA((6, nctx)),
            pltpu.SemaphoreType.DMA((ndp,)),
            pltpu.SemaphoreType.DMA((ndp,)),
        ],
        compiler_params=pltpu.CompilerParams(collective_id=0, has_side_effects=True, vmem_limit_bytes=48 * 1024 * 1024),
        name="hyena",
    )(inputs, cotangent, residues, decay_rates, skip_gain.reshape(1, channels), forward, back, trig)
    return outputs, grad_inputs, grad_residues, grad_skip.reshape(channels)


def solution(mesh):
    placed = (P("dp", "ctx", "tp"), P("dp", "ctx", "tp"), P("tp", None), P("tp", None), P("tp"))
    return jax.shard_map(
        functools.partial(shards, mesh.shape["ctx"], mesh.shape["dp"]),
        mesh=mesh,
        in_specs=placed,
        out_specs=(P("dp", "ctx", "tp"), P("dp", "ctx", "tp"), P("tp", None), P("tp")),
        check_vma=False,
    )
```

```python
import functools
import math

import jax
import jax.numpy as jnp
import numpy as np
from jax import lax
from jax.experimental import pallas as pl
from jax.experimental.pallas import tpu as pltpu
from jax.sharding import PartitionSpec as P

MESH = pl.DeviceIdType.MESH
highest = lax.Precision.HIGHEST
f32 = jnp.float32
bf16 = jnp.bfloat16
COMM = True
UNROLL = True


def split(value):
    high = value.astype(bf16)
    return high, (value - high.astype(f32)).astype(bf16)


def times(left, right):
    total = jnp.dot(left[0], right[0], preferred_element_type=f32)
    total += jnp.dot(left[0], right[1], preferred_element_type=f32)
    return total + jnp.dot(left[1], right[0], preferred_element_type=f32)


def times_row(left, right):
    return jnp.dot(left, right, precision=highest, preferred_element_type=f32)


def split_store(target, piece, value):
    high, low = split(value)
    target[0, :, piece] = high
    target[1, :, piece] = low


def same_block(shape):
    return lax.broadcasted_iota(jnp.int32, shape, 0) // 16 == lax.broadcasted_iota(jnp.int32, shape, 1) // 16


def on_blocks(piece):
    return jnp.where(same_block((256, 256)), jnp.concatenate([piece] * 16, axis=0), 0.0)


def off_blocks(array):
    return jnp.sum(jnp.where(same_block((256, 256)), array, 0.0).reshape(16, 16, 256), axis=0)


def kernel(sizes, x_hbm, d_hbm, res_hbm, rate_hbm, skip_hbm, fwd_hbm, inv_hbm, trig_hbm,
           y_ref, zlocal, wb_ref, carried_ref, gres_ref, gskip_ref,
           x_ref, d_ref, res_ref, rate_ref, skip_ref, fwd_ref, inv_ref, trig_ref,
           wf_ref, h_ref, ylocal, rate_row, states, coefs, packs, e_send, e_recv, s_send, s_recv,
           g_send, g_recv, p_send, p_recv, o_send, o_recv, load_sem, send_sem, recv_sem, psend_sem, precv_sem):
    nctx, ndp, rows, channels, groups, modes, scale = sizes
    half = rows // 2
    tiles = channels // 256
    me = lax.axis_index("ctx")
    mine = lax.axis_index("dp")

    barrier = pltpu.get_barrier_semaphore()

    def greet(step, carried):
        pl.semaphore_signal(barrier, inc=1, device_id={"ctx": lax.rem(me + step, nctx)}, device_id_type=MESH)
        return carried

    if COMM:
        lax.fori_loop(1, nctx, greet, 0)
        for step in range(1, ndp):
            pl.semaphore_signal(barrier, inc=1, device_id={"dp": lax.rem(mine + step, ndp)}, device_id_type=MESH)

    loads = [
        pltpu.make_async_copy(source, target, load_sem.at[number])
        for number, (source, target) in enumerate(
            [(rate_hbm, rate_ref), (res_hbm, res_ref), (x_hbm.at[0], x_ref), (d_hbm.at[0], d_ref), (trig_hbm, trig_ref),
             (fwd_hbm, fwd_ref), (inv_hbm, inv_ref), (skip_hbm, skip_ref)]
        )
    ]
    for load in loads:
        load.start()

    lanes = lax.broadcasted_iota(jnp.int32, (8, 128), 1)
    lower = lanes < 64
    lower_row = lax.broadcasted_iota(jnp.int32, (1, 128), 1) < 64
    positions = lax.broadcasted_iota(jnp.int32, (rows, 1), 0).astype(f32)
    own_group = (
        lax.broadcasted_iota(jnp.int32, (groups, channels), 1) // modes == lax.broadcasted_iota(jnp.int32, (groups, channels), 0)
    ).astype(f32)
    own_mode = (
        lax.broadcasted_iota(jnp.int32, (modes, channels), 1) % modes == lax.broadcasted_iota(jnp.int32, (modes, channels), 0)
    )

    def by_tiles(body):
        if UNROLL:
            for q in range(tiles):
                body(q, slice(256 * q, 256 * q + 256))
        else:
            def turn(q, carried):
                body(q, pl.ds(pl.multiple_of(q * 256, 256), 256))
                return carried

            lax.fori_loop(0, tiles, turn, 0)

    def pack(array, target):
        for pair in range(nctx // 2):
            low = array[0:8, 128 * pair : 128 * pair + 128]
            high = array[8:16, 128 * pair : 128 * pair + 128]
            target[2 * pair] = jnp.where(lower, low, pltpu.roll(high, 64, 1))
            target[2 * pair + 1] = jnp.where(lower, pltpu.roll(low, 64, 1), high)

    def unpack(source):
        lows, highs = [], []
        for pair in range(nctx // 2):
            first, second = source[2 * pair], source[2 * pair + 1]
            lows.append(jnp.where(lower, first, pltpu.roll(second, 64, 1)))
            highs.append(jnp.where(lower, pltpu.roll(first, 64, 1), second))
        return jnp.concatenate([jnp.concatenate(lows, axis=1), jnp.concatenate(highs, axis=1)], axis=0)

    def transposed_dot(left, right):
        return lax.dot_general(left, right, (((0,), (0,)), ((), ())), preferred_element_type=f32)

    loads[0].wait()
    rate_wide = times_row(rate_ref[...], own_group)
    rate_row[...] = jnp.sum(jnp.where(own_mode, rate_wide, 0.0), axis=0, keepdims=True)

    def end_states(q, piece):
        split_store(wb_ref, piece, jnp.exp(-rate_row[:, piece] * (rows - 1.0 - positions)))
        full = transposed_dot(wb_ref[0, :, piece], x_ref[:, piece]) + transposed_dot(wb_ref[1, :, piece], x_ref[:, piece])
        states[0, :, piece] = off_blocks(full)

    def start_states(q, piece):
        split_store(wf_ref, piece, jnp.exp(-rate_row[:, piece] * positions))
        full = transposed_dot(wf_ref[0, :, piece], d_ref[:, piece]) + transposed_dot(wf_ref[1, :, piece], d_ref[:, piece])
        states[1, :, piece] = off_blocks(full)

    loads[2].wait()
    by_tiles(end_states)
    pack(states[0], e_send)
    loads[3].wait()
    by_tiles(start_states)
    pack(states[1], s_send)

    def state_copy(there, kind, send, recv, slot_there):
        return pltpu.make_async_remote_copy(
            src_ref=send.at[there] if kind < 5 else send,
            dst_ref=recv.at[slot_there],
            send_sem=send_sem.at[kind, there],
            recv_sem=recv_sem.at[kind, slot_there],
            device_id={"ctx": there},
            device_id_type=MESH,
        )

    def over_peers(body):
        def turn(step, carried):
            body(lax.rem(me + step, nctx))
            return carried

        if COMM:
            lax.fori_loop(1, nctx, turn, 0)

    def send_all(kind, send, recv):
        def turn(count, carried):
            step = nctx // 2 + jnp.where(count % 2 == 1, -((count + 1) // 2), count // 2)
            state_copy(lax.rem(me + step, nctx), kind, send, recv, me).start()
            return carried

        if COMM:
            lax.fori_loop(0, nctx - 1, turn, 0)

    def await_all(kind, send, recv):
        over_peers(lambda origin: state_copy(origin, kind, send, recv, origin).wait_recv())

    def await_sent(kind, send, recv):
        over_peers(lambda origin: state_copy(origin, kind, send, recv, origin).wait_send())

    if COMM:
        pl.semaphore_wait(barrier, nctx - 1 + ndp - 1)
    send_all(0, e_send, e_recv.at[0])
    send_all(1, s_send, s_recv.at[0])
    e_recv[0, me] = e_send[me]
    s_recv[0, me] = s_send[me]

    loads[1].wait()
    coefs[0] = times_row(res_ref[...], own_group) * jnp.sqrt(1.0 - jnp.exp(-2.0 * rate_wide))
    step_wide = jnp.exp(-rate_wide)
    block_wide = jnp.exp(-rate_wide * float(rows))
    inverse_wide = 1.0 / (1.0 + block_wide)
    coefs[1] = coefs[0] * step_wide
    coefs[2] = inverse_wide
    pack(block_wide, packs.at[0])
    pack(inverse_wide, packs.at[1])
    pack(step_wide, packs.at[2])
    for load in loads[4:]:
        load.wait()

    def own_part(q, piece):
        step_piece = jnp.exp(-rate_row[:, piece])
        less_cos, sine = trig_ref[:, 0:1], trig_ref[:, 1:2]
        rest = 1.0 - step_piece
        near = step_piece * less_cos
        below = 1.0 / (rest * rest + 2.0 * near)
        h_ref[0:half] = (rest + near) * below
        h_ref[half:rows] = (-step_piece * sine) * below
        response = times(split(h_ref[...]), split(on_blocks(coefs[0, :, piece])))
        f_re, f_im = response[0:half], response[half:rows]
        x_piece, d_piece = x_ref[:, piece], d_ref[:, piece]
        x_hat = jnp.dot(fwd_ref[0], x_piece, preferred_element_type=f32) + jnp.dot(fwd_ref[1], x_piece, preferred_element_type=f32)
        d_hat = jnp.dot(fwd_ref[0], d_piece, preferred_element_type=f32) + jnp.dot(fwd_ref[1], d_piece, preferred_element_type=f32)
        x_re, x_im, d_re, d_im = x_hat[0:half], x_hat[half:rows], d_hat[0:half], d_hat[half:rows]
        skip = skip_ref[:, piece]
        x_wide, d_wide = x_piece.astype(f32), d_piece.astype(f32)
        y_hat = jnp.concatenate([f_re * x_re - f_im * x_im, f_re * x_im + f_im * x_re], axis=0)
        ylocal[:, piece] = times((inv_ref[0], inv_ref[1]), split(y_hat)) + skip * x_wide
        z_hat = jnp.concatenate([f_re * d_re + f_im * d_im, f_re * d_im - f_im * d_re], axis=0)
        zlocal[:, piece] = times((inv_ref[0], inv_ref[1]), split(z_hat)) + skip * d_wide
        cross = jnp.concatenate([d_re * x_re + d_im * x_im, d_im * x_re - d_re * x_im], axis=0)
        cross_high, cross_low = split(cross)
        ones = same_block((256, 256)).astype(bf16)
        grouped = jnp.dot(cross_high, ones, preferred_element_type=f32) + jnp.dot(cross_low, ones, preferred_element_type=f32)
        grad_piece = jnp.sum(grouped * h_ref[...], axis=0, keepdims=True) * (2.0 / rows)
        skip_piece = jnp.sum(x_wide * d_wide, axis=0, keepdims=True)
        for part in range(2):
            pair = 2 * q + part
            grad_row, skip_row = grad_piece[:, 128 * part : 128 * part + 128], skip_piece[:, 128 * part : 128 * part + 128]
            g_send[2 * pair] = jnp.where(lower_row, grad_row, pltpu.roll(skip_row, 64, 1))
            g_send[2 * pair + 1] = jnp.where(lower_row, pltpu.roll(grad_row, 64, 1), skip_row)

    by_tiles(own_part)
    send_all(2, g_send, g_recv)
    g_recv[me] = g_send[me]

    block_own, inverse_own, step_own = packs[0, me], packs[1, me], packs[2, me]
    await_all(0, e_send, e_recv.at[0])
    running = jnp.zeros((8, 128), f32)
    for block in range(nctx):
        e_recv[1, block] = running
        running = running * block_own + e_recv[0, block]
    send_all(3, e_recv.at[1], p_recv.at[0])
    p_recv[0, me] = e_recv[1, me]
    await_all(1, s_send, s_recv.at[0])
    running = jnp.zeros((8, 128), f32)
    owned = jnp.zeros((8, 128), f32)
    for block in range(nctx - 1, -1, -1):
        s_recv[1, block] = running
        start = s_recv[0, block]
        running = running * block_own + start
        owned += start * (e_recv[1, block] + e_recv[0, block] * inverse_own)
    owned = owned * step_own
    lane_row = lax.broadcasted_iota(jnp.int32, (128, 128), 0)
    lane_column = lax.broadcasted_iota(jnp.int32, (128, 128), 1)
    chosen = (
        (lane_row // 64 == (lane_column % 16) // 8) & ((lane_row % 64) // 16 == lane_column // 16)
    ).astype(f32)
    summed = times_row(owned, chosen)
    right_row = lax.broadcasted_iota(jnp.int32, (8, 128), 0) == lanes % 8
    gradient = jnp.sum(jnp.where(right_row & lower, summed, 0.0), axis=0, keepdims=True)
    await_all(2, g_send, g_recv)
    for block in range(nctx):
        gradient += g_recv[block]
    p_send[...] = gradient
    from_dp = o_recv.at[1]

    def dp_copy(step, here):
        there = lax.rem(mine + step, ndp)
        slot = there if here else mine
        return pltpu.make_async_remote_copy(
            src_ref=p_send,
            dst_ref=from_dp.at[slot],
            send_sem=psend_sem.at[there],
            recv_sem=precv_sem.at[slot],
            device_id={"dp": there},
            device_id_type=MESH,
        )

    if COMM:
        for step in range(1, ndp):
            dp_copy(step, False).start()
    send_all(4, s_recv.at[1], p_recv.at[1])
    p_recv[1, me] = s_recv[1, me]
    from_dp[mine] = gradient
    if COMM:
        for step in range(1, ndp):
            dp_copy(step, True).wait_recv()
    gradient = from_dp[0]
    for other in range(1, ndp):
        gradient += from_dp[other]
    o_send[...] = gradient * scale
    send_all(5, o_send, o_recv.at[0])
    o_recv[0, me] = gradient * scale

    await_all(3, e_recv.at[1], p_recv.at[0])
    carried_ref[...] = (unpack(p_recv.at[0]) + states[0] * coefs[2]) * coefs[1]

    def finish(q, piece):
        product = times((wf_ref[0, :, piece], wf_ref[1, :, piece]), split(on_blocks(carried_ref[:, piece])))
        y_ref[:, piece] = (ylocal[:, piece] + product).astype(bf16)

    by_tiles(finish)
    await_all(4, s_recv.at[1], p_recv.at[1])
    carried_ref[...] = (unpack(p_recv.at[1]) + states[1] * coefs[2]) * coefs[1]
    await_all(5, o_send, o_recv.at[0])
    final = []
    for pair in range(nctx // 2):
        first, second = o_recv[0, 2 * pair], o_recv[0, 2 * pair + 1]
        gskip_ref[:, 128 * pair : 128 * pair + 128] = jnp.where(lower_row, pltpu.roll(first, 64, 1), second)
        final.append(jnp.where(lower_row, first, pltpu.roll(second, 64, 1)))
    by_group = lax.dot_general(
        jnp.where(own_mode, jnp.concatenate(final, axis=1), 0.0), own_group, (((1,), (1,)), ((), ())), precision=highest,
        preferred_element_type=f32,
    )
    gres_ref[...] = by_group * jnp.sqrt(1.0 - jnp.exp(-2.0 * rate_ref[...]))

    for sent in ((0, e_send, e_recv.at[0]), (1, s_send, s_recv.at[0]), (2, g_send, g_recv),
                 (3, e_recv.at[1], p_recv.at[0]), (4, s_recv.at[1], p_recv.at[1]), (5, o_send, o_recv.at[0])):
        await_sent(*sent)
    if COMM:
        for step in range(1, ndp):
            dp_copy(step, True).wait_send()


def last_kernel(y_in, zlocal, wb_ref, carried_ref, gres_in, gskip_in, y_hbm, z_hbm, gres_hbm, gskip_hbm, z_ref, sem):
    tiles = zlocal.shape[1] // 256
    copies = [
        pltpu.make_async_copy(source, target, sem.at[number])
        for number, (source, target) in enumerate([(y_in, y_hbm.at[0]), (gres_in, gres_hbm), (gskip_in, gskip_hbm)])
    ]
    for copy in copies:
        copy.start()
    for q in range(tiles):
        piece = slice(256 * q, 256 * q + 256)
        product = times((wb_ref[0, :, piece], wb_ref[1, :, piece]), split(on_blocks(carried_ref[:, piece])))
        z_ref[:, piece] = (zlocal[:, piece] + product).astype(bf16)
        copy = pltpu.make_async_copy(z_ref.at[:, piece], z_hbm.at[0, :, piece], sem.at[3 + q])
        copy.start()
        copies.append(copy)
    for copy in copies:
        copy.wait()


def transform(rows):
    frequency = np.pi * (2 * np.arange(rows // 2) + 1) / rows
    angle = frequency[:, None] * np.arange(rows)[None, :]
    forward = np.concatenate([np.cos(angle), -np.sin(angle)], axis=0)
    high = forward.astype(jnp.bfloat16)
    low = (forward - high.astype(np.float64)).astype(jnp.bfloat16)
    both = np.stack([high, low])
    back = (both.transpose(0, 2, 1).astype(np.float32) * (2.0 / rows)).astype(jnp.bfloat16)
    trig = np.zeros((rows // 2, 128), np.float32)
    trig[:, 0] = 2.0 * np.sin(frequency / 2.0) ** 2
    trig[:, 1] = np.sin(frequency)
    return jnp.asarray(both), jnp.asarray(back), jnp.asarray(trig)


def shards(nctx, ndp, inputs, cotangent, residues, decay_rates, skip_gain):
    _, rows, channels = inputs.shape
    groups, modes = residues.shape
    sizes = (nctx, ndp, rows, channels, groups, modes, 1.0 / math.sqrt(rows * nctx * ndp))
    forward, back, trig = transform(rows)
    hbm = pl.BlockSpec(memory_space=pltpu.HBM)
    vmem = pl.BlockSpec(memory_space=pltpu.VMEM)
    wide = (1, rows, channels)
    parts = pl.pallas_call(
        functools.partial(kernel, sizes),
        out_shape=(
            jax.ShapeDtypeStruct((rows, channels), bf16),
            jax.ShapeDtypeStruct((rows, channels), f32),
            jax.ShapeDtypeStruct((2, rows, channels), bf16),
            jax.ShapeDtypeStruct((modes, channels), f32),
            jax.ShapeDtypeStruct((modes, groups), f32),
            jax.ShapeDtypeStruct((1, channels), f32),
        ),
        in_specs=[hbm] * 8,
        out_specs=(vmem,) * 6,
        scratch_shapes=[
            pltpu.VMEM((rows, channels), bf16),
            pltpu.VMEM((rows, channels), bf16),
            pltpu.VMEM((modes, groups), f32),
            pltpu.VMEM((modes, groups), f32),
            pltpu.VMEM((1, channels), f32),
            pltpu.VMEM((2, rows, rows), bf16),
            pltpu.VMEM((2, rows, rows), bf16),
            pltpu.VMEM((rows // 2, 128), f32),
            pltpu.VMEM((2, rows, channels), bf16),
            pltpu.VMEM((rows, 256), f32),
            pltpu.VMEM((rows, channels), f32),
            pltpu.VMEM((1, channels), f32),
            pltpu.VMEM((2, modes, channels), f32),
            pltpu.VMEM((3, modes, channels), f32),
            pltpu.VMEM((3, nctx, 8, 128), f32),
            pltpu.VMEM((nctx, 8, 128), f32),
            pltpu.VMEM((2, nctx, 8, 128), f32),
            pltpu.VMEM((nctx, 8, 128), f32),
            pltpu.VMEM((2, nctx, 8, 128), f32),
            pltpu.VMEM((nctx, 1, 128), f32),
            pltpu.VMEM((nctx, 1, 128), f32),
            pltpu.VMEM((1, 128), f32),
            pltpu.VMEM((2, nctx, 8, 128), f32),
            pltpu.VMEM((1, 128), f32),
            pltpu.VMEM((2, nctx, 1, 128), f32),
            pltpu.SemaphoreType.DMA((8,)),
            pltpu.SemaphoreType.DMA((6, nctx)),
            pltpu.SemaphoreType.DMA((6, nctx)),
            pltpu.SemaphoreType.DMA((ndp,)),
            pltpu.SemaphoreType.DMA((ndp,)),
        ],
        compiler_params=pltpu.CompilerParams(collective_id=0, has_side_effects=True, vmem_limit_bytes=32 * 1024 * 1024),
        name="hyena",
    )(*[pltpu.with_memory_space_constraint(a, pltpu.HBM) for a in (inputs, cotangent, residues.T, decay_rates.T, skip_gain.reshape(1, channels), forward, back, trig)])
    outputs, grad_inputs, grad_residues, grad_skip = pl.pallas_call(
        last_kernel,
        out_shape=(
            jax.ShapeDtypeStruct(wide, bf16),
            jax.ShapeDtypeStruct(wide, bf16),
            jax.ShapeDtypeStruct((modes, groups), f32),
            jax.ShapeDtypeStruct((1, channels), f32),
        ),
        in_specs=[vmem] * 6,
        out_specs=(hbm,) * 4,
        scratch_shapes=[pltpu.VMEM((rows, channels), bf16), pltpu.SemaphoreType.DMA((3 + channels // 256,))],
        compiler_params=pltpu.CompilerParams(vmem_limit_bytes=32 * 1024 * 1024),
        name="last",
    )(*parts)
    return outputs, grad_inputs, grad_residues.T, grad_skip.reshape(channels)


def solution(mesh):
    placed = (P("dp", "ctx", "tp"), P("dp", "ctx", "tp"), P("tp", None), P("tp", None), P("tp"))
    return jax.shard_map(
        functools.partial(shards, mesh.shape["ctx"], mesh.shape["dp"]),
        mesh=mesh,
        in_specs=placed,
        out_specs=(P("dp", "ctx", "tp"), P("dp", "ctx", "tp"), P("tp", None), P("tp")),
        check_vma=False,
    )
```

```python
import functools
import math

import jax
import jax.numpy as jnp
import numpy as np
from jax import lax
from jax.experimental import pallas as pl
from jax.experimental.pallas import tpu as pltpu
from jax.sharding import PartitionSpec as P

MESH = pl.DeviceIdType.MESH
highest = lax.Precision.HIGHEST
f32 = jnp.float32
bf16 = jnp.bfloat16
COMM = True
UNROLL = True


def split(value):
    high = value.astype(bf16)
    return high, (value - high.astype(f32)).astype(bf16)


def times(left, right):
    total = jnp.dot(left[0], right[0], preferred_element_type=f32)
    total += jnp.dot(left[0], right[1], preferred_element_type=f32)
    return total + jnp.dot(left[1], right[0], preferred_element_type=f32)


def times_row(left, right):
    return jnp.dot(left, right, precision=highest, preferred_element_type=f32)


def split_store(target, piece, value):
    high, low = split(value)
    target[0, :, piece] = high
    target[1, :, piece] = low


def same_block(shape):
    return lax.broadcasted_iota(jnp.int32, shape, 0) // 16 == lax.broadcasted_iota(jnp.int32, shape, 1) // 16


def on_blocks(piece):
    return jnp.where(same_block((256, 256)), jnp.concatenate([piece] * 16, axis=0), 0.0)


def off_blocks(array):
    return jnp.sum(jnp.where(same_block((256, 256)), array, 0.0).reshape(16, 16, 256), axis=0)


def kernel(sizes, x_hbm, d_hbm, res_hbm, rate_hbm, skip_hbm, fwd_hbm, inv_hbm, trig_hbm,
           y_ref, zlocal, wb_ref, carried_ref, final_ref,
           x_ref, d_ref, res_ref, rate_ref, skip_ref, fwd_ref, inv_ref, trig_ref,
           wf_ref, h_ref, x_hat, d_hat, ylocal, rate_row, states, coefs, packs, e_send, e_recv, s_send, s_recv,
           g_send, g_recv, p_send, p_recv, o_send, o_recv, load_sem, send_sem, recv_sem, psend_sem, precv_sem):
    nctx, ndp, rows, channels, groups, modes, scale = sizes
    half = rows // 2
    tiles = channels // 256
    me = lax.axis_index("ctx")
    mine = lax.axis_index("dp")

    barrier = pltpu.get_barrier_semaphore()

    def greet(step, carried):
        pl.semaphore_signal(barrier, inc=1, device_id={"ctx": lax.rem(me + step, nctx)}, device_id_type=MESH)
        return carried

    if COMM:
        lax.fori_loop(1, nctx, greet, 0)
        for step in range(1, ndp):
            pl.semaphore_signal(barrier, inc=1, device_id={"dp": lax.rem(mine + step, ndp)}, device_id_type=MESH)

    loads = [
        pltpu.make_async_copy(source, target, load_sem.at[number])
        for number, (source, target) in enumerate(
            [(rate_hbm, rate_ref), (res_hbm, res_ref), (x_hbm.at[0], x_ref), (d_hbm.at[0], d_ref), (trig_hbm, trig_ref),
             (fwd_hbm, fwd_ref), (inv_hbm, inv_ref), (skip_hbm, skip_ref)]
        )
    ]
    for load in loads:
        load.start()

    lanes = lax.broadcasted_iota(jnp.int32, (8, 128), 1)
    lower = lanes < 64
    lower_row = lax.broadcasted_iota(jnp.int32, (1, 128), 1) < 64
    positions = lax.broadcasted_iota(jnp.int32, (rows, 1), 0).astype(f32)
    own_group = (
        lax.broadcasted_iota(jnp.int32, (groups, channels), 1) // modes == lax.broadcasted_iota(jnp.int32, (groups, channels), 0)
    ).astype(f32)
    own_mode = (
        lax.broadcasted_iota(jnp.int32, (modes, channels), 1) % modes == lax.broadcasted_iota(jnp.int32, (modes, channels), 0)
    )

    def by_tiles(body):
        if UNROLL:
            for q in range(tiles):
                body(q, slice(256 * q, 256 * q + 256))
        else:
            def turn(q, carried):
                body(q, pl.ds(pl.multiple_of(q * 256, 256), 256))
                return carried

            lax.fori_loop(0, tiles, turn, 0)

    def pack(array, target):
        for pair in range(nctx // 2):
            low = array[0:8, 128 * pair : 128 * pair + 128]
            high = array[8:16, 128 * pair : 128 * pair + 128]
            target[2 * pair] = jnp.where(lower, low, pltpu.roll(high, 64, 1))
            target[2 * pair + 1] = jnp.where(lower, pltpu.roll(low, 64, 1), high)

    def unpack(source):
        lows, highs = [], []
        for pair in range(nctx // 2):
            first, second = source[2 * pair], source[2 * pair + 1]
            lows.append(jnp.where(lower, first, pltpu.roll(second, 64, 1)))
            highs.append(jnp.where(lower, pltpu.roll(first, 64, 1), second))
        return jnp.concatenate([jnp.concatenate(lows, axis=1), jnp.concatenate(highs, axis=1)], axis=0)

    def transposed_dot(left, right):
        return lax.dot_general(left, right, (((0,), (0,)), ((), ())), preferred_element_type=f32)

    loads[0].wait()
    rate_wide = times_row(rate_ref[...], own_group)
    rate_row[...] = jnp.sum(jnp.where(own_mode, rate_wide, 0.0), axis=0, keepdims=True)

    def end_states(q, piece):
        split_store(wb_ref, piece, jnp.exp(-rate_row[:, piece] * (rows - 1.0 - positions)))
        full = transposed_dot(wb_ref[0, :, piece], x_ref[:, piece]) + transposed_dot(wb_ref[1, :, piece], x_ref[:, piece])
        states[0, :, piece] = off_blocks(full)

    def start_states(q, piece):
        split_store(wf_ref, piece, jnp.exp(-rate_row[:, piece] * positions))
        full = transposed_dot(wf_ref[0, :, piece], d_ref[:, piece]) + transposed_dot(wf_ref[1, :, piece], d_ref[:, piece])
        states[1, :, piece] = off_blocks(full)

    loads[2].wait()
    by_tiles(end_states)
    pack(states[0], e_send)
    loads[3].wait()
    by_tiles(start_states)
    pack(states[1], s_send)

    def state_copy(there, kind, send, recv, slot_there):
        return pltpu.make_async_remote_copy(
            src_ref=send.at[there] if kind < 5 else send,
            dst_ref=recv.at[slot_there],
            send_sem=send_sem.at[kind, there],
            recv_sem=recv_sem.at[kind, slot_there],
            device_id={"ctx": there},
            device_id_type=MESH,
        )

    def over_peers(body):
        def turn(step, carried):
            body(lax.rem(me + step, nctx))
            return carried

        if COMM:
            lax.fori_loop(1, nctx, turn, 0)

    def send_all(kind, send, recv):
        def turn(count, carried):
            step = nctx // 2 + jnp.where(count % 2 == 1, -((count + 1) // 2), count // 2)
            state_copy(lax.rem(me + step, nctx), kind, send, recv, me).start()
            return carried

        if COMM:
            lax.fori_loop(0, nctx - 1, turn, 0)

    def await_all(kind, send, recv):
        over_peers(lambda origin: state_copy(origin, kind, send, recv, origin).wait_recv())

    def await_sent(kind, send, recv):
        over_peers(lambda origin: state_copy(origin, kind, send, recv, origin).wait_send())

    for load in loads[4:]:
        load.wait()

    def spectra(q, piece):
        step_piece = jnp.exp(-rate_row[:, piece])
        less_cos, sine = trig_ref[:, 0:1], trig_ref[:, 1:2]
        rest = 1.0 - step_piece
        near = step_piece * less_cos
        below = 1.0 / (rest * rest + 2.0 * near)
        h_ref[0:half, piece] = (rest + near) * below
        h_ref[half:rows, piece] = (-step_piece * sine) * below
        x_piece, d_piece = x_ref[:, piece], d_ref[:, piece]
        x_new = jnp.dot(fwd_ref[0], x_piece, preferred_element_type=f32) + jnp.dot(fwd_ref[1], x_piece, preferred_element_type=f32)
        d_new = jnp.dot(fwd_ref[0], d_piece, preferred_element_type=f32) + jnp.dot(fwd_ref[1], d_piece, preferred_element_type=f32)
        x_hat[:, piece] = x_new
        d_hat[:, piece] = d_new
        x_re, x_im, d_re, d_im = x_new[0:half], x_new[half:rows], d_new[0:half], d_new[half:rows]
        cross = jnp.concatenate([d_re * x_re + d_im * x_im, d_im * x_re - d_re * x_im], axis=0)
        cross_high, cross_low = split(cross)
        ones = same_block((256, 256)).astype(bf16)
        grouped = jnp.dot(cross_high, ones, preferred_element_type=f32) + jnp.dot(cross_low, ones, preferred_element_type=f32)
        grad_piece = jnp.sum(grouped * h_ref[:, piece], axis=0, keepdims=True) * (2.0 / rows)
        skip_piece = jnp.sum(x_piece.astype(f32) * d_piece.astype(f32), axis=0, keepdims=True)
        for part in range(2):
            pair = 2 * q + part
            grad_row, skip_row = grad_piece[:, 128 * part : 128 * part + 128], skip_piece[:, 128 * part : 128 * part + 128]
            g_send[2 * pair] = jnp.where(lower_row, grad_row, pltpu.roll(skip_row, 64, 1))
            g_send[2 * pair + 1] = jnp.where(lower_row, pltpu.roll(grad_row, 64, 1), skip_row)

    by_tiles(spectra)

    if COMM:
        pl.semaphore_wait(barrier, nctx - 1 + ndp - 1)
    send_all(0, e_send, e_recv.at[0])
    send_all(2, g_send, g_recv)
    send_all(1, s_send, s_recv.at[0])
    e_recv[0, me] = e_send[me]
    s_recv[0, me] = s_send[me]
    g_recv[me] = g_send[me]

    loads[1].wait()
    coefs[0] = times_row(res_ref[...], own_group) * jnp.sqrt(1.0 - jnp.exp(-2.0 * rate_wide))
    step_wide = jnp.exp(-rate_wide)
    block_wide = jnp.exp(-rate_wide * float(rows))
    inverse_wide = 1.0 / (1.0 + block_wide)
    coefs[1] = coefs[0] * step_wide
    coefs[2] = inverse_wide
    pack(block_wide, packs.at[0])
    pack(inverse_wide, packs.at[1])
    pack(step_wide, packs.at[2])

    def own_part(q, piece):
        response = times(split(h_ref[:, piece]), split(on_blocks(coefs[0, :, piece])))
        f_re, f_im = response[0:half], response[half:rows]
        x_re, x_im, d_re, d_im = x_hat[0:half, piece], x_hat[half:rows, piece], d_hat[0:half, piece], d_hat[half:rows, piece]
        skip = skip_ref[:, piece]
        y_hat = jnp.concatenate([f_re * x_re - f_im * x_im, f_re * x_im + f_im * x_re], axis=0)
        ylocal[:, piece] = times((inv_ref[0], inv_ref[1]), split(y_hat)) + skip * x_ref[:, piece].astype(f32)
        z_hat = jnp.concatenate([f_re * d_re + f_im * d_im, f_re * d_im - f_im * d_re], axis=0)
        zlocal[:, piece] = times((inv_ref[0], inv_ref[1]), split(z_hat)) + skip * d_ref[:, piece].astype(f32)

    by_tiles(own_part)

    block_own, inverse_own, step_own = packs[0, me], packs[1, me], packs[2, me]
    await_all(0, e_send, e_recv.at[0])
    running = jnp.zeros((8, 128), f32)
    for block in range(nctx):
        e_recv[1, block] = running
        running = running * block_own + e_recv[0, block]
    send_all(3, e_recv.at[1], p_recv.at[0])
    p_recv[0, me] = e_recv[1, me]
    await_all(2, g_send, g_recv)
    gradient = g_recv[0]
    for block in range(1, nctx):
        gradient += g_recv[block]
    await_all(1, s_send, s_recv.at[0])
    running = jnp.zeros((8, 128), f32)
    owned = jnp.zeros((8, 128), f32)
    for block in range(nctx - 1, -1, -1):
        s_recv[1, block] = running
        start = s_recv[0, block]
        running = running * block_own + start
        owned += start * (e_recv[1, block] + e_recv[0, block] * inverse_own)
    high, low = split(owned * step_own)
    lane_row = lax.broadcasted_iota(jnp.int32, (128, 128), 0)
    lane_column = lax.broadcasted_iota(jnp.int32, (128, 128), 1)
    chosen = (
        (lane_row // 64 == (lane_column % 16) // 8) & ((lane_row % 64) // 16 == lane_column // 16)
    ).astype(bf16)
    summed = jnp.dot(high, chosen, preferred_element_type=f32) + jnp.dot(low, chosen, preferred_element_type=f32)
    right_row = lax.broadcasted_iota(jnp.int32, (8, 128), 0) == lanes % 8
    gradient += jnp.sum(jnp.where(right_row & lower, summed, 0.0), axis=0, keepdims=True)
    p_send[...] = gradient
    from_dp = o_recv.at[1]

    def dp_copy(step, here):
        there = lax.rem(mine + step, ndp)
        slot = there if here else mine
        return pltpu.make_async_remote_copy(
            src_ref=p_send,
            dst_ref=from_dp.at[slot],
            send_sem=psend_sem.at[there],
            recv_sem=precv_sem.at[slot],
            device_id={"dp": there},
            device_id_type=MESH,
        )

    if COMM:
        for step in range(1, ndp):
            dp_copy(step, False).start()
    send_all(4, s_recv.at[1], p_recv.at[1])
    p_recv[1, me] = s_recv[1, me]
    from_dp[mine] = gradient
    if COMM:
        for step in range(1, ndp):
            dp_copy(step, True).wait_recv()
    gradient = from_dp[0]
    for other in range(1, ndp):
        gradient += from_dp[other]
    o_send[...] = gradient * scale
    send_all(5, o_send, o_recv.at[0])
    o_recv[0, me] = gradient * scale

    await_all(3, e_recv.at[1], p_recv.at[0])
    carried_ref[...] = (unpack(p_recv.at[0]) + states[0] * coefs[2]) * coefs[1]

    def finish(q, piece):
        product = times((wf_ref[0, :, piece], wf_ref[1, :, piece]), split(on_blocks(carried_ref[:, piece])))
        y_ref[:, piece] = (ylocal[:, piece] + product).astype(bf16)

    by_tiles(finish)
    await_all(4, s_recv.at[1], p_recv.at[1])
    carried_ref[...] = (unpack(p_recv.at[1]) + states[1] * coefs[2]) * coefs[1]
    await_all(5, o_send, o_recv.at[0])
    final_ref[...] = o_recv[0]

    for sent in ((0, e_send, e_recv.at[0]), (1, s_send, s_recv.at[0]), (2, g_send, g_recv),
                 (3, e_recv.at[1], p_recv.at[0]), (4, s_recv.at[1], p_recv.at[1]), (5, o_send, o_recv.at[0])):
        await_sent(*sent)
    if COMM:
        for step in range(1, ndp):
            dp_copy(step, True).wait_send()


def last_kernel(y_in, zlocal, wb_ref, carried_ref, final_ref, rate_ref, y_hbm, z_hbm, gres_hbm, gskip_hbm,
                z_ref, gres_ref, gskip_ref, sem):
    channels = zlocal.shape[1]
    modes, groups = rate_ref.shape
    copies = []

    def send(source, target):
        copies.append(pltpu.make_async_copy(source, target, sem.at[len(copies)]))
        copies[-1].start()

    send(y_in, y_hbm.at[0])
    for q in range(channels // 256):
        piece = slice(256 * q, 256 * q + 256)
        product = times((wb_ref[0, :, piece], wb_ref[1, :, piece]), split(on_blocks(carried_ref[:, piece])))
        z_ref[:, piece] = (zlocal[:, piece] + product).astype(bf16)
        send(z_ref.at[:, piece], z_hbm.at[0, :, piece])
    lower_row = lax.broadcasted_iota(jnp.int32, (1, 128), 1) < 64
    final = []
    for pair in range(channels // 128):
        first, second = final_ref[2 * pair], final_ref[2 * pair + 1]
        gskip_ref[:, 128 * pair : 128 * pair + 128] = jnp.where(lower_row, pltpu.roll(first, 64, 1), second)
        final.append(jnp.where(lower_row, first, pltpu.roll(second, 64, 1)))
    send(gskip_ref, gskip_hbm)
    own_group = (
        lax.broadcasted_iota(jnp.int32, (groups, channels), 1) // modes == lax.broadcasted_iota(jnp.int32, (groups, channels), 0)
    ).astype(bf16)
    own_mode = (
        lax.broadcasted_iota(jnp.int32, (modes, channels), 1) % modes == lax.broadcasted_iota(jnp.int32, (modes, channels), 0)
    )
    high, low = split(jnp.where(own_mode, jnp.concatenate(final, axis=1), 0.0))
    over_lanes = (((1,), (1,)), ((), ()))
    by_group = lax.dot_general(high, own_group, over_lanes, preferred_element_type=f32)
    by_group += lax.dot_general(low, own_group, over_lanes, preferred_element_type=f32)
    gres_ref[...] = by_group * jnp.sqrt(1.0 - jnp.exp(-2.0 * rate_ref[...]))
    send(gres_ref, gres_hbm)
    for copy in copies:
        copy.wait()


def transform(rows):
    frequency = np.pi * (2 * np.arange(rows // 2) + 1) / rows
    angle = frequency[:, None] * np.arange(rows)[None, :]
    forward = np.concatenate([np.cos(angle), -np.sin(angle)], axis=0)
    high = forward.astype(jnp.bfloat16)
    low = (forward - high.astype(np.float64)).astype(jnp.bfloat16)
    both = np.stack([high, low])
    back = (both.transpose(0, 2, 1).astype(np.float32) * (2.0 / rows)).astype(jnp.bfloat16)
    trig = np.zeros((rows // 2, 128), np.float32)
    trig[:, 0] = 2.0 * np.sin(frequency / 2.0) ** 2
    trig[:, 1] = np.sin(frequency)
    return jnp.asarray(both), jnp.asarray(back), jnp.asarray(trig)


def shards(nctx, ndp, inputs, cotangent, residues, decay_rates, skip_gain):
    _, rows, channels = inputs.shape
    groups, modes = residues.shape
    sizes = (nctx, ndp, rows, channels, groups, modes, 1.0 / math.sqrt(rows * nctx * ndp))
    forward, back, trig = transform(rows)
    hbm = pl.BlockSpec(memory_space=pltpu.HBM)
    vmem = pl.BlockSpec(memory_space=pltpu.VMEM)
    wide = (1, rows, channels)
    parts = pl.pallas_call(
        functools.partial(kernel, sizes),
        out_shape=(
            jax.ShapeDtypeStruct((rows, channels), bf16),
            jax.ShapeDtypeStruct((rows, channels), f32),
            jax.ShapeDtypeStruct((2, rows, channels), bf16),
            jax.ShapeDtypeStruct((modes, channels), f32),
            jax.ShapeDtypeStruct((nctx, 1, 128), f32),
        ),
        in_specs=[hbm] * 8,
        out_specs=(vmem,) * 5,
        scratch_shapes=[
            pltpu.VMEM((rows, channels), bf16),
            pltpu.VMEM((rows, channels), bf16),
            pltpu.VMEM((modes, groups), f32),
            pltpu.VMEM((modes, groups), f32),
            pltpu.VMEM((1, channels), f32),
            pltpu.VMEM((2, rows, rows), bf16),
            pltpu.VMEM((2, rows, rows), bf16),
            pltpu.VMEM((rows // 2, 128), f32),
            pltpu.VMEM((2, rows, channels), bf16),
            pltpu.VMEM((rows, channels), f32),
            pltpu.VMEM((rows, channels), f32),
            pltpu.VMEM((rows, channels), f32),
            pltpu.VMEM((rows, channels), f32),
            pltpu.VMEM((1, channels), f32),
            pltpu.VMEM((2, modes, channels), f32),
            pltpu.VMEM((3, modes, channels), f32),
            pltpu.VMEM((3, nctx, 8, 128), f32),
            pltpu.VMEM((nctx, 8, 128), f32),
            pltpu.VMEM((2, nctx, 8, 128), f32),
            pltpu.VMEM((nctx, 8, 128), f32),
            pltpu.VMEM((2, nctx, 8, 128), f32),
            pltpu.VMEM((nctx, 1, 128), f32),
            pltpu.VMEM((nctx, 1, 128), f32),
            pltpu.VMEM((1, 128), f32),
            pltpu.VMEM((2, nctx, 8, 128), f32),
            pltpu.VMEM((1, 128), f32),
            pltpu.VMEM((2, nctx, 1, 128), f32),
            pltpu.SemaphoreType.DMA((8,)),
            pltpu.SemaphoreType.DMA((6, nctx)),
            pltpu.SemaphoreType.DMA((6, nctx)),
            pltpu.SemaphoreType.DMA((ndp,)),
            pltpu.SemaphoreType.DMA((ndp,)),
        ],
        compiler_params=pltpu.CompilerParams(collective_id=0, has_side_effects=True, vmem_limit_bytes=32 * 1024 * 1024),
        name="hyena",
    )(*[pltpu.with_memory_space_constraint(a, pltpu.HBM) for a in (inputs, cotangent, residues.T, decay_rates.T, skip_gain.reshape(1, channels), forward, back, trig)])
    outputs, grad_inputs, grad_residues, grad_skip = pl.pallas_call(
        last_kernel,
        out_shape=(
            jax.ShapeDtypeStruct(wide, bf16),
            jax.ShapeDtypeStruct(wide, bf16),
            jax.ShapeDtypeStruct((modes, groups), f32),
            jax.ShapeDtypeStruct((1, channels), f32),
        ),
        in_specs=[vmem] * 6,
        out_specs=(hbm,) * 4,
        scratch_shapes=[
            pltpu.VMEM((rows, channels), bf16),
            pltpu.VMEM((modes, groups), f32),
            pltpu.VMEM((1, channels), f32),
            pltpu.SemaphoreType.DMA((3 + channels // 256,)),
        ],
        compiler_params=pltpu.CompilerParams(vmem_limit_bytes=32 * 1024 * 1024),
        name="last",
    )(*parts, decay_rates.T)
    return outputs, grad_inputs, grad_residues.T, grad_skip.reshape(channels)


def solution(mesh):
    placed = (P("dp", "ctx", "tp"), P("dp", "ctx", "tp"), P("tp", None), P("tp", None), P("tp"))
    return jax.shard_map(
        functools.partial(shards, mesh.shape["ctx"], mesh.shape["dp"]),
        mesh=mesh,
        in_specs=placed,
        out_specs=(P("dp", "ctx", "tp"), P("dp", "ctx", "tp"), P("tp", None), P("tp")),
        check_vma=False,
    )
```

```python
import functools
import math

import jax
import jax.numpy as jnp
import numpy as np
from jax import lax
from jax.experimental import pallas as pl
from jax.experimental.pallas import tpu as pltpu
from jax.sharding import PartitionSpec as P

MESH = pl.DeviceIdType.MESH
highest = lax.Precision.HIGHEST
f32 = jnp.float32
bf16 = jnp.bfloat16
COMM = True
UNROLL = True


def split(value):
    high = value.astype(bf16)
    return high, (value - high.astype(f32)).astype(bf16)


def times(left, right):
    total = jnp.dot(left[0], right[0], preferred_element_type=f32)
    total += jnp.dot(left[0], right[1], preferred_element_type=f32)
    return total + jnp.dot(left[1], right[0], preferred_element_type=f32)


def times_row(left, right):
    return jnp.dot(left, right, precision=highest, preferred_element_type=f32)


def split_store(target, piece, value):
    high, low = split(value)
    target[0, :, piece] = high
    target[1, :, piece] = low


def same_block(shape):
    return lax.broadcasted_iota(jnp.int32, shape, 0) // 16 == lax.broadcasted_iota(jnp.int32, shape, 1) // 16


def on_blocks(piece):
    return jnp.where(same_block((256, 256)), jnp.concatenate([piece] * 16, axis=0), 0.0)


def off_blocks(array):
    return jnp.sum(jnp.where(same_block((256, 256)), array, 0.0).reshape(16, 16, 256), axis=0)


def kernel(sizes, x_hbm, d_hbm, res_hbm, rate_hbm, skip_hbm, fwd_hbm, inv_hbm, trig_hbm,
           y_ref, zlocal, wb_ref, carried_ref, final_ref,
           x_ref, d_ref, res_ref, rate_ref, skip_ref, fwd_ref, inv_ref, trig_ref,
           wf_ref, h_ref, x_hat, d_hat, ylocal, rate_row, states, coefs, packs, e_send, e_recv, s_send, s_recv,
           g_send, g_recv, p_recv, o_send, o_recv, load_sem, send_sem, recv_sem, osend_sem, orecv_sem, ring_sem):
    nctx, ndp, rows, channels, groups, modes, scale = sizes
    half = rows // 2
    tiles = channels // 256
    me = lax.axis_index("ctx")
    mine = lax.axis_index("dp")

    barrier = pltpu.get_barrier_semaphore()

    def greet(step, carried):
        pl.semaphore_signal(barrier, inc=1, device_id={"ctx": lax.rem(me + step, nctx)}, device_id_type=MESH)
        return carried

    if COMM:
        lax.fori_loop(1, nctx, greet, 0)
        for step in range(1, ndp):
            pl.semaphore_signal(barrier, inc=1, device_id={"dp": lax.rem(mine + step, ndp)}, device_id_type=MESH)

    loads = [
        pltpu.make_async_copy(source, target, load_sem.at[number])
        for number, (source, target) in enumerate(
            [(rate_hbm, rate_ref), (res_hbm, res_ref), (x_hbm.at[0], x_ref), (d_hbm.at[0], d_ref), (trig_hbm, trig_ref),
             (fwd_hbm, fwd_ref), (inv_hbm, inv_ref), (skip_hbm, skip_ref)]
        )
    ]
    for load in loads:
        load.start()

    lanes = lax.broadcasted_iota(jnp.int32, (8, 128), 1)
    lower = lanes < 64
    lower_row = lax.broadcasted_iota(jnp.int32, (1, 128), 1) < 64
    positions = lax.broadcasted_iota(jnp.int32, (rows, 1), 0).astype(f32)
    own_group = (
        lax.broadcasted_iota(jnp.int32, (groups, channels), 1) // modes == lax.broadcasted_iota(jnp.int32, (groups, channels), 0)
    ).astype(f32)
    own_mode = (
        lax.broadcasted_iota(jnp.int32, (modes, channels), 1) % modes == lax.broadcasted_iota(jnp.int32, (modes, channels), 0)
    )

    def by_tiles(body):
        if UNROLL:
            for q in range(tiles):
                body(q, slice(256 * q, 256 * q + 256))
        else:
            def turn(q, carried):
                body(q, pl.ds(pl.multiple_of(q * 256, 256), 256))
                return carried

            lax.fori_loop(0, tiles, turn, 0)

    def pack(array, target):
        for pair in range(nctx // 2):
            low = array[0:8, 128 * pair : 128 * pair + 128]
            high = array[8:16, 128 * pair : 128 * pair + 128]
            target[2 * pair] = jnp.where(lower, low, pltpu.roll(high, 64, 1))
            target[2 * pair + 1] = jnp.where(lower, pltpu.roll(low, 64, 1), high)

    def unpack(source):
        lows, highs = [], []
        for pair in range(nctx // 2):
            first, second = source[2 * pair], source[2 * pair + 1]
            lows.append(jnp.where(lower, first, pltpu.roll(second, 64, 1)))
            highs.append(jnp.where(lower, pltpu.roll(first, 64, 1), second))
        return jnp.concatenate([jnp.concatenate(lows, axis=1), jnp.concatenate(highs, axis=1)], axis=0)

    def transposed_dot(left, right):
        return lax.dot_general(left, right, (((0,), (0,)), ((), ())), preferred_element_type=f32)

    loads[0].wait()
    rate_wide = times_row(rate_ref[...], own_group)
    rate_row[...] = jnp.sum(jnp.where(own_mode, rate_wide, 0.0), axis=0, keepdims=True)

    def end_states(q, piece):
        split_store(wb_ref, piece, jnp.exp(-rate_row[:, piece] * (rows - 1.0 - positions)))
        full = transposed_dot(wb_ref[0, :, piece], x_ref[:, piece]) + transposed_dot(wb_ref[1, :, piece], x_ref[:, piece])
        states[0, :, piece] = off_blocks(full)

    def start_states(q, piece):
        split_store(wf_ref, piece, jnp.exp(-rate_row[:, piece] * positions))
        full = transposed_dot(wf_ref[0, :, piece], d_ref[:, piece]) + transposed_dot(wf_ref[1, :, piece], d_ref[:, piece])
        states[1, :, piece] = off_blocks(full)

    loads[2].wait()
    by_tiles(end_states)
    pack(states[0], e_send)
    loads[3].wait()
    by_tiles(start_states)
    pack(states[1], s_send)

    def state_copy(there, kind, send, recv, slot_there):
        return pltpu.make_async_remote_copy(
            src_ref=send.at[there],
            dst_ref=recv.at[slot_there],
            send_sem=send_sem.at[kind, there],
            recv_sem=recv_sem.at[kind, slot_there],
            device_id={"ctx": there},
            device_id_type=MESH,
        )

    def over_peers(body):
        def turn(step, carried):
            body(lax.rem(me + step, nctx))
            return carried

        if COMM:
            lax.fori_loop(1, nctx, turn, 0)

    def send_all(kind, send, recv):
        def turn(count, carried):
            step = nctx // 2 + jnp.where(count % 2 == 1, -((count + 1) // 2), count // 2)
            state_copy(lax.rem(me + step, nctx), kind, send, recv, me).start()
            return carried

        if COMM:
            lax.fori_loop(0, nctx - 1, turn, 0)

    def await_all(kind, send, recv):
        over_peers(lambda origin: state_copy(origin, kind, send, recv, origin).wait_recv())

    def await_sent(kind, send, recv):
        over_peers(lambda origin: state_copy(origin, kind, send, recv, origin).wait_send())

    for load in loads[4:]:
        load.wait()

    def spectra(q, piece):
        step_piece = jnp.exp(-rate_row[:, piece])
        less_cos, sine = trig_ref[:, 0:1], trig_ref[:, 1:2]
        rest = 1.0 - step_piece
        near = step_piece * less_cos
        below = 1.0 / (rest * rest + 2.0 * near)
        h_ref[0:half, piece] = (rest + near) * below
        h_ref[half:rows, piece] = (-step_piece * sine) * below
        x_piece, d_piece = x_ref[:, piece], d_ref[:, piece]
        x_new = jnp.dot(fwd_ref[0], x_piece, preferred_element_type=f32) + jnp.dot(fwd_ref[1], x_piece, preferred_element_type=f32)
        d_new = jnp.dot(fwd_ref[0], d_piece, preferred_element_type=f32) + jnp.dot(fwd_ref[1], d_piece, preferred_element_type=f32)
        x_hat[:, piece] = x_new
        d_hat[:, piece] = d_new
        x_re, x_im, d_re, d_im = x_new[0:half], x_new[half:rows], d_new[0:half], d_new[half:rows]
        cross = jnp.concatenate([d_re * x_re + d_im * x_im, d_im * x_re - d_re * x_im], axis=0)
        cross_high, cross_low = split(cross)
        ones = same_block((256, 256)).astype(bf16)
        grouped = jnp.dot(cross_high, ones, preferred_element_type=f32) + jnp.dot(cross_low, ones, preferred_element_type=f32)
        grad_piece = jnp.sum(grouped * h_ref[:, piece], axis=0, keepdims=True) * (2.0 / rows)
        skip_piece = jnp.sum(x_piece.astype(f32) * d_piece.astype(f32), axis=0, keepdims=True)
        for part in range(2):
            pair = 2 * q + part
            grad_row, skip_row = grad_piece[:, 128 * part : 128 * part + 128], skip_piece[:, 128 * part : 128 * part + 128]
            g_send[2 * pair] = jnp.where(lower_row, grad_row, pltpu.roll(skip_row, 64, 1))
            g_send[2 * pair + 1] = jnp.where(lower_row, pltpu.roll(grad_row, 64, 1), skip_row)

    by_tiles(spectra)

    if COMM:
        pl.semaphore_wait(barrier, nctx - 1 + ndp - 1)
        for step in range(1, ndp):
            pl.semaphore_signal(ring_sem, inc=1, device_id={"dp": lax.rem(mine + step, ndp)}, device_id_type=MESH)
    send_all(0, e_send, e_recv.at[0])
    send_all(2, g_send, g_recv)
    send_all(1, s_send, s_recv.at[0])
    e_recv[0, me] = e_send[me]
    s_recv[0, me] = s_send[me]
    g_recv[me] = g_send[me]

    loads[1].wait()
    coefs[0] = times_row(res_ref[...], own_group) * jnp.sqrt(1.0 - jnp.exp(-2.0 * rate_wide))
    step_wide = jnp.exp(-rate_wide)
    block_wide = jnp.exp(-rate_wide * float(rows))
    inverse_wide = 1.0 / (1.0 + block_wide)
    coefs[1] = coefs[0] * step_wide
    coefs[2] = inverse_wide
    pack(block_wide, packs.at[0])
    pack(inverse_wide, packs.at[1])
    pack(step_wide, packs.at[2])

    def own_part(q, piece):
        response = times(split(h_ref[:, piece]), split(on_blocks(coefs[0, :, piece])))
        f_re, f_im = response[0:half], response[half:rows]
        x_re, x_im, d_re, d_im = x_hat[0:half, piece], x_hat[half:rows, piece], d_hat[0:half, piece], d_hat[half:rows, piece]
        skip = skip_ref[:, piece]
        y_hat = jnp.concatenate([f_re * x_re - f_im * x_im, f_re * x_im + f_im * x_re], axis=0)
        ylocal[:, piece] = times((inv_ref[0], inv_ref[1]), split(y_hat)) + skip * x_ref[:, piece].astype(f32)
        z_hat = jnp.concatenate([f_re * d_re + f_im * d_im, f_re * d_im - f_im * d_re], axis=0)
        zlocal[:, piece] = times((inv_ref[0], inv_ref[1]), split(z_hat)) + skip * d_ref[:, piece].astype(f32)

    by_tiles(own_part)

    block_own, inverse_own, step_own = packs[0, me], packs[1, me], packs[2, me]
    await_all(0, e_send, e_recv.at[0])
    running = jnp.zeros((8, 128), f32)
    for block in range(nctx):
        e_recv[1, block] = running
        running = running * block_own + e_recv[0, block]
    send_all(3, e_recv.at[1], p_recv.at[0])
    p_recv[0, me] = e_recv[1, me]
    await_all(2, g_send, g_recv)
    gradient = g_recv[0]
    for block in range(1, nctx):
        gradient += g_recv[block]
    await_all(1, s_send, s_recv.at[0])
    running = jnp.zeros((8, 128), f32)
    owned = jnp.zeros((8, 128), f32)
    for block in range(nctx - 1, -1, -1):
        s_recv[1, block] = running
        start = s_recv[0, block]
        running = running * block_own + start
        owned += start * (e_recv[1, block] + e_recv[0, block] * inverse_own)
    send_all(4, s_recv.at[1], p_recv.at[1])
    p_recv[1, me] = s_recv[1, me]
    high, low = split(owned * step_own)
    lane_row = lax.broadcasted_iota(jnp.int32, (128, 128), 0)
    lane_column = lax.broadcasted_iota(jnp.int32, (128, 128), 1)
    chosen = (
        (lane_row // 64 == (lane_column % 16) // 8) & ((lane_row % 64) // 16 == lane_column // 16)
    ).astype(bf16)
    summed = jnp.dot(high, chosen, preferred_element_type=f32) + jnp.dot(low, chosen, preferred_element_type=f32)
    right_row = lax.broadcasted_iota(jnp.int32, (8, 128), 0) == lanes % 8
    gradient += jnp.sum(jnp.where(right_row & lower, summed, 0.0), axis=0, keepdims=True)
    o_send[...] = gradient * scale
    o_recv[mine, me] = gradient * scale

    def gradient_copy(part, there, slot_part, slot):
        return pltpu.make_async_remote_copy(
            src_ref=o_send,
            dst_ref=o_recv.at[slot_part, slot],
            send_sem=osend_sem.at[part, there],
            recv_sem=orecv_sem.at[slot_part, slot],
            device_id={"dp": part, "ctx": there},
            device_id_type=MESH,
        )

    def over_parts(body):
        for offset in range(ndp):
            part = lax.rem(mine + offset, ndp)

            def turn(count, carried):
                step = nctx // 2 + jnp.where(count % 2 == 1, -((count + 1) // 2), count // 2)
                body(part, lax.rem(me + step, nctx))
                return carried

            if COMM:
                lax.fori_loop(0, nctx - 1 if offset == 0 else nctx, turn, 0)

    if COMM:
        pl.semaphore_wait(ring_sem, ndp - 1)
    over_parts(lambda part, there: gradient_copy(part, there, mine, me).start())

    await_all(3, e_recv.at[1], p_recv.at[0])
    carried_ref[...] = (unpack(p_recv.at[0]) + states[0] * coefs[2]) * coefs[1]

    def finish(q, piece):
        product = times((wf_ref[0, :, piece], wf_ref[1, :, piece]), split(on_blocks(carried_ref[:, piece])))
        y_ref[:, piece] = (ylocal[:, piece] + product).astype(bf16)

    by_tiles(finish)
    await_all(4, s_recv.at[1], p_recv.at[1])
    carried_ref[...] = (unpack(p_recv.at[1]) + states[1] * coefs[2]) * coefs[1]
    over_parts(lambda part, there: gradient_copy(part, there, part, there).wait_recv())
    final_ref[...] = o_recv[...]

    for sent in ((0, e_send, e_recv.at[0]), (1, s_send, s_recv.at[0]), (2, g_send, g_recv),
                 (3, e_recv.at[1], p_recv.at[0]), (4, s_recv.at[1], p_recv.at[1])):
        await_sent(*sent)
    over_parts(lambda part, there: gradient_copy(part, there, part, there).wait_send())


def last_kernel(y_in, zlocal, wb_ref, carried_ref, final_ref, rate_ref, y_hbm, z_hbm, gres_hbm, gskip_hbm,
                z_ref, gres_ref, gskip_ref, sem):
    channels = zlocal.shape[1]
    modes, groups = rate_ref.shape
    copies = []

    def send(source, target):
        copies.append(pltpu.make_async_copy(source, target, sem.at[len(copies)]))
        copies[-1].start()

    send(y_in, y_hbm.at[0])
    lower_row = lax.broadcasted_iota(jnp.int32, (1, 128), 1) < 64
    totals = jnp.sum(final_ref[...], axis=0)
    final = []
    for pair in range(channels // 128):
        first, second = totals[2 * pair], totals[2 * pair + 1]
        gskip_ref[:, 128 * pair : 128 * pair + 128] = jnp.where(lower_row, pltpu.roll(first, 64, 1), second)
        final.append(jnp.where(lower_row, first, pltpu.roll(second, 64, 1)))
    send(gskip_ref, gskip_hbm)
    own_group = (
        lax.broadcasted_iota(jnp.int32, (groups, channels), 1) // modes == lax.broadcasted_iota(jnp.int32, (groups, channels), 0)
    ).astype(bf16)
    own_mode = (
        lax.broadcasted_iota(jnp.int32, (modes, channels), 1) % modes == lax.broadcasted_iota(jnp.int32, (modes, channels), 0)
    )
    high, low = split(jnp.where(own_mode, jnp.concatenate(final, axis=1), 0.0))
    over_lanes = (((1,), (1,)), ((), ()))
    by_group = lax.dot_general(high, own_group, over_lanes, preferred_element_type=f32)
    by_group += lax.dot_general(low, own_group, over_lanes, preferred_element_type=f32)
    gres_ref[...] = by_group * jnp.sqrt(1.0 - jnp.exp(-2.0 * rate_ref[...]))
    send(gres_ref, gres_hbm)
    for q in range(channels // 256):
        piece = slice(256 * q, 256 * q + 256)
        product = times((wb_ref[0, :, piece], wb_ref[1, :, piece]), split(on_blocks(carried_ref[:, piece])))
        z_ref[:, piece] = (zlocal[:, piece] + product).astype(bf16)
        send(z_ref.at[:, piece], z_hbm.at[0, :, piece])
    for copy in copies:
        copy.wait()


def transform(rows):
    frequency = np.pi * (2 * np.arange(rows // 2) + 1) / rows
    angle = frequency[:, None] * np.arange(rows)[None, :]
    forward = np.concatenate([np.cos(angle), -np.sin(angle)], axis=0)
    high = forward.astype(jnp.bfloat16)
    low = (forward - high.astype(np.float64)).astype(jnp.bfloat16)
    both = np.stack([high, low])
    back = (both.transpose(0, 2, 1).astype(np.float32) * (2.0 / rows)).astype(jnp.bfloat16)
    trig = np.zeros((rows // 2, 128), np.float32)
    trig[:, 0] = 2.0 * np.sin(frequency / 2.0) ** 2
    trig[:, 1] = np.sin(frequency)
    return jnp.asarray(both), jnp.asarray(back), jnp.asarray(trig)


def shards(nctx, ndp, inputs, cotangent, residues, decay_rates, skip_gain):
    _, rows, channels = inputs.shape
    groups, modes = residues.shape
    sizes = (nctx, ndp, rows, channels, groups, modes, 1.0 / math.sqrt(rows * nctx * ndp))
    forward, back, trig = transform(rows)
    hbm = pl.BlockSpec(memory_space=pltpu.HBM)
    vmem = pl.BlockSpec(memory_space=pltpu.VMEM)
    wide = (1, rows, channels)
    parts = pl.pallas_call(
        functools.partial(kernel, sizes),
        out_shape=(
            jax.ShapeDtypeStruct((rows, channels), bf16),
            jax.ShapeDtypeStruct((rows, channels), f32),
            jax.ShapeDtypeStruct((2, rows, channels), bf16),
            jax.ShapeDtypeStruct((modes, channels), f32),
            jax.ShapeDtypeStruct((ndp, nctx, 1, 128), f32),
        ),
        in_specs=[hbm] * 8,
        out_specs=(vmem,) * 5,
        scratch_shapes=[
            pltpu.VMEM((rows, channels), bf16),
            pltpu.VMEM((rows, channels), bf16),
            pltpu.VMEM((modes, groups), f32),
            pltpu.VMEM((modes, groups), f32),
            pltpu.VMEM((1, channels), f32),
            pltpu.VMEM((2, rows, rows), bf16),
            pltpu.VMEM((2, rows, rows), bf16),
            pltpu.VMEM((rows // 2, 128), f32),
            pltpu.VMEM((2, rows, channels), bf16),
            pltpu.VMEM((rows, channels), f32),
            pltpu.VMEM((rows, channels), f32),
            pltpu.VMEM((rows, channels), f32),
            pltpu.VMEM((rows, channels), f32),
            pltpu.VMEM((1, channels), f32),
            pltpu.VMEM((2, modes, channels), f32),
            pltpu.VMEM((3, modes, channels), f32),
            pltpu.VMEM((3, nctx, 8, 128), f32),
            pltpu.VMEM((nctx, 8, 128), f32),
            pltpu.VMEM((2, nctx, 8, 128), f32),
            pltpu.VMEM((nctx, 8, 128), f32),
            pltpu.VMEM((2, nctx, 8, 128), f32),
            pltpu.VMEM((nctx, 1, 128), f32),
            pltpu.VMEM((nctx, 1, 128), f32),
            pltpu.VMEM((2, nctx, 8, 128), f32),
            pltpu.VMEM((1, 128), f32),
            pltpu.VMEM((ndp, nctx, 1, 128), f32),
            pltpu.SemaphoreType.DMA((8,)),
            pltpu.SemaphoreType.DMA((5, nctx)),
            pltpu.SemaphoreType.DMA((5, nctx)),
            pltpu.SemaphoreType.DMA((ndp, nctx)),
            pltpu.SemaphoreType.DMA((ndp, nctx)),
            pltpu.SemaphoreType.REGULAR,
        ],
        compiler_params=pltpu.CompilerParams(collective_id=0, has_side_effects=True, vmem_limit_bytes=32 * 1024 * 1024),
        name="hyena",
    )(*[pltpu.with_memory_space_constraint(a, pltpu.HBM) for a in (inputs, cotangent, residues.T, decay_rates.T, skip_gain.reshape(1, channels), forward, back, trig)])
    outputs, grad_inputs, grad_residues, grad_skip = pl.pallas_call(
        last_kernel,
        out_shape=(
            jax.ShapeDtypeStruct(wide, bf16),
            jax.ShapeDtypeStruct(wide, bf16),
            jax.ShapeDtypeStruct((modes, groups), f32),
            jax.ShapeDtypeStruct((1, channels), f32),
        ),
        in_specs=[vmem] * 6,
        out_specs=(hbm,) * 4,
        scratch_shapes=[
            pltpu.VMEM((rows, channels), bf16),
            pltpu.VMEM((modes, groups), f32),
            pltpu.VMEM((1, channels), f32),
            pltpu.SemaphoreType.DMA((3 + channels // 256,)),
        ],
        compiler_params=pltpu.CompilerParams(vmem_limit_bytes=32 * 1024 * 1024),
        name="last",
    )(*parts, decay_rates.T)
    return outputs, grad_inputs, grad_residues.T, grad_skip.reshape(channels)


def solution(mesh):
    placed = (P("dp", "ctx", "tp"), P("dp", "ctx", "tp"), P("tp", None), P("tp", None), P("tp"))
    return jax.shard_map(
        functools.partial(shards, mesh.shape["ctx"], mesh.shape["dp"]),
        mesh=mesh,
        in_specs=placed,
        out_specs=(P("dp", "ctx", "tp"), P("dp", "ctx", "tp"), P("tp", None), P("tp")),
        check_vma=False,
    )
```

```python
import functools
import math

import jax
import jax.numpy as jnp
import numpy as np
from jax import lax
from jax.experimental import pallas as pl
from jax.experimental.pallas import tpu as pltpu
from jax.sharding import PartitionSpec as P

MESH = pl.DeviceIdType.MESH
highest = lax.Precision.HIGHEST
f32 = jnp.float32
bf16 = jnp.bfloat16
COMM = True
UNROLL = True


def split(value):
    high = value.astype(bf16)
    return high, (value - high.astype(f32)).astype(bf16)


def times(left, right):
    total = jnp.dot(left[0], right[0], preferred_element_type=f32)
    total += jnp.dot(left[0], right[1], preferred_element_type=f32)
    return total + jnp.dot(left[1], right[0], preferred_element_type=f32)


def times_row(left, right):
    return jnp.dot(left, right, precision=highest, preferred_element_type=f32)


def split_store(target, piece, value):
    high, low = split(value)
    target[0, :, piece] = high
    target[1, :, piece] = low


def same_block(shape):
    return lax.broadcasted_iota(jnp.int32, shape, 0) // 16 == lax.broadcasted_iota(jnp.int32, shape, 1) // 16


def on_blocks(piece):
    return jnp.where(same_block((256, 256)), jnp.concatenate([piece] * 16, axis=0), 0.0)


def off_blocks(array):
    return jnp.sum(jnp.where(same_block((256, 256)), array, 0.0).reshape(16, 16, 256), axis=0)


def kernel(sizes, x_hbm, d_hbm, res_hbm, rate_hbm, skip_hbm, fwd_hbm, inv_hbm, trig_hbm,
           y_ref, z_ref, final_ref, weight_ref, chosen_ref,
           x_ref, d_ref, res_ref, rate_ref, skip_ref, fwd_ref, inv_ref, trig_ref,
           wf_ref, wb_ref, h_ref, x_hat, d_hat, ylocal, zlocal, rate_row, states, coefs, carried_ref, packs,
           out_send, out_recv, back_send, back_recv, p_send, from_dp, o_send, o_recv,
           load_sem, send_sem, recv_sem, psend_sem, precv_sem):
    nctx, ndp, rows, channels, groups, modes, scale = sizes
    half = rows // 2
    tiles = channels // 256
    me = lax.axis_index("ctx")
    mine = lax.axis_index("dp")

    barrier = pltpu.get_barrier_semaphore()

    def far_first(count):
        return nctx // 2 + jnp.where(count % 2 == 1, -((count + 1) // 2), count // 2)

    def greet(count, carried):
        step = far_first(count)
        pl.semaphore_signal(barrier, inc=1, device_id={"ctx": lax.rem(me + step, nctx)}, device_id_type=MESH)
        return carried

    if COMM:
        lax.fori_loop(0, nctx - 1, greet, 0)
        for step in range(1, ndp):
            pl.semaphore_signal(barrier, inc=1, device_id={"dp": lax.rem(mine + step, ndp)}, device_id_type=MESH)

    loads = [
        pltpu.make_async_copy(source, target, load_sem.at[number])
        for number, (source, target) in enumerate(
            [(rate_hbm, rate_ref), (res_hbm, res_ref), (x_hbm.at[0], x_ref), (d_hbm.at[0], d_ref), (trig_hbm, trig_ref),
             (fwd_hbm, fwd_ref), (inv_hbm, inv_ref), (skip_hbm, skip_ref)]
        )
    ]
    for load in loads:
        load.start()

    lanes = lax.broadcasted_iota(jnp.int32, (8, 128), 1)
    lower = lanes < 64
    lower_row = lax.broadcasted_iota(jnp.int32, (1, 128), 1) < 64
    positions = lax.broadcasted_iota(jnp.int32, (rows, 1), 0).astype(f32)
    own_group = (
        lax.broadcasted_iota(jnp.int32, (groups, channels), 1) // modes == lax.broadcasted_iota(jnp.int32, (groups, channels), 0)
    ).astype(f32)
    own_mode = (
        lax.broadcasted_iota(jnp.int32, (modes, channels), 1) % modes == lax.broadcasted_iota(jnp.int32, (modes, channels), 0)
    )

    def by_tiles(body):
        if UNROLL:
            for q in range(tiles):
                body(q, slice(256 * q, 256 * q + 256))
        else:
            def turn(q, carried):
                body(q, pl.ds(pl.multiple_of(q * 256, 256), 256))
                return carried

            lax.fori_loop(0, tiles, turn, 0)

    def pack(array, target, top):
        for pair in range(nctx // 2):
            low = array[0:8, 128 * pair : 128 * pair + 128]
            high = array[8:16, 128 * pair : 128 * pair + 128]
            target[2 * pair, top : top + 8] = jnp.where(lower, low, pltpu.roll(high, 64, 1))
            target[2 * pair + 1, top : top + 8] = jnp.where(lower, pltpu.roll(low, 64, 1), high)

    def unpack(source, top):
        lows, highs = [], []
        for pair in range(nctx // 2):
            first, second = source[2 * pair, top : top + 8], source[2 * pair + 1, top : top + 8]
            lows.append(jnp.where(lower, first, pltpu.roll(second, 64, 1)))
            highs.append(jnp.where(lower, pltpu.roll(first, 64, 1), second))
        return jnp.concatenate([jnp.concatenate(lows, axis=1), jnp.concatenate(highs, axis=1)], axis=0)

    def transposed_dot(left, right):
        return lax.dot_general(left, right, (((0,), (0,)), ((), ())), preferred_element_type=f32)

    loads[0].wait()
    rate_wide = times_row(rate_ref[...], own_group)
    rate_row[...] = jnp.sum(jnp.where(own_mode, rate_wide, 0.0), axis=0, keepdims=True)

    def end_states(q, piece):
        split_store(wb_ref, piece, jnp.exp(-rate_row[:, piece] * (rows - 1.0 - positions)))
        full = transposed_dot(wb_ref[0, :, piece], x_ref[:, piece]) + transposed_dot(wb_ref[1, :, piece], x_ref[:, piece])
        states[0, :, piece] = off_blocks(full)

    def start_states(q, piece):
        split_store(wf_ref, piece, jnp.exp(-rate_row[:, piece] * positions))
        full = transposed_dot(wf_ref[0, :, piece], d_ref[:, piece]) + transposed_dot(wf_ref[1, :, piece], d_ref[:, piece])
        states[1, :, piece] = off_blocks(full)

    loads[2].wait()
    by_tiles(end_states)
    pack(states[0], out_send, 0)
    loads[3].wait()
    by_tiles(start_states)
    pack(states[1], out_send, 8)

    def state_copy(there, kind, send, recv, slot_there):
        return pltpu.make_async_remote_copy(
            src_ref=send.at[there] if kind < 2 else send,
            dst_ref=recv.at[slot_there],
            send_sem=send_sem.at[kind, there],
            recv_sem=recv_sem.at[kind, slot_there],
            device_id={"ctx": there},
            device_id_type=MESH,
        )

    def over_peers(body):
        def turn(step, carried):
            body(lax.rem(me + step, nctx))
            return carried

        if COMM:
            lax.fori_loop(1, nctx, turn, 0)

    def send_all(kind, send, recv):
        def turn(count, carried):
            state_copy(lax.rem(me + far_first(count), nctx), kind, send, recv, me).start()
            return carried

        if COMM:
            lax.fori_loop(0, nctx - 1, turn, 0)

    def await_all(kind, send, recv):
        over_peers(lambda origin: state_copy(origin, kind, send, recv, origin).wait_recv())

    def await_sent(kind, send, recv):
        over_peers(lambda origin: state_copy(origin, kind, send, recv, origin).wait_send())

    for load in loads[4:]:
        load.wait()

    def spectra(q, piece):
        step_piece = jnp.exp(-rate_row[:, piece])
        less_cos, sine = trig_ref[:, 0:1], trig_ref[:, 1:2]
        rest = 1.0 - step_piece
        near = step_piece * less_cos
        below = 1.0 / (rest * rest + 2.0 * near)
        h_ref[0:half, piece] = (rest + near) * below
        h_ref[half:rows, piece] = (-step_piece * sine) * below
        x_piece, d_piece = x_ref[:, piece], d_ref[:, piece]
        x_new = jnp.dot(fwd_ref[0], x_piece, preferred_element_type=f32) + jnp.dot(fwd_ref[1], x_piece, preferred_element_type=f32)
        d_new = jnp.dot(fwd_ref[0], d_piece, preferred_element_type=f32) + jnp.dot(fwd_ref[1], d_piece, preferred_element_type=f32)
        x_hat[:, piece] = x_new
        d_hat[:, piece] = d_new
        x_re, x_im, d_re, d_im = x_new[0:half], x_new[half:rows], d_new[0:half], d_new[half:rows]
        cross = jnp.concatenate([d_re * x_re + d_im * x_im, d_im * x_re - d_re * x_im], axis=0)
        cross_high, cross_low = split(cross)
        ones = same_block((256, 256)).astype(bf16)
        grouped = jnp.dot(cross_high, ones, preferred_element_type=f32) + jnp.dot(cross_low, ones, preferred_element_type=f32)
        grad_piece = jnp.sum(grouped * h_ref[:, piece], axis=0, keepdims=True) * (2.0 / rows)
        skip_piece = jnp.sum(x_piece.astype(f32) * d_piece.astype(f32), axis=0, keepdims=True)
        for part in range(2):
            pair = 2 * q + part
            grad_row, skip_row = grad_piece[:, 128 * part : 128 * part + 128], skip_piece[:, 128 * part : 128 * part + 128]
            out_send[2 * pair, 16:17] = jnp.where(lower_row, grad_row, pltpu.roll(skip_row, 64, 1))
            out_send[2 * pair + 1, 16:17] = jnp.where(lower_row, pltpu.roll(grad_row, 64, 1), skip_row)

    by_tiles(spectra)

    if COMM:
        pl.semaphore_wait(barrier, nctx - 1 + ndp - 1)
    send_all(0, out_send, out_recv)
    out_recv[me] = out_send[me]

    loads[1].wait()
    coefs[0] = times_row(res_ref[...], own_group) * jnp.sqrt(1.0 - jnp.exp(-2.0 * rate_wide))
    step_wide = jnp.exp(-rate_wide)
    block_wide = jnp.exp(-rate_wide * float(rows))
    inverse_wide = 1.0 / (1.0 + block_wide)
    coefs[1] = coefs[0] * step_wide
    coefs[2] = inverse_wide
    pack(block_wide, packs.at[0], 0)
    pack(inverse_wide, packs.at[1], 0)
    pack(step_wide, packs.at[2], 0)

    weight_ref[...] = jnp.sqrt(1.0 - jnp.exp(-2.0 * rate_ref[...]))
    chosen_ref[...] = (
        lax.broadcasted_iota(jnp.int32, (channels, groups), 0) // modes == lax.broadcasted_iota(jnp.int32, (channels, groups), 1)
    ).astype(bf16)

    def own_part(q, piece):
        response = times(split(h_ref[:, piece]), split(on_blocks(coefs[0, :, piece])))
        f_re, f_im = response[0:half], response[half:rows]
        x_re, x_im, d_re, d_im = x_hat[0:half, piece], x_hat[half:rows, piece], d_hat[0:half, piece], d_hat[half:rows, piece]
        skip = skip_ref[:, piece]
        y_hat = jnp.concatenate([f_re * x_re - f_im * x_im, f_re * x_im + f_im * x_re], axis=0)
        ylocal[:, piece] = times((inv_ref[0], inv_ref[1]), split(y_hat)) + skip * x_ref[:, piece].astype(f32)
        z_hat = jnp.concatenate([f_re * d_re + f_im * d_im, f_re * d_im - f_im * d_re], axis=0)
        zlocal[:, piece] = times((inv_ref[0], inv_ref[1]), split(z_hat)) + skip * d_ref[:, piece].astype(f32)

    by_tiles(own_part)

    block_own, inverse_own, step_own = packs[0, me], packs[1, me], packs[2, me]
    lane_row = lax.broadcasted_iota(jnp.int32, (128, 128), 0)
    lane_column = lax.broadcasted_iota(jnp.int32, (128, 128), 1)
    chosen = (
        (lane_row // 64 == (lane_column % 16) // 8) & ((lane_row % 64) // 16 == lane_column // 16)
    ).astype(bf16)
    right_row = lax.broadcasted_iota(jnp.int32, (8, 128), 0) == lanes % 8
    await_all(0, out_send, out_recv)
    running = jnp.zeros((8, 128), f32)
    inner = []
    for block in range(nctx):
        end = out_recv[block, 0:8]
        back_send[block, 0:8] = running
        inner.append(running + end * inverse_own)
        running = running * block_own + end
    running = jnp.zeros((8, 128), f32)
    owned = jnp.zeros((8, 128), f32)
    gradient = jnp.zeros((1, 128), f32)
    for block in range(nctx - 1, -1, -1):
        start = out_recv[block, 8:16]
        back_send[block, 8:16] = running
        running = running * block_own + start
        owned += start * inner[block]
        gradient += out_recv[block, 16:17]
    high, low = split(owned * step_own)
    summed = jnp.dot(high, chosen, preferred_element_type=f32) + jnp.dot(low, chosen, preferred_element_type=f32)
    gradient += jnp.sum(jnp.where(right_row & lower, summed, 0.0), axis=0, keepdims=True)
    p_send[...] = gradient

    def dp_copy(step, here):
        there = lax.rem(mine + step, ndp)
        slot = there if here else mine
        return pltpu.make_async_remote_copy(
            src_ref=p_send,
            dst_ref=from_dp.at[slot],
            send_sem=psend_sem.at[there],
            recv_sem=precv_sem.at[slot],
            device_id={"dp": there},
            device_id_type=MESH,
        )

    if COMM:
        for step in range(1, ndp):
            dp_copy(step, False).start()
    send_all(1, back_send, back_recv)
    back_recv[me] = back_send[me]
    from_dp[mine] = gradient
    if COMM:
        for step in range(1, ndp):
            dp_copy(step, True).wait_recv()
    gradient = from_dp[0]
    for other in range(1, ndp):
        gradient += from_dp[other]
    o_send[...] = gradient * scale
    send_all(2, o_send, o_recv)
    o_recv[me] = gradient * scale

    await_all(1, back_send, back_recv)
    carried_ref[0] = (unpack(back_recv, 0) + states[0] * coefs[2]) * coefs[1]
    carried_ref[1] = (unpack(back_recv, 8) + states[1] * coefs[2]) * coefs[1]

    def finish(q, piece):
        product = times((wf_ref[0, :, piece], wf_ref[1, :, piece]), split(on_blocks(carried_ref[0, :, piece])))
        y_ref[:, piece] = (ylocal[:, piece] + product).astype(bf16)
        product = times((wb_ref[0, :, piece], wb_ref[1, :, piece]), split(on_blocks(carried_ref[1, :, piece])))
        z_ref[:, piece] = (zlocal[:, piece] + product).astype(bf16)

    by_tiles(finish)
    for sent in ((0, out_send, out_recv), (1, back_send, back_recv), (2, o_send, o_recv)):
        await_sent(*sent)
    if COMM:
        for step in range(1, ndp):
            dp_copy(step, True).wait_send()
    await_all(2, o_send, o_recv)
    final_ref[...] = o_recv[...]


def last_kernel(y_in, z_in, final_ref, weight_ref, chosen_ref, y_hbm, z_hbm, gres_hbm, gskip_hbm, gres_ref, gskip_ref, sem):
    channels = y_in.shape[1]
    modes = weight_ref.shape[0]
    copies = []

    def send(source, target):
        copies.append(pltpu.make_async_copy(source, target, sem.at[len(copies)]))
        copies[-1].start()

    send(y_in, y_hbm.at[0])
    send(z_in, z_hbm.at[0])
    lower_row = lax.broadcasted_iota(jnp.int32, (1, 128), 1) < 64
    final = []
    for pair in range(channels // 128):
        first, second = final_ref[2 * pair], final_ref[2 * pair + 1]
        gskip_ref[:, 128 * pair : 128 * pair + 128] = jnp.where(lower_row, pltpu.roll(first, 64, 1), second)
        final.append(jnp.where(lower_row, first, pltpu.roll(second, 64, 1)))
    send(gskip_ref, gskip_hbm)
    own_mode = (
        lax.broadcasted_iota(jnp.int32, (modes, channels), 1) % modes == lax.broadcasted_iota(jnp.int32, (modes, channels), 0)
    )
    high, low = split(jnp.where(own_mode, jnp.concatenate(final, axis=1), 0.0))
    chosen = chosen_ref[...]
    by_group = jnp.dot(high, chosen, preferred_element_type=f32) + jnp.dot(low, chosen, preferred_element_type=f32)
    gres_ref[...] = by_group * weight_ref[...]
    send(gres_ref, gres_hbm)
    for copy in copies:
        copy.wait()


def transform(rows):
    frequency = np.pi * (2 * np.arange(rows // 2) + 1) / rows
    angle = frequency[:, None] * np.arange(rows)[None, :]
    forward = np.concatenate([np.cos(angle), -np.sin(angle)], axis=0)
    high = forward.astype(jnp.bfloat16)
    low = (forward - high.astype(np.float64)).astype(jnp.bfloat16)
    both = np.stack([high, low])
    back = (both.transpose(0, 2, 1).astype(np.float32) * (2.0 / rows)).astype(jnp.bfloat16)
    trig = np.zeros((rows // 2, 128), np.float32)
    trig[:, 0] = 2.0 * np.sin(frequency / 2.0) ** 2
    trig[:, 1] = np.sin(frequency)
    return jnp.asarray(both), jnp.asarray(back), jnp.asarray(trig)


def shards(nctx, ndp, inputs, cotangent, residues, decay_rates, skip_gain):
    _, rows, channels = inputs.shape
    groups, modes = residues.shape
    sizes = (nctx, ndp, rows, channels, groups, modes, 1.0 / math.sqrt(rows * nctx * ndp))
    forward, back, trig = transform(rows)
    hbm = pl.BlockSpec(memory_space=pltpu.HBM)
    vmem = pl.BlockSpec(memory_space=pltpu.VMEM)
    wide = (1, rows, channels)
    parts = pl.pallas_call(
        functools.partial(kernel, sizes),
        out_shape=(
            jax.ShapeDtypeStruct((rows, channels), bf16),
            jax.ShapeDtypeStruct((rows, channels), bf16),
            jax.ShapeDtypeStruct((nctx, 1, 128), f32),
            jax.ShapeDtypeStruct((modes, groups), f32),
            jax.ShapeDtypeStruct((channels, groups), bf16),
        ),
        in_specs=[hbm] * 8,
        out_specs=(vmem,) * 5,
        scratch_shapes=[
            pltpu.VMEM((rows, channels), bf16),
            pltpu.VMEM((rows, channels), bf16),
            pltpu.VMEM((modes, groups), f32),
            pltpu.VMEM((modes, groups), f32),
            pltpu.VMEM((1, channels), f32),
            pltpu.VMEM((2, rows, rows), bf16),
            pltpu.VMEM((2, rows, rows), bf16),
            pltpu.VMEM((rows // 2, 128), f32),
            pltpu.VMEM((2, rows, channels), bf16),
            pltpu.VMEM((2, rows, channels), bf16),
            pltpu.VMEM((rows, channels), f32),
            pltpu.VMEM((rows, channels), f32),
            pltpu.VMEM((rows, channels), f32),
            pltpu.VMEM((rows, channels), f32),
            pltpu.VMEM((rows, channels), f32),
            pltpu.VMEM((1, channels), f32),
            pltpu.VMEM((2, modes, channels), f32),
            pltpu.VMEM((3, modes, channels), f32),
            pltpu.VMEM((2, modes, channels), f32),
            pltpu.VMEM((3, nctx, 8, 128), f32),
            pltpu.VMEM((nctx, 17, 128), f32),
            pltpu.VMEM((nctx, 17, 128), f32),
            pltpu.VMEM((nctx, 16, 128), f32),
            pltpu.VMEM((nctx, 16, 128), f32),
            pltpu.VMEM((1, 128), f32),
            pltpu.VMEM((ndp, 1, 128), f32),
            pltpu.VMEM((1, 128), f32),
            pltpu.VMEM((nctx, 1, 128), f32),
            pltpu.SemaphoreType.DMA((8,)),
            pltpu.SemaphoreType.DMA((3, nctx)),
            pltpu.SemaphoreType.DMA((3, nctx)),
            pltpu.SemaphoreType.DMA((ndp,)),
            pltpu.SemaphoreType.DMA((ndp,)),
        ],
        compiler_params=pltpu.CompilerParams(collective_id=0, has_side_effects=True, vmem_limit_bytes=32 * 1024 * 1024),
        name="hyena",
    )(*[pltpu.with_memory_space_constraint(a, pltpu.HBM) for a in (inputs, cotangent, residues.T, decay_rates.T, skip_gain.reshape(1, channels), forward, back, trig)])
    outputs, grad_inputs, grad_residues, grad_skip = pl.pallas_call(
        last_kernel,
        out_shape=(
            jax.ShapeDtypeStruct(wide, bf16),
            jax.ShapeDtypeStruct(wide, bf16),
            jax.ShapeDtypeStruct((modes, groups), f32),
            jax.ShapeDtypeStruct((1, channels), f32),
        ),
        in_specs=[vmem] * 5,
        out_specs=(hbm,) * 4,
        scratch_shapes=[
            pltpu.VMEM((modes, groups), f32),
            pltpu.VMEM((1, channels), f32),
            pltpu.SemaphoreType.DMA((4,)),
        ],
        compiler_params=pltpu.CompilerParams(vmem_limit_bytes=32 * 1024 * 1024),
        name="last",
    )(*parts)
    return outputs, grad_inputs, grad_residues.T, grad_skip.reshape(channels)


def solution(mesh):
    placed = (P("dp", "ctx", "tp"), P("dp", "ctx", "tp"), P("tp", None), P("tp", None), P("tp"))
    return jax.shard_map(
        functools.partial(shards, mesh.shape["ctx"], mesh.shape["dp"]),
        mesh=mesh,
        in_specs=placed,
        out_specs=(P("dp", "ctx", "tp"), P("dp", "ctx", "tp"), P("tp", None), P("tp")),
        check_vma=False,
    )
```

```python
import functools
import math

import jax
import jax.numpy as jnp
import numpy as np
from jax import lax
from jax.experimental import pallas as pl
from jax.experimental.pallas import tpu as pltpu
from jax.sharding import PartitionSpec as P

MESH = pl.DeviceIdType.MESH
highest = lax.Precision.HIGHEST
f32 = jnp.float32
bf16 = jnp.bfloat16
COMM = True
UNROLL = True


def split(value):
    high = value.astype(bf16)
    return high, (value - high.astype(f32)).astype(bf16)


def times(left, right):
    total = jnp.dot(left[0], right[0], preferred_element_type=f32)
    total += jnp.dot(left[0], right[1], preferred_element_type=f32)
    return total + jnp.dot(left[1], right[0], preferred_element_type=f32)


def times_row(left, right):
    return jnp.dot(left, right, precision=highest, preferred_element_type=f32)


def split_store(target, piece, value):
    high, low = split(value)
    target[0, :, piece] = high
    target[1, :, piece] = low


def same_block(shape):
    return lax.broadcasted_iota(jnp.int32, shape, 0) // 16 == lax.broadcasted_iota(jnp.int32, shape, 1) // 16


def on_blocks(piece):
    return jnp.where(same_block((256, 256)), jnp.concatenate([piece] * 16, axis=0), 0.0)


def off_blocks(array):
    return jnp.sum(jnp.where(same_block((256, 256)), array, 0.0).reshape(16, 16, 256), axis=0)


def kernel(sizes, x_hbm, d_hbm, res_hbm, rate_hbm, skip_hbm, fwd_hbm, inv_hbm, trig_hbm,
           y_ref, z_ref, final_ref, weight_ref, chosen_ref,
           x_ref, d_ref, res_ref, rate_ref, skip_ref, fwd_ref, inv_ref, trig_ref,
           wf_ref, wb_ref, h_ref, x_hat, d_hat, ylocal, zlocal, rate_row, states, coefs, carried_ref, packs,
           out_send, out_recv, back_send, back_recv, p_send, from_dp, o_send, o_recv,
           load_sem, send_sem, recv_sem, psend_sem, precv_sem):
    nctx, ndp, rows, channels, groups, modes, scale = sizes
    half = rows // 2
    tiles = channels // 256
    me = lax.axis_index("ctx")
    mine = lax.axis_index("dp")

    barrier = pltpu.get_barrier_semaphore()

    def far_first(count):
        return nctx // 2 + jnp.where(count % 2 == 1, -((count + 1) // 2), count // 2)

    def greet(count, carried):
        step = far_first(count)
        pl.semaphore_signal(barrier, inc=1, device_id={"ctx": lax.rem(me + step, nctx)}, device_id_type=MESH)
        return carried

    if COMM:
        lax.fori_loop(0, nctx - 1, greet, 0)
        for step in range(1, ndp):
            pl.semaphore_signal(barrier, inc=1, device_id={"dp": lax.rem(mine + step, ndp)}, device_id_type=MESH)

    loads = [
        pltpu.make_async_copy(source, target, load_sem.at[number])
        for number, (source, target) in enumerate(
            [(rate_hbm, rate_ref), (res_hbm, res_ref), (x_hbm.at[0], x_ref), (d_hbm.at[0], d_ref), (trig_hbm, trig_ref),
             (fwd_hbm, fwd_ref), (inv_hbm, inv_ref), (skip_hbm, skip_ref)]
        )
    ]
    for load in loads:
        load.start()

    lanes = lax.broadcasted_iota(jnp.int32, (8, 128), 1)
    lower = lanes < 64
    lower_row = lax.broadcasted_iota(jnp.int32, (1, 128), 1) < 64
    positions = lax.broadcasted_iota(jnp.int32, (rows, 1), 0).astype(f32)
    own_group = (
        lax.broadcasted_iota(jnp.int32, (groups, channels), 1) // modes == lax.broadcasted_iota(jnp.int32, (groups, channels), 0)
    ).astype(f32)
    own_mode = (
        lax.broadcasted_iota(jnp.int32, (modes, channels), 1) % modes == lax.broadcasted_iota(jnp.int32, (modes, channels), 0)
    )

    def by_tiles(body):
        if UNROLL:
            for q in range(tiles):
                body(q, slice(256 * q, 256 * q + 256))
        else:
            def turn(q, carried):
                body(q, pl.ds(pl.multiple_of(q * 256, 256), 256))
                return carried

            lax.fori_loop(0, tiles, turn, 0)

    def pack(array, target, top):
        for pair in range(nctx // 2):
            low = array[0:8, 128 * pair : 128 * pair + 128]
            high = array[8:16, 128 * pair : 128 * pair + 128]
            target[2 * pair, top : top + 8] = jnp.where(lower, low, pltpu.roll(high, 64, 1))
            target[2 * pair + 1, top : top + 8] = jnp.where(lower, pltpu.roll(low, 64, 1), high)

    def unpack(source, top):
        lows, highs = [], []
        for pair in range(nctx // 2):
            first, second = source[2 * pair, top : top + 8], source[2 * pair + 1, top : top + 8]
            lows.append(jnp.where(lower, first, pltpu.roll(second, 64, 1)))
            highs.append(jnp.where(lower, pltpu.roll(first, 64, 1), second))
        return jnp.concatenate([jnp.concatenate(lows, axis=1), jnp.concatenate(highs, axis=1)], axis=0)

    def transposed_dot(left, right):
        return lax.dot_general(left, right, (((0,), (0,)), ((), ())), preferred_element_type=f32)

    loads[0].wait()
    rate_wide = times_row(rate_ref[...], own_group)
    rate_row[...] = jnp.sum(jnp.where(own_mode, rate_wide, 0.0), axis=0, keepdims=True)

    def end_states(q, piece):
        split_store(wb_ref, piece, jnp.exp(-rate_row[:, piece] * (rows - 1.0 - positions)))
        full = transposed_dot(wb_ref[0, :, piece], x_ref[:, piece]) + transposed_dot(wb_ref[1, :, piece], x_ref[:, piece])
        states[0, :, piece] = off_blocks(full)

    def start_states(q, piece):
        split_store(wf_ref, piece, jnp.exp(-rate_row[:, piece] * positions))
        full = transposed_dot(wf_ref[0, :, piece], d_ref[:, piece]) + transposed_dot(wf_ref[1, :, piece], d_ref[:, piece])
        states[1, :, piece] = off_blocks(full)

    loads[2].wait()
    by_tiles(end_states)
    pack(states[0], out_send, 0)
    loads[3].wait()
    by_tiles(start_states)
    pack(states[1], out_send, 8)

    def state_copy(there, kind, send, recv, slot_there):
        return pltpu.make_async_remote_copy(
            src_ref=send.at[there] if kind < 2 else send,
            dst_ref=recv.at[slot_there],
            send_sem=send_sem.at[kind, there],
            recv_sem=recv_sem.at[kind, slot_there],
            device_id={"ctx": there},
            device_id_type=MESH,
        )

    def over_peers(body):
        def turn(step, carried):
            body(lax.rem(me + step, nctx))
            return carried

        if COMM:
            lax.fori_loop(1, nctx, turn, 0)

    def send_all(kind, send, recv):
        def turn(count, carried):
            state_copy(lax.rem(me + far_first(count), nctx), kind, send, recv, me).start()
            return carried

        if COMM:
            lax.fori_loop(0, nctx - 1, turn, 0)

    def await_all(kind, send, recv):
        over_peers(lambda origin: state_copy(origin, kind, send, recv, origin).wait_recv())

    def await_sent(kind, send, recv):
        over_peers(lambda origin: state_copy(origin, kind, send, recv, origin).wait_send())

    for load in loads[4:]:
        load.wait()

    def spectra(q, piece):
        step_piece = jnp.exp(-rate_row[:, piece])
        less_cos, sine = trig_ref[:, 0:1], trig_ref[:, 1:2]
        rest = 1.0 - step_piece
        near = step_piece * less_cos
        below = 1.0 / (rest * rest + 2.0 * near)
        h_ref[0:half, piece] = (rest + near) * below
        h_ref[half:rows, piece] = (-step_piece * sine) * below
        x_piece, d_piece = x_ref[:, piece], d_ref[:, piece]
        x_new = jnp.dot(fwd_ref[0], x_piece, preferred_element_type=f32) + jnp.dot(fwd_ref[1], x_piece, preferred_element_type=f32)
        d_new = jnp.dot(fwd_ref[0], d_piece, preferred_element_type=f32) + jnp.dot(fwd_ref[1], d_piece, preferred_element_type=f32)
        x_hat[:, piece] = x_new
        d_hat[:, piece] = d_new
        x_re, x_im, d_re, d_im = x_new[0:half], x_new[half:rows], d_new[0:half], d_new[half:rows]
        cross = jnp.concatenate([d_re * x_re + d_im * x_im, d_im * x_re - d_re * x_im], axis=0)
        cross_high, cross_low = split(cross)
        ones = same_block((256, 256)).astype(bf16)
        grouped = jnp.dot(cross_high, ones, preferred_element_type=f32) + jnp.dot(cross_low, ones, preferred_element_type=f32)
        grad_piece = jnp.sum(grouped * h_ref[:, piece], axis=0, keepdims=True) * (2.0 / rows)
        skip_piece = jnp.sum(x_piece.astype(f32) * d_piece.astype(f32), axis=0, keepdims=True)
        for part in range(2):
            pair = 2 * q + part
            grad_row, skip_row = grad_piece[:, 128 * part : 128 * part + 128], skip_piece[:, 128 * part : 128 * part + 128]
            out_send[2 * pair, 16:17] = jnp.where(lower_row, grad_row, pltpu.roll(skip_row, 64, 1))
            out_send[2 * pair + 1, 16:17] = jnp.where(lower_row, pltpu.roll(grad_row, 64, 1), skip_row)

    by_tiles(spectra)

    if COMM:
        pl.semaphore_wait(barrier, nctx - 1 + ndp - 1)
    second = lax.rem(lax.axis_index("tp"), 2) == 1

    @pl.when(jnp.logical_not(second))
    def _():
        send_all(0, out_send, out_recv)

    out_recv[me] = out_send[me]

    loads[1].wait()
    coefs[0] = times_row(res_ref[...], own_group) * jnp.sqrt(1.0 - jnp.exp(-2.0 * rate_wide))
    step_wide = jnp.exp(-rate_wide)
    block_wide = jnp.exp(-rate_wide * float(rows))
    inverse_wide = 1.0 / (1.0 + block_wide)
    coefs[1] = coefs[0] * step_wide
    coefs[2] = inverse_wide
    pack(block_wide, packs.at[0], 0)
    pack(inverse_wide, packs.at[1], 0)
    pack(step_wide, packs.at[2], 0)

    weight_ref[...] = jnp.sqrt(1.0 - jnp.exp(-2.0 * rate_ref[...]))
    chosen_ref[...] = (
        lax.broadcasted_iota(jnp.int32, (channels, groups), 0) // modes == lax.broadcasted_iota(jnp.int32, (channels, groups), 1)
    ).astype(bf16)

    def own_part(q, piece):
        response = times(split(h_ref[:, piece]), split(on_blocks(coefs[0, :, piece])))
        f_re, f_im = response[0:half], response[half:rows]
        x_re, x_im, d_re, d_im = x_hat[0:half, piece], x_hat[half:rows, piece], d_hat[0:half, piece], d_hat[half:rows, piece]
        skip = skip_ref[:, piece]
        y_hat = jnp.concatenate([f_re * x_re - f_im * x_im, f_re * x_im + f_im * x_re], axis=0)
        ylocal[:, piece] = times((inv_ref[0], inv_ref[1]), split(y_hat)) + skip * x_ref[:, piece].astype(f32)
        z_hat = jnp.concatenate([f_re * d_re + f_im * d_im, f_re * d_im - f_im * d_re], axis=0)
        zlocal[:, piece] = times((inv_ref[0], inv_ref[1]), split(z_hat)) + skip * d_ref[:, piece].astype(f32)

    by_tiles(own_part)

    @pl.when(second)
    def _():
        send_all(0, out_send, out_recv)


    block_own, inverse_own, step_own = packs[0, me], packs[1, me], packs[2, me]
    lane_row = lax.broadcasted_iota(jnp.int32, (128, 128), 0)
    lane_column = lax.broadcasted_iota(jnp.int32, (128, 128), 1)
    chosen = (
        (lane_row // 64 == (lane_column % 16) // 8) & ((lane_row % 64) // 16 == lane_column // 16)
    ).astype(bf16)
    right_row = lax.broadcasted_iota(jnp.int32, (8, 128), 0) == lanes % 8
    await_all(0, out_send, out_recv)
    running = jnp.zeros((8, 128), f32)
    inner = []
    for block in range(nctx):
        end = out_recv[block, 0:8]
        back_send[block, 0:8] = running
        inner.append(running + end * inverse_own)
        running = running * block_own + end
    running = jnp.zeros((8, 128), f32)
    owned = jnp.zeros((8, 128), f32)
    gradient = jnp.zeros((1, 128), f32)
    for block in range(nctx - 1, -1, -1):
        start = out_recv[block, 8:16]
        back_send[block, 8:16] = running
        running = running * block_own + start
        owned += start * inner[block]
        gradient += out_recv[block, 16:17]
    high, low = split(owned * step_own)
    summed = jnp.dot(high, chosen, preferred_element_type=f32) + jnp.dot(low, chosen, preferred_element_type=f32)
    gradient += jnp.sum(jnp.where(right_row & lower, summed, 0.0), axis=0, keepdims=True)
    p_send[...] = gradient

    def dp_copy(step, here):
        there = lax.rem(mine + step, ndp)
        slot = there if here else mine
        return pltpu.make_async_remote_copy(
            src_ref=p_send,
            dst_ref=from_dp.at[slot],
            send_sem=psend_sem.at[there],
            recv_sem=precv_sem.at[slot],
            device_id={"dp": there},
            device_id_type=MESH,
        )

    if COMM:
        for step in range(1, ndp):
            dp_copy(step, False).start()
    send_all(1, back_send, back_recv)
    back_recv[me] = back_send[me]
    from_dp[mine] = gradient
    if COMM:
        for step in range(1, ndp):
            dp_copy(step, True).wait_recv()
    gradient = from_dp[0]
    for other in range(1, ndp):
        gradient += from_dp[other]
    o_send[...] = gradient * scale
    send_all(2, o_send, o_recv)
    o_recv[me] = gradient * scale

    await_all(1, back_send, back_recv)
    carried_ref[0] = (unpack(back_recv, 0) + states[0] * coefs[2]) * coefs[1]
    carried_ref[1] = (unpack(back_recv, 8) + states[1] * coefs[2]) * coefs[1]

    def finish(q, piece):
        product = times((wf_ref[0, :, piece], wf_ref[1, :, piece]), split(on_blocks(carried_ref[0, :, piece])))
        y_ref[:, piece] = (ylocal[:, piece] + product).astype(bf16)
        product = times((wb_ref[0, :, piece], wb_ref[1, :, piece]), split(on_blocks(carried_ref[1, :, piece])))
        z_ref[:, piece] = (zlocal[:, piece] + product).astype(bf16)

    by_tiles(finish)
    for sent in ((0, out_send, out_recv), (1, back_send, back_recv), (2, o_send, o_recv)):
        await_sent(*sent)
    if COMM:
        for step in range(1, ndp):
            dp_copy(step, True).wait_send()
    await_all(2, o_send, o_recv)
    final_ref[...] = o_recv[...]


def last_kernel(y_in, z_in, final_ref, weight_ref, chosen_ref, y_hbm, z_hbm, gres_hbm, gskip_hbm, gres_ref, gskip_ref, sem):
    channels = y_in.shape[1]
    modes = weight_ref.shape[0]
    copies = []

    def send(source, target):
        copies.append(pltpu.make_async_copy(source, target, sem.at[len(copies)]))
        copies[-1].start()

    send(y_in, y_hbm.at[0])
    send(z_in, z_hbm.at[0])
    lower_row = lax.broadcasted_iota(jnp.int32, (1, 128), 1) < 64
    final = []
    for pair in range(channels // 128):
        first, second = final_ref[2 * pair], final_ref[2 * pair + 1]
        gskip_ref[:, 128 * pair : 128 * pair + 128] = jnp.where(lower_row, pltpu.roll(first, 64, 1), second)
        final.append(jnp.where(lower_row, first, pltpu.roll(second, 64, 1)))
    send(gskip_ref, gskip_hbm)
    own_mode = (
        lax.broadcasted_iota(jnp.int32, (modes, channels), 1) % modes == lax.broadcasted_iota(jnp.int32, (modes, channels), 0)
    )
    high, low = split(jnp.where(own_mode, jnp.concatenate(final, axis=1), 0.0))
    chosen = chosen_ref[...]
    by_group = jnp.dot(high, chosen, preferred_element_type=f32) + jnp.dot(low, chosen, preferred_element_type=f32)
    gres_ref[...] = by_group * weight_ref[...]
    send(gres_ref, gres_hbm)
    for copy in copies:
        copy.wait()


def transform(rows):
    frequency = np.pi * (2 * np.arange(rows // 2) + 1) / rows
    angle = frequency[:, None] * np.arange(rows)[None, :]
    forward = np.concatenate([np.cos(angle), -np.sin(angle)], axis=0)
    high = forward.astype(jnp.bfloat16)
    low = (forward - high.astype(np.float64)).astype(jnp.bfloat16)
    both = np.stack([high, low])
    back = (both.transpose(0, 2, 1).astype(np.float32) * (2.0 / rows)).astype(jnp.bfloat16)
    trig = np.zeros((rows // 2, 128), np.float32)
    trig[:, 0] = 2.0 * np.sin(frequency / 2.0) ** 2
    trig[:, 1] = np.sin(frequency)
    return jnp.asarray(both), jnp.asarray(back), jnp.asarray(trig)


def shards(nctx, ndp, inputs, cotangent, residues, decay_rates, skip_gain):
    _, rows, channels = inputs.shape
    groups, modes = residues.shape
    sizes = (nctx, ndp, rows, channels, groups, modes, 1.0 / math.sqrt(rows * nctx * ndp))
    forward, back, trig = transform(rows)
    hbm = pl.BlockSpec(memory_space=pltpu.HBM)
    vmem = pl.BlockSpec(memory_space=pltpu.VMEM)
    wide = (1, rows, channels)
    parts = pl.pallas_call(
        functools.partial(kernel, sizes),
        out_shape=(
            jax.ShapeDtypeStruct((rows, channels), bf16),
            jax.ShapeDtypeStruct((rows, channels), bf16),
            jax.ShapeDtypeStruct((nctx, 1, 128), f32),
            jax.ShapeDtypeStruct((modes, groups), f32),
            jax.ShapeDtypeStruct((channels, groups), bf16),
        ),
        in_specs=[hbm] * 8,
        out_specs=(vmem,) * 5,
        scratch_shapes=[
            pltpu.VMEM((rows, channels), bf16),
            pltpu.VMEM((rows, channels), bf16),
            pltpu.VMEM((modes, groups), f32),
            pltpu.VMEM((modes, groups), f32),
            pltpu.VMEM((1, channels), f32),
            pltpu.VMEM((2, rows, rows), bf16),
            pltpu.VMEM((2, rows, rows), bf16),
            pltpu.VMEM((rows // 2, 128), f32),
            pltpu.VMEM((2, rows, channels), bf16),
            pltpu.VMEM((2, rows, channels), bf16),
            pltpu.VMEM((rows, channels), f32),
            pltpu.VMEM((rows, channels), f32),
            pltpu.VMEM((rows, channels), f32),
            pltpu.VMEM((rows, channels), f32),
            pltpu.VMEM((rows, channels), f32),
            pltpu.VMEM((1, channels), f32),
            pltpu.VMEM((2, modes, channels), f32),
            pltpu.VMEM((3, modes, channels), f32),
            pltpu.VMEM((2, modes, channels), f32),
            pltpu.VMEM((3, nctx, 8, 128), f32),
            pltpu.VMEM((nctx, 17, 128), f32),
            pltpu.VMEM((nctx, 17, 128), f32),
            pltpu.VMEM((nctx, 16, 128), f32),
            pltpu.VMEM((nctx, 16, 128), f32),
            pltpu.VMEM((1, 128), f32),
            pltpu.VMEM((ndp, 1, 128), f32),
            pltpu.VMEM((1, 128), f32),
            pltpu.VMEM((nctx, 1, 128), f32),
            pltpu.SemaphoreType.DMA((8,)),
            pltpu.SemaphoreType.DMA((3, nctx)),
            pltpu.SemaphoreType.DMA((3, nctx)),
            pltpu.SemaphoreType.DMA((ndp,)),
            pltpu.SemaphoreType.DMA((ndp,)),
        ],
        compiler_params=pltpu.CompilerParams(collective_id=0, has_side_effects=True, vmem_limit_bytes=32 * 1024 * 1024),
        name="hyena",
    )(*[pltpu.with_memory_space_constraint(a, pltpu.HBM) for a in (inputs, cotangent, residues.T, decay_rates.T, skip_gain.reshape(1, channels), forward, back, trig)])
    outputs, grad_inputs, grad_residues, grad_skip = pl.pallas_call(
        last_kernel,
        out_shape=(
            jax.ShapeDtypeStruct(wide, bf16),
            jax.ShapeDtypeStruct(wide, bf16),
            jax.ShapeDtypeStruct((modes, groups), f32),
            jax.ShapeDtypeStruct((1, channels), f32),
        ),
        in_specs=[vmem] * 5,
        out_specs=(hbm,) * 4,
        scratch_shapes=[
            pltpu.VMEM((modes, groups), f32),
            pltpu.VMEM((1, channels), f32),
            pltpu.SemaphoreType.DMA((4,)),
        ],
        compiler_params=pltpu.CompilerParams(vmem_limit_bytes=32 * 1024 * 1024),
        name="last",
    )(*parts)
    return outputs, grad_inputs, grad_residues.T, grad_skip.reshape(channels)


def solution(mesh):
    placed = (P("dp", "ctx", "tp"), P("dp", "ctx", "tp"), P("tp", None), P("tp", None), P("tp"))
    return jax.shard_map(
        functools.partial(shards, mesh.shape["ctx"], mesh.shape["dp"]),
        mesh=mesh,
        in_specs=placed,
        out_specs=(P("dp", "ctx", "tp"), P("dp", "ctx", "tp"), P("tp", None), P("tp")),
        check_vma=False,
    )
```

```python
import functools
import math

import jax
import jax.numpy as jnp
import numpy as np
from jax import lax
from jax.experimental import pallas as pl
from jax.experimental.pallas import tpu as pltpu
from jax.sharding import PartitionSpec as P

MESH = pl.DeviceIdType.MESH
highest = lax.Precision.HIGHEST
f32 = jnp.float32
bf16 = jnp.bfloat16
COMM = True
UNROLL = True


def split(value):
    high = value.astype(bf16)
    return high, (value - high.astype(f32)).astype(bf16)


def times(left, right):
    total = jnp.dot(left[0], right[0], preferred_element_type=f32)
    total += jnp.dot(left[0], right[1], preferred_element_type=f32)
    return total + jnp.dot(left[1], right[0], preferred_element_type=f32)


def times_row(left, right):
    return jnp.dot(left, right, precision=highest, preferred_element_type=f32)


def split_store(target, piece, value):
    high, low = split(value)
    target[0, :, piece] = high
    target[1, :, piece] = low


def same_block(shape):
    return lax.broadcasted_iota(jnp.int32, shape, 0) // 16 == lax.broadcasted_iota(jnp.int32, shape, 1) // 16


def on_blocks(piece):
    return jnp.where(same_block((256, 256)), jnp.concatenate([piece] * 16, axis=0), 0.0)


def off_blocks(array):
    return jnp.sum(jnp.where(same_block((256, 256)), array, 0.0).reshape(16, 16, 256), axis=0)


def kernel(sizes, x_hbm, d_hbm, res_hbm, rate_hbm, skip_hbm, fwd_hbm, inv_hbm, trig_hbm,
           y_ref, z_ref, final_ref, weight_ref, chosen_ref,
           x_ref, d_ref, res_ref, rate_ref, skip_ref, fwd_ref, inv_ref, trig_ref,
           wf_ref, wb_ref, h_ref, x_hat, d_hat, ylocal, zlocal, rate_row, states, coefs, carried_ref, packs,
           out_send, out_recv, back_send, back_recv, o_send, o_recv,
           load_sem, send_sem, recv_sem, osend_sem, orecv_sem, ring_sem):
    nctx, ndp, rows, channels, groups, modes, scale = sizes
    half = rows // 2
    tiles = channels // 256
    me = lax.axis_index("ctx")
    mine = lax.axis_index("dp")

    barrier = pltpu.get_barrier_semaphore()

    def far_first(count):
        return nctx // 2 + jnp.where(count % 2 == 1, -((count + 1) // 2), count // 2)

    def greet(count, carried):
        step = far_first(count)
        pl.semaphore_signal(barrier, inc=1, device_id={"ctx": lax.rem(me + step, nctx)}, device_id_type=MESH)
        return carried

    if COMM:
        lax.fori_loop(0, nctx - 1, greet, 0)
        for step in range(1, ndp):
            pl.semaphore_signal(barrier, inc=1, device_id={"dp": lax.rem(mine + step, ndp)}, device_id_type=MESH)

    loads = [
        pltpu.make_async_copy(source, target, load_sem.at[number])
        for number, (source, target) in enumerate(
            [(rate_hbm, rate_ref), (res_hbm, res_ref), (x_hbm.at[0], x_ref), (d_hbm.at[0], d_ref), (trig_hbm, trig_ref),
             (fwd_hbm, fwd_ref), (inv_hbm, inv_ref), (skip_hbm, skip_ref)]
        )
    ]
    for load in loads:
        load.start()

    lanes = lax.broadcasted_iota(jnp.int32, (8, 128), 1)
    lower = lanes < 64
    lower_row = lax.broadcasted_iota(jnp.int32, (1, 128), 1) < 64
    positions = lax.broadcasted_iota(jnp.int32, (rows, 1), 0).astype(f32)
    own_group = (
        lax.broadcasted_iota(jnp.int32, (groups, channels), 1) // modes == lax.broadcasted_iota(jnp.int32, (groups, channels), 0)
    ).astype(f32)
    own_mode = (
        lax.broadcasted_iota(jnp.int32, (modes, channels), 1) % modes == lax.broadcasted_iota(jnp.int32, (modes, channels), 0)
    )

    def by_tiles(body):
        if UNROLL:
            for q in range(tiles):
                body(q, slice(256 * q, 256 * q + 256))
        else:
            def turn(q, carried):
                body(q, pl.ds(pl.multiple_of(q * 256, 256), 256))
                return carried

            lax.fori_loop(0, tiles, turn, 0)

    def pack(array, target, top):
        for pair in range(nctx // 2):
            low = array[0:8, 128 * pair : 128 * pair + 128]
            high = array[8:16, 128 * pair : 128 * pair + 128]
            target[2 * pair, top : top + 8] = jnp.where(lower, low, pltpu.roll(high, 64, 1))
            target[2 * pair + 1, top : top + 8] = jnp.where(lower, pltpu.roll(low, 64, 1), high)

    def unpack(source, top):
        lows, highs = [], []
        for pair in range(nctx // 2):
            first, second = source[2 * pair, top : top + 8], source[2 * pair + 1, top : top + 8]
            lows.append(jnp.where(lower, first, pltpu.roll(second, 64, 1)))
            highs.append(jnp.where(lower, pltpu.roll(first, 64, 1), second))
        return jnp.concatenate([jnp.concatenate(lows, axis=1), jnp.concatenate(highs, axis=1)], axis=0)

    def transposed_dot(left, right):
        return lax.dot_general(left, right, (((0,), (0,)), ((), ())), preferred_element_type=f32)

    loads[0].wait()
    rate_wide = times_row(rate_ref[...], own_group)
    rate_row[...] = jnp.sum(jnp.where(own_mode, rate_wide, 0.0), axis=0, keepdims=True)

    def end_states(q, piece):
        split_store(wb_ref, piece, jnp.exp(-rate_row[:, piece] * (rows - 1.0 - positions)))
        full = transposed_dot(wb_ref[0, :, piece], x_ref[:, piece]) + transposed_dot(wb_ref[1, :, piece], x_ref[:, piece])
        states[0, :, piece] = off_blocks(full)

    def start_states(q, piece):
        split_store(wf_ref, piece, jnp.exp(-rate_row[:, piece] * positions))
        full = transposed_dot(wf_ref[0, :, piece], d_ref[:, piece]) + transposed_dot(wf_ref[1, :, piece], d_ref[:, piece])
        states[1, :, piece] = off_blocks(full)

    loads[2].wait()
    by_tiles(end_states)
    pack(states[0], out_send, 0)
    loads[3].wait()
    by_tiles(start_states)
    pack(states[1], out_send, 8)

    def state_copy(there, kind, send, recv, slot_there):
        return pltpu.make_async_remote_copy(
            src_ref=send.at[there],
            dst_ref=recv.at[slot_there],
            send_sem=send_sem.at[kind, there],
            recv_sem=recv_sem.at[kind, slot_there],
            device_id={"ctx": there},
            device_id_type=MESH,
        )

    def over_peers(body):
        def turn(count, carried):
            body(lax.rem(me + far_first(nctx - 2 - count), nctx))
            return carried

        if COMM:
            lax.fori_loop(0, nctx - 1, turn, 0)

    def send_all(kind, send, recv):
        def turn(count, carried):
            state_copy(lax.rem(me + far_first(count), nctx), kind, send, recv, me).start()
            return carried

        if COMM:
            lax.fori_loop(0, nctx - 1, turn, 0)

    def await_all(kind, send, recv):
        over_peers(lambda origin: state_copy(origin, kind, send, recv, origin).wait_recv())

    def await_sent(kind, send, recv):
        over_peers(lambda origin: state_copy(origin, kind, send, recv, origin).wait_send())

    for load in loads[4:]:
        load.wait()

    def spectra(q, piece):
        step_piece = jnp.exp(-rate_row[:, piece])
        less_cos, sine = trig_ref[:, 0:1], trig_ref[:, 1:2]
        rest = 1.0 - step_piece
        near = step_piece * less_cos
        below = 1.0 / (rest * rest + 2.0 * near)
        h_ref[0:half, piece] = (rest + near) * below
        h_ref[half:rows, piece] = (-step_piece * sine) * below
        x_piece, d_piece = x_ref[:, piece], d_ref[:, piece]
        x_new = jnp.dot(fwd_ref[0], x_piece, preferred_element_type=f32) + jnp.dot(fwd_ref[1], x_piece, preferred_element_type=f32)
        d_new = jnp.dot(fwd_ref[0], d_piece, preferred_element_type=f32) + jnp.dot(fwd_ref[1], d_piece, preferred_element_type=f32)
        x_hat[:, piece] = x_new
        d_hat[:, piece] = d_new
        x_re, x_im, d_re, d_im = x_new[0:half], x_new[half:rows], d_new[0:half], d_new[half:rows]
        cross = jnp.concatenate([d_re * x_re + d_im * x_im, d_im * x_re - d_re * x_im], axis=0)
        cross_high, cross_low = split(cross)
        ones = same_block((256, 256)).astype(bf16)
        grouped = jnp.dot(cross_high, ones, preferred_element_type=f32) + jnp.dot(cross_low, ones, preferred_element_type=f32)
        grad_piece = jnp.sum(grouped * h_ref[:, piece], axis=0, keepdims=True) * (2.0 / rows)
        skip_piece = jnp.sum(x_piece.astype(f32) * d_piece.astype(f32), axis=0, keepdims=True)
        for part in range(2):
            pair = 2 * q + part
            grad_row, skip_row = grad_piece[:, 128 * part : 128 * part + 128], skip_piece[:, 128 * part : 128 * part + 128]
            out_send[2 * pair, 16:17] = jnp.where(lower_row, grad_row, pltpu.roll(skip_row, 64, 1))
            out_send[2 * pair + 1, 16:17] = jnp.where(lower_row, pltpu.roll(grad_row, 64, 1), skip_row)

    by_tiles(spectra)

    if COMM:
        pl.semaphore_wait(barrier, nctx - 1 + ndp - 1)
        for step in range(1, ndp):
            pl.semaphore_signal(ring_sem, inc=1, device_id={"dp": lax.rem(mine + step, ndp)}, device_id_type=MESH)
    send_all(0, out_send, out_recv)
    out_recv[me] = out_send[me]

    loads[1].wait()
    coefs[0] = times_row(res_ref[...], own_group) * jnp.sqrt(1.0 - jnp.exp(-2.0 * rate_wide))
    step_wide = jnp.exp(-rate_wide)
    block_wide = jnp.exp(-rate_wide * float(rows))
    inverse_wide = 1.0 / (1.0 + block_wide)
    coefs[1] = coefs[0] * step_wide
    coefs[2] = inverse_wide
    pack(block_wide, packs.at[0], 0)
    pack(inverse_wide, packs.at[1], 0)
    pack(step_wide, packs.at[2], 0)

    weight_ref[...] = jnp.sqrt(1.0 - jnp.exp(-2.0 * rate_ref[...]))
    chosen_ref[...] = (
        lax.broadcasted_iota(jnp.int32, (channels, groups), 0) // modes == lax.broadcasted_iota(jnp.int32, (channels, groups), 1)
    ).astype(bf16)

    def own_part(q, piece):
        response = times(split(h_ref[:, piece]), split(on_blocks(coefs[0, :, piece])))
        f_re, f_im = response[0:half], response[half:rows]
        x_re, x_im, d_re, d_im = x_hat[0:half, piece], x_hat[half:rows, piece], d_hat[0:half, piece], d_hat[half:rows, piece]
        skip = skip_ref[:, piece]
        y_hat = jnp.concatenate([f_re * x_re - f_im * x_im, f_re * x_im + f_im * x_re], axis=0)
        ylocal[:, piece] = times((inv_ref[0], inv_ref[1]), split(y_hat)) + skip * x_ref[:, piece].astype(f32)
        z_hat = jnp.concatenate([f_re * d_re + f_im * d_im, f_re * d_im - f_im * d_re], axis=0)
        zlocal[:, piece] = times((inv_ref[0], inv_ref[1]), split(z_hat)) + skip * d_ref[:, piece].astype(f32)

    by_tiles(own_part)

    block_own, inverse_own, step_own = packs[0, me], packs[1, me], packs[2, me]
    lane_row = lax.broadcasted_iota(jnp.int32, (128, 128), 0)
    lane_column = lax.broadcasted_iota(jnp.int32, (128, 128), 1)
    chosen = (
        (lane_row // 64 == (lane_column % 16) // 8) & ((lane_row % 64) // 16 == lane_column // 16)
    ).astype(bf16)
    right_row = lax.broadcasted_iota(jnp.int32, (8, 128), 0) == lanes % 8
    await_all(0, out_send, out_recv)
    running = jnp.zeros((8, 128), f32)
    inner = []
    for block in range(nctx):
        end = out_recv[block, 0:8]
        back_send[block, 0:8] = running
        inner.append(running + end * inverse_own)
        running = running * block_own + end
    running = jnp.zeros((8, 128), f32)
    owned = jnp.zeros((8, 128), f32)
    gradient = jnp.zeros((1, 128), f32)
    for block in range(nctx - 1, -1, -1):
        start = out_recv[block, 8:16]
        back_send[block, 8:16] = running
        running = running * block_own + start
        owned += start * inner[block]
        gradient += out_recv[block, 16:17]
    send_all(1, back_send, back_recv)
    back_recv[me] = back_send[me]
    high, low = split(owned * step_own)
    summed = jnp.dot(high, chosen, preferred_element_type=f32) + jnp.dot(low, chosen, preferred_element_type=f32)
    gradient += jnp.sum(jnp.where(right_row & lower, summed, 0.0), axis=0, keepdims=True)
    gradient = gradient * scale
    o_send[...] = gradient
    o_recv[mine * nctx + me] = gradient

    def gradient_copy(offset, step):
        part, there = lax.rem(mine + offset, ndp), lax.rem(me + step, nctx)
        return pltpu.make_async_remote_copy(
            src_ref=o_send,
            dst_ref=o_recv.at[mine * nctx + me],
            send_sem=osend_sem,
            recv_sem=orecv_sem,
            device_id={"dp": part, "ctx": there},
            device_id_type=MESH,
        )

    def send_gradients(count, carried):
        for offset in range(ndp):
            gradient_copy(offset, far_first(count)).start()
        return carried

    if COMM:
        pl.semaphore_wait(ring_sem, ndp - 1)
        lax.fori_loop(0, nctx - 1, send_gradients, 0)
        for offset in range(1, ndp):
            gradient_copy(offset, 0).start()

    await_all(1, back_send, back_recv)
    carried_ref[0] = (unpack(back_recv, 0) + states[0] * coefs[2]) * coefs[1]
    carried_ref[1] = (unpack(back_recv, 8) + states[1] * coefs[2]) * coefs[1]

    def finish(q, piece):
        product = times((wf_ref[0, :, piece], wf_ref[1, :, piece]), split(on_blocks(carried_ref[0, :, piece])))
        y_ref[:, piece] = (ylocal[:, piece] + product).astype(bf16)
        product = times((wb_ref[0, :, piece], wb_ref[1, :, piece]), split(on_blocks(carried_ref[1, :, piece])))
        z_ref[:, piece] = (zlocal[:, piece] + product).astype(bf16)

    by_tiles(finish)
    for sent in ((0, out_send, out_recv), (1, back_send, back_recv)):
        await_sent(*sent)
    if COMM:
        others = o_recv.at[pl.ds(0, ndp * nctx - 1)]
        everything = pltpu.make_async_remote_copy(
            src_ref=others,
            dst_ref=others,
            send_sem=osend_sem,
            recv_sem=orecv_sem,
            device_id={"ctx": lax.rem(me + 1, nctx)},
            device_id_type=MESH,
        )
        everything.wait_send()
        everything.wait_recv()
    for owner in range(nctx):
        total = o_recv[owner]
        for part in range(1, ndp):
            total += o_recv[part * nctx + owner]
        final_ref[owner] = total


def last_kernel(y_in, z_in, final_ref, weight_ref, chosen_ref, y_hbm, z_hbm, gres_hbm, gskip_hbm, gres_ref, gskip_ref, sem):
    channels = y_in.shape[1]
    modes = weight_ref.shape[0]
    copies = []

    def send(source, target):
        copies.append(pltpu.make_async_copy(source, target, sem.at[len(copies)]))
        copies[-1].start()

    send(y_in, y_hbm.at[0])
    send(z_in, z_hbm.at[0])
    lower_row = lax.broadcasted_iota(jnp.int32, (1, 128), 1) < 64
    final = []
    for pair in range(channels // 128):
        first, second = final_ref[2 * pair], final_ref[2 * pair + 1]
        gskip_ref[:, 128 * pair : 128 * pair + 128] = jnp.where(lower_row, pltpu.roll(first, 64, 1), second)
        final.append(jnp.where(lower_row, first, pltpu.roll(second, 64, 1)))
    send(gskip_ref, gskip_hbm)
    own_mode = (
        lax.broadcasted_iota(jnp.int32, (modes, channels), 1) % modes == lax.broadcasted_iota(jnp.int32, (modes, channels), 0)
    )
    high, low = split(jnp.where(own_mode, jnp.concatenate(final, axis=1), 0.0))
    chosen = chosen_ref[...]
    by_group = jnp.dot(high, chosen, preferred_element_type=f32) + jnp.dot(low, chosen, preferred_element_type=f32)
    gres_ref[...] = by_group * weight_ref[...]
    send(gres_ref, gres_hbm)
    for copy in copies:
        copy.wait()


def transform(rows):
    frequency = np.pi * (2 * np.arange(rows // 2) + 1) / rows
    angle = frequency[:, None] * np.arange(rows)[None, :]
    forward = np.concatenate([np.cos(angle), -np.sin(angle)], axis=0)
    high = forward.astype(jnp.bfloat16)
    low = (forward - high.astype(np.float64)).astype(jnp.bfloat16)
    both = np.stack([high, low])
    back = (both.transpose(0, 2, 1).astype(np.float32) * (2.0 / rows)).astype(jnp.bfloat16)
    trig = np.zeros((rows // 2, 128), np.float32)
    trig[:, 0] = 2.0 * np.sin(frequency / 2.0) ** 2
    trig[:, 1] = np.sin(frequency)
    return jnp.asarray(both), jnp.asarray(back), jnp.asarray(trig)


def shards(nctx, ndp, inputs, cotangent, residues, decay_rates, skip_gain):
    _, rows, channels = inputs.shape
    groups, modes = residues.shape
    sizes = (nctx, ndp, rows, channels, groups, modes, 1.0 / math.sqrt(rows * nctx * ndp))
    forward, back, trig = transform(rows)
    hbm = pl.BlockSpec(memory_space=pltpu.HBM)
    vmem = pl.BlockSpec(memory_space=pltpu.VMEM)
    wide = (1, rows, channels)
    parts = pl.pallas_call(
        functools.partial(kernel, sizes),
        out_shape=(
            jax.ShapeDtypeStruct((rows, channels), bf16),
            jax.ShapeDtypeStruct((rows, channels), bf16),
            jax.ShapeDtypeStruct((nctx, 1, 128), f32),
            jax.ShapeDtypeStruct((modes, groups), f32),
            jax.ShapeDtypeStruct((channels, groups), bf16),
        ),
        in_specs=[hbm] * 8,
        out_specs=(vmem,) * 5,
        scratch_shapes=[
            pltpu.VMEM((rows, channels), bf16),
            pltpu.VMEM((rows, channels), bf16),
            pltpu.VMEM((modes, groups), f32),
            pltpu.VMEM((modes, groups), f32),
            pltpu.VMEM((1, channels), f32),
            pltpu.VMEM((2, rows, rows), bf16),
            pltpu.VMEM((2, rows, rows), bf16),
            pltpu.VMEM((rows // 2, 128), f32),
            pltpu.VMEM((2, rows, channels), bf16),
            pltpu.VMEM((2, rows, channels), bf16),
            pltpu.VMEM((rows, channels), f32),
            pltpu.VMEM((rows, channels), f32),
            pltpu.VMEM((rows, channels), f32),
            pltpu.VMEM((rows, channels), f32),
            pltpu.VMEM((rows, channels), f32),
            pltpu.VMEM((1, channels), f32),
            pltpu.VMEM((2, modes, channels), f32),
            pltpu.VMEM((3, modes, channels), f32),
            pltpu.VMEM((2, modes, channels), f32),
            pltpu.VMEM((3, nctx, 8, 128), f32),
            pltpu.VMEM((nctx, 17, 128), f32),
            pltpu.VMEM((nctx, 17, 128), f32),
            pltpu.VMEM((nctx, 16, 128), f32),
            pltpu.VMEM((nctx, 16, 128), f32),
            pltpu.VMEM((1, 128), f32),
            pltpu.VMEM((ndp * nctx, 1, 128), f32),
            pltpu.SemaphoreType.DMA((8,)),
            pltpu.SemaphoreType.DMA((2, nctx)),
            pltpu.SemaphoreType.DMA((2, nctx)),
            pltpu.SemaphoreType.DMA,
            pltpu.SemaphoreType.DMA,
            pltpu.SemaphoreType.REGULAR,
        ],
        compiler_params=pltpu.CompilerParams(collective_id=0, has_side_effects=True, vmem_limit_bytes=32 * 1024 * 1024),
        name="hyena",
    )(*[pltpu.with_memory_space_constraint(a, pltpu.HBM) for a in (inputs, cotangent, residues.T, decay_rates.T, skip_gain.reshape(1, channels), forward, back, trig)])
    outputs, grad_inputs, grad_residues, grad_skip = pl.pallas_call(
        last_kernel,
        out_shape=(
            jax.ShapeDtypeStruct(wide, bf16),
            jax.ShapeDtypeStruct(wide, bf16),
            jax.ShapeDtypeStruct((modes, groups), f32),
            jax.ShapeDtypeStruct((1, channels), f32),
        ),
        in_specs=[vmem] * 5,
        out_specs=(hbm,) * 4,
        scratch_shapes=[
            pltpu.VMEM((modes, groups), f32),
            pltpu.VMEM((1, channels), f32),
            pltpu.SemaphoreType.DMA((4,)),
        ],
        compiler_params=pltpu.CompilerParams(vmem_limit_bytes=32 * 1024 * 1024),
        name="last",
    )(*parts)
    return outputs, grad_inputs, grad_residues.T, grad_skip.reshape(channels)


def solution(mesh):
    placed = (P("dp", "ctx", "tp"), P("dp", "ctx", "tp"), P("tp", None), P("tp", None), P("tp"))
    return jax.shard_map(
        functools.partial(shards, mesh.shape["ctx"], mesh.shape["dp"]),
        mesh=mesh,
        in_specs=placed,
        out_specs=(P("dp", "ctx", "tp"), P("dp", "ctx", "tp"), P("tp", None), P("tp")),
        check_vma=False,
    )
```

```python
import functools
import math

import jax
import jax.numpy as jnp
import numpy as np
from jax import lax
from jax.experimental import pallas as pl
from jax.experimental.pallas import tpu as pltpu
from jax.sharding import PartitionSpec as P

MESH = pl.DeviceIdType.MESH
highest = lax.Precision.HIGHEST
f32 = jnp.float32
bf16 = jnp.bfloat16
COMM = True
UNROLL = True


def split(value):
    high = value.astype(bf16)
    return high, (value - high.astype(f32)).astype(bf16)


def times(left, right):
    total = jnp.dot(left[0], right[0], preferred_element_type=f32)
    total += jnp.dot(left[0], right[1], preferred_element_type=f32)
    return total + jnp.dot(left[1], right[0], preferred_element_type=f32)


def times_row(left, right):
    return jnp.dot(left, right, precision=highest, preferred_element_type=f32)


def split_store(target, piece, value):
    high, low = split(value)
    target[0, :, piece] = high
    target[1, :, piece] = low


def same_block(shape):
    return lax.broadcasted_iota(jnp.int32, shape, 0) // 16 == lax.broadcasted_iota(jnp.int32, shape, 1) // 16


def on_blocks(piece):
    return jnp.where(same_block((256, 256)), jnp.concatenate([piece] * 16, axis=0), 0.0)


def off_blocks(array):
    return jnp.sum(jnp.where(same_block((256, 256)), array, 0.0).reshape(16, 16, 256), axis=0)


def kernel(sizes, x_hbm, d_hbm, res_hbm, rate_hbm, skip_hbm, fwd_hbm, inv_hbm, trig_hbm,
           y_ref, z_ref, final_ref, weight_ref, chosen_ref,
           x_ref, d_ref, res_ref, rate_ref, skip_ref, fwd_ref, inv_ref, trig_ref,
           wf_ref, wb_ref, h_ref, x_hat, d_hat, ylocal, zlocal, rate_row, states, coefs, carried_ref, packs,
           out_send, out_recv, back_send, back_recv, o_send, o_recv,
           load_sem, send_sem, recv_sem, osend_sem, orecv_sem, ring_sem):
    nctx, ndp, rows, channels, groups, modes, scale = sizes
    half = rows // 2
    tiles = channels // 256
    me = lax.axis_index("ctx")
    mine = lax.axis_index("dp")

    barrier = pltpu.get_barrier_semaphore()

    def far_first(count):
        return nctx // 2 + jnp.where(count % 2 == 1, -((count + 1) // 2), count // 2)

    def greet(count, carried):
        step = far_first(count)
        pl.semaphore_signal(barrier, inc=1, device_id={"ctx": lax.rem(me + step, nctx)}, device_id_type=MESH)
        return carried

    if COMM:
        lax.fori_loop(0, nctx - 1, greet, 0)
        for step in range(1, ndp):
            pl.semaphore_signal(barrier, inc=1, device_id={"dp": lax.rem(mine + step, ndp)}, device_id_type=MESH)

    loads = [
        pltpu.make_async_copy(source, target, load_sem.at[number])
        for number, (source, target) in enumerate(
            [(rate_hbm, rate_ref), (res_hbm, res_ref), (x_hbm.at[0], x_ref), (d_hbm.at[0], d_ref), (trig_hbm, trig_ref),
             (fwd_hbm, fwd_ref), (inv_hbm, inv_ref), (skip_hbm, skip_ref)]
        )
    ]
    for load in loads:
        load.start()

    lanes = lax.broadcasted_iota(jnp.int32, (8, 128), 1)
    lower = lanes < 64
    lower_row = lax.broadcasted_iota(jnp.int32, (1, 128), 1) < 64
    positions = lax.broadcasted_iota(jnp.int32, (rows, 1), 0).astype(f32)
    own_group = (
        lax.broadcasted_iota(jnp.int32, (groups, channels), 1) // modes == lax.broadcasted_iota(jnp.int32, (groups, channels), 0)
    ).astype(f32)
    own_mode = (
        lax.broadcasted_iota(jnp.int32, (modes, channels), 1) % modes == lax.broadcasted_iota(jnp.int32, (modes, channels), 0)
    )

    def by_tiles(body):
        if UNROLL:
            for q in range(tiles):
                body(q, slice(256 * q, 256 * q + 256))
        else:
            def turn(q, carried):
                body(q, pl.ds(pl.multiple_of(q * 256, 256), 256))
                return carried

            lax.fori_loop(0, tiles, turn, 0)

    def pack(array, target, top):
        for pair in range(nctx // 2):
            low = array[0:8, 128 * pair : 128 * pair + 128]
            high = array[8:16, 128 * pair : 128 * pair + 128]
            target[2 * pair, top : top + 8] = jnp.where(lower, low, pltpu.roll(high, 64, 1))
            target[2 * pair + 1, top : top + 8] = jnp.where(lower, pltpu.roll(low, 64, 1), high)

    def unpack(source, top):
        lows, highs = [], []
        for pair in range(nctx // 2):
            first, second = source[2 * pair, top : top + 8], source[2 * pair + 1, top : top + 8]
            lows.append(jnp.where(lower, first, pltpu.roll(second, 64, 1)))
            highs.append(jnp.where(lower, pltpu.roll(first, 64, 1), second))
        return jnp.concatenate([jnp.concatenate(lows, axis=1), jnp.concatenate(highs, axis=1)], axis=0)

    def transposed_dot(left, right):
        return lax.dot_general(left, right, (((0,), (0,)), ((), ())), preferred_element_type=f32)

    loads[0].wait()
    rate_wide = times_row(rate_ref[...], own_group)
    rate_row[...] = jnp.sum(jnp.where(own_mode, rate_wide, 0.0), axis=0, keepdims=True)

    def end_states(q, piece):
        split_store(wb_ref, piece, jnp.exp(-rate_row[:, piece] * (rows - 1.0 - positions)))
        full = transposed_dot(wb_ref[0, :, piece], x_ref[:, piece]) + transposed_dot(wb_ref[1, :, piece], x_ref[:, piece])
        states[0, :, piece] = off_blocks(full)

    def start_states(q, piece):
        split_store(wf_ref, piece, jnp.exp(-rate_row[:, piece] * positions))
        full = transposed_dot(wf_ref[0, :, piece], d_ref[:, piece]) + transposed_dot(wf_ref[1, :, piece], d_ref[:, piece])
        states[1, :, piece] = off_blocks(full)

    loads[2].wait()
    by_tiles(end_states)
    pack(states[0], out_send, 0)
    loads[3].wait()
    by_tiles(start_states)
    pack(states[1], out_send, 8)

    def state_copy(there, kind, send, recv, slot_there):
        return pltpu.make_async_remote_copy(
            src_ref=send.at[there],
            dst_ref=recv.at[slot_there],
            send_sem=send_sem.at[kind, there],
            recv_sem=recv_sem.at[kind, slot_there],
            device_id={"ctx": there},
            device_id_type=MESH,
        )

    def over_peers(body):
        def turn(count, carried):
            body(lax.rem(me + far_first(nctx - 2 - count), nctx))
            return carried

        if COMM:
            lax.fori_loop(0, nctx - 1, turn, 0)

    def send_all(kind, send, recv):
        def turn(count, carried):
            state_copy(lax.rem(me + far_first(count), nctx), kind, send, recv, me).start()
            return carried

        if COMM:
            lax.fori_loop(0, nctx - 1, turn, 0)

    def await_all(kind, send, recv):
        over_peers(lambda origin: state_copy(origin, kind, send, recv, origin).wait_recv())

    def await_sent(kind, send, recv):
        over_peers(lambda origin: state_copy(origin, kind, send, recv, origin).wait_send())

    for load in loads[4:]:
        load.wait()

    def spectra(q, piece):
        step_piece = jnp.exp(-rate_row[:, piece])
        less_cos, sine = trig_ref[:, 0:1], trig_ref[:, 1:2]
        rest = 1.0 - step_piece
        near = step_piece * less_cos
        below = 1.0 / (rest * rest + 2.0 * near)
        h_ref[0:half, piece] = (rest + near) * below
        h_ref[half:rows, piece] = (-step_piece * sine) * below
        x_piece, d_piece = x_ref[:, piece], d_ref[:, piece]
        x_new = jnp.dot(fwd_ref[0], x_piece, preferred_element_type=f32) + jnp.dot(fwd_ref[1], x_piece, preferred_element_type=f32)
        d_new = jnp.dot(fwd_ref[0], d_piece, preferred_element_type=f32) + jnp.dot(fwd_ref[1], d_piece, preferred_element_type=f32)
        x_hat[:, piece] = x_new
        d_hat[:, piece] = d_new
        x_re, x_im, d_re, d_im = x_new[0:half], x_new[half:rows], d_new[0:half], d_new[half:rows]
        cross = jnp.concatenate([d_re * x_re + d_im * x_im, d_im * x_re - d_re * x_im], axis=0)
        cross_high, cross_low = split(cross)
        ones = same_block((256, 256)).astype(bf16)
        grouped = jnp.dot(cross_high, ones, preferred_element_type=f32) + jnp.dot(cross_low, ones, preferred_element_type=f32)
        grad_piece = jnp.sum(grouped * h_ref[:, piece], axis=0, keepdims=True) * (2.0 / rows)
        skip_piece = jnp.sum(x_piece.astype(f32) * d_piece.astype(f32), axis=0, keepdims=True)
        for part in range(2):
            pair = 2 * q + part
            grad_row, skip_row = grad_piece[:, 128 * part : 128 * part + 128], skip_piece[:, 128 * part : 128 * part + 128]
            out_send[2 * pair, 16:17] = jnp.where(lower_row, grad_row, pltpu.roll(skip_row, 64, 1))
            out_send[2 * pair + 1, 16:17] = jnp.where(lower_row, pltpu.roll(grad_row, 64, 1), skip_row)

    by_tiles(spectra)

    if COMM:
        pl.semaphore_wait(barrier, nctx - 1 + ndp - 1)
        for step in range(1, ndp):
            pl.semaphore_signal(ring_sem, inc=1, device_id={"dp": lax.rem(mine + step, ndp)}, device_id_type=MESH)
    send_all(0, out_send, out_recv)
    out_recv[me] = out_send[me]

    loads[1].wait()
    coefs[0] = times_row(res_ref[...], own_group) * jnp.sqrt(1.0 - jnp.exp(-2.0 * rate_wide))
    step_wide = jnp.exp(-rate_wide)
    block_wide = jnp.exp(-rate_wide * float(rows))
    inverse_wide = 1.0 / (1.0 + block_wide)
    coefs[1] = coefs[0] * step_wide
    coefs[2] = inverse_wide
    pack(block_wide, packs.at[0], 0)
    pack(inverse_wide, packs.at[1], 0)
    pack(step_wide, packs.at[2], 0)

    weight_ref[...] = jnp.sqrt(1.0 - jnp.exp(-2.0 * rate_ref[...]))
    chosen_ref[...] = (
        lax.broadcasted_iota(jnp.int32, (channels, groups), 0) // modes == lax.broadcasted_iota(jnp.int32, (channels, groups), 1)
    ).astype(bf16)

    def own_part(q, piece):
        response = times(split(h_ref[:, piece]), split(on_blocks(coefs[0, :, piece])))
        f_re, f_im = response[0:half], response[half:rows]
        x_re, x_im, d_re, d_im = x_hat[0:half, piece], x_hat[half:rows, piece], d_hat[0:half, piece], d_hat[half:rows, piece]
        skip = skip_ref[:, piece]
        y_hat = jnp.concatenate([f_re * x_re - f_im * x_im, f_re * x_im + f_im * x_re], axis=0)
        ylocal[:, piece] = times((inv_ref[0], inv_ref[1]), split(y_hat)) + skip * x_ref[:, piece].astype(f32)
        z_hat = jnp.concatenate([f_re * d_re + f_im * d_im, f_re * d_im - f_im * d_re], axis=0)
        zlocal[:, piece] = times((inv_ref[0], inv_ref[1]), split(z_hat)) + skip * d_ref[:, piece].astype(f32)

    by_tiles(own_part)

    block_own, inverse_own, step_own = packs[0, me], packs[1, me], packs[2, me]
    lane_row = lax.broadcasted_iota(jnp.int32, (128, 128), 0)
    lane_column = lax.broadcasted_iota(jnp.int32, (128, 128), 1)
    chosen = (
        (lane_row // 64 == (lane_column % 16) // 8) & ((lane_row % 64) // 16 == lane_column // 16)
    ).astype(bf16)
    right_row = lax.broadcasted_iota(jnp.int32, (8, 128), 0) == lanes % 8
    await_all(0, out_send, out_recv)
    running = jnp.zeros((8, 128), f32)
    inner = []
    for block in range(nctx):
        end = out_recv[block, 0:8]
        back_send[block, 0:8] = running
        inner.append(running + end * inverse_own)
        running = running * block_own + end
    running = jnp.zeros((8, 128), f32)
    owned = jnp.zeros((8, 128), f32)
    gradient = jnp.zeros((1, 128), f32)
    for block in range(nctx - 1, -1, -1):
        start = out_recv[block, 8:16]
        back_send[block, 8:16] = running
        running = running * block_own + start
        owned += start * inner[block]
        gradient += out_recv[block, 16:17]
    send_all(1, back_send, back_recv)
    back_recv[me] = back_send[me]
    high, low = split(owned * step_own)
    summed = jnp.dot(high, chosen, preferred_element_type=f32) + jnp.dot(low, chosen, preferred_element_type=f32)
    gradient += jnp.sum(jnp.where(right_row & lower, summed, 0.0), axis=0, keepdims=True)
    gradient = gradient * scale
    o_send[...] = gradient
    o_recv[mine * nctx + me] = gradient

    def gradient_copy(offset, step):
        part, there = lax.rem(mine + offset, ndp), lax.rem(me + step, nctx)
        return pltpu.make_async_remote_copy(
            src_ref=o_send,
            dst_ref=o_recv.at[mine * nctx + me],
            send_sem=osend_sem,
            recv_sem=orecv_sem,
            device_id={"dp": part, "ctx": there},
            device_id_type=MESH,
        )

    def send_gradients(count, carried):
        for offset in range(ndp):
            gradient_copy(offset, far_first(count)).start()
        return carried

    if COMM:
        pl.semaphore_wait(ring_sem, ndp - 1)
        lax.fori_loop(0, nctx - 1, send_gradients, 0)
        for offset in range(1, ndp):
            gradient_copy(offset, 0).start()

    for sent in ((0, out_send, out_recv), (1, back_send, back_recv)):
        await_sent(*sent)
    await_all(1, back_send, back_recv)
    carried_ref[0] = (unpack(back_recv, 0) + states[0] * coefs[2]) * coefs[1]
    carried_ref[1] = (unpack(back_recv, 8) + states[1] * coefs[2]) * coefs[1]

    def finish(q, piece):
        product = times((wf_ref[0, :, piece], wf_ref[1, :, piece]), split(on_blocks(carried_ref[0, :, piece])))
        y_ref[:, piece] = (ylocal[:, piece] + product).astype(bf16)
        product = times((wb_ref[0, :, piece], wb_ref[1, :, piece]), split(on_blocks(carried_ref[1, :, piece])))
        z_ref[:, piece] = (zlocal[:, piece] + product).astype(bf16)

    by_tiles(finish)
    if COMM:
        others = o_recv.at[pl.ds(0, ndp * nctx - 1)]
        everything = pltpu.make_async_remote_copy(
            src_ref=others,
            dst_ref=others,
            send_sem=osend_sem,
            recv_sem=orecv_sem,
            device_id={"ctx": lax.rem(me + 1, nctx)},
            device_id_type=MESH,
        )
        everything.wait_send()
        everything.wait_recv()
    for owner in range(nctx):
        total = o_recv[owner]
        for part in range(1, ndp):
            total += o_recv[part * nctx + owner]
        final_ref[owner] = total


def last_kernel(y_in, z_in, final_ref, weight_ref, chosen_ref, y_hbm, z_hbm, gres_hbm, gskip_hbm, gres_ref, gskip_ref, sem):
    channels = y_in.shape[1]
    modes = weight_ref.shape[0]
    copies = []

    def send(source, target):
        copies.append(pltpu.make_async_copy(source, target, sem.at[len(copies)]))
        copies[-1].start()

    send(y_in, y_hbm.at[0])
    send(z_in, z_hbm.at[0])
    lower_row = lax.broadcasted_iota(jnp.int32, (1, 128), 1) < 64
    final = []
    for pair in range(channels // 128):
        first, second = final_ref[2 * pair], final_ref[2 * pair + 1]
        gskip_ref[:, 128 * pair : 128 * pair + 128] = jnp.where(lower_row, pltpu.roll(first, 64, 1), second)
        final.append(jnp.where(lower_row, first, pltpu.roll(second, 64, 1)))
    send(gskip_ref, gskip_hbm)
    own_mode = (
        lax.broadcasted_iota(jnp.int32, (modes, channels), 1) % modes == lax.broadcasted_iota(jnp.int32, (modes, channels), 0)
    )
    high, low = split(jnp.where(own_mode, jnp.concatenate(final, axis=1), 0.0))
    chosen = chosen_ref[...]
    by_group = jnp.dot(high, chosen, preferred_element_type=f32) + jnp.dot(low, chosen, preferred_element_type=f32)
    gres_ref[...] = by_group * weight_ref[...]
    send(gres_ref, gres_hbm)
    for copy in copies:
        copy.wait()


def transform(rows):
    frequency = np.pi * (2 * np.arange(rows // 2) + 1) / rows
    angle = frequency[:, None] * np.arange(rows)[None, :]
    forward = np.concatenate([np.cos(angle), -np.sin(angle)], axis=0)
    high = forward.astype(jnp.bfloat16)
    low = (forward - high.astype(np.float64)).astype(jnp.bfloat16)
    both = np.stack([high, low])
    back = (both.transpose(0, 2, 1).astype(np.float32) * (2.0 / rows)).astype(jnp.bfloat16)
    trig = np.zeros((rows // 2, 128), np.float32)
    trig[:, 0] = 2.0 * np.sin(frequency / 2.0) ** 2
    trig[:, 1] = np.sin(frequency)
    return jnp.asarray(both), jnp.asarray(back), jnp.asarray(trig)


def shards(nctx, ndp, inputs, cotangent, residues, decay_rates, skip_gain):
    _, rows, channels = inputs.shape
    groups, modes = residues.shape
    sizes = (nctx, ndp, rows, channels, groups, modes, 1.0 / math.sqrt(rows * nctx * ndp))
    forward, back, trig = transform(rows)
    hbm = pl.BlockSpec(memory_space=pltpu.HBM)
    vmem = pl.BlockSpec(memory_space=pltpu.VMEM)
    wide = (1, rows, channels)
    parts = pl.pallas_call(
        functools.partial(kernel, sizes),
        out_shape=(
            jax.ShapeDtypeStruct((rows, channels), bf16),
            jax.ShapeDtypeStruct((rows, channels), bf16),
            jax.ShapeDtypeStruct((nctx, 1, 128), f32),
            jax.ShapeDtypeStruct((modes, groups), f32),
            jax.ShapeDtypeStruct((channels, groups), bf16),
        ),
        in_specs=[hbm] * 8,
        out_specs=(vmem,) * 5,
        scratch_shapes=[
            pltpu.VMEM((rows, channels), bf16),
            pltpu.VMEM((rows, channels), bf16),
            pltpu.VMEM((modes, groups), f32),
            pltpu.VMEM((modes, groups), f32),
            pltpu.VMEM((1, channels), f32),
            pltpu.VMEM((2, rows, rows), bf16),
            pltpu.VMEM((2, rows, rows), bf16),
            pltpu.VMEM((rows // 2, 128), f32),
            pltpu.VMEM((2, rows, channels), bf16),
            pltpu.VMEM((2, rows, channels), bf16),
            pltpu.VMEM((rows, channels), f32),
            pltpu.VMEM((rows, channels), f32),
            pltpu.VMEM((rows, channels), f32),
            pltpu.VMEM((rows, channels), f32),
            pltpu.VMEM((rows, channels), f32),
            pltpu.VMEM((1, channels), f32),
            pltpu.VMEM((2, modes, channels), f32),
            pltpu.VMEM((3, modes, channels), f32),
            pltpu.VMEM((2, modes, channels), f32),
            pltpu.VMEM((3, nctx, 8, 128), f32),
            pltpu.VMEM((nctx, 17, 128), f32),
            pltpu.VMEM((nctx, 17, 128), f32),
            pltpu.VMEM((nctx, 16, 128), f32),
            pltpu.VMEM((nctx, 16, 128), f32),
            pltpu.VMEM((1, 128), f32),
            pltpu.VMEM((ndp * nctx, 1, 128), f32),
            pltpu.SemaphoreType.DMA((8,)),
            pltpu.SemaphoreType.DMA((2, nctx)),
            pltpu.SemaphoreType.DMA((2, nctx)),
            pltpu.SemaphoreType.DMA,
            pltpu.SemaphoreType.DMA,
            pltpu.SemaphoreType.REGULAR,
        ],
        compiler_params=pltpu.CompilerParams(collective_id=0, has_side_effects=True, vmem_limit_bytes=32 * 1024 * 1024),
        name="hyena",
    )(*[pltpu.with_memory_space_constraint(a, pltpu.HBM) for a in (inputs, cotangent, residues.T, decay_rates.T, skip_gain.reshape(1, channels), forward, back, trig)])
    outputs, grad_inputs, grad_residues, grad_skip = pl.pallas_call(
        last_kernel,
        out_shape=(
            jax.ShapeDtypeStruct(wide, bf16),
            jax.ShapeDtypeStruct(wide, bf16),
            jax.ShapeDtypeStruct((modes, groups), f32),
            jax.ShapeDtypeStruct((1, channels), f32),
        ),
        in_specs=[vmem] * 5,
        out_specs=(hbm,) * 4,
        scratch_shapes=[
            pltpu.VMEM((modes, groups), f32),
            pltpu.VMEM((1, channels), f32),
            pltpu.SemaphoreType.DMA((4,)),
        ],
        compiler_params=pltpu.CompilerParams(vmem_limit_bytes=32 * 1024 * 1024),
        name="last",
    )(*parts)
    return outputs, grad_inputs, grad_residues.T, grad_skip.reshape(channels)


def solution(mesh):
    placed = (P("dp", "ctx", "tp"), P("dp", "ctx", "tp"), P("tp", None), P("tp", None), P("tp"))
    return jax.shard_map(
        functools.partial(shards, mesh.shape["ctx"], mesh.shape["dp"]),
        mesh=mesh,
        in_specs=placed,
        out_specs=(P("dp", "ctx", "tp"), P("dp", "ctx", "tp"), P("tp", None), P("tp")),
        check_vma=False,
    )
```

```python
import functools
import math

import jax
import jax.numpy as jnp
import numpy as np
from jax import lax
from jax.experimental import pallas as pl
from jax.experimental.pallas import tpu as pltpu
from jax.sharding import PartitionSpec as P

MESH = pl.DeviceIdType.MESH
highest = lax.Precision.HIGHEST
f32 = jnp.float32
bf16 = jnp.bfloat16
COMM = True
UNROLL = True


def split(value):
    high = value.astype(bf16)
    return high, (value - high.astype(f32)).astype(bf16)


def times(left, right):
    total = jnp.dot(left[0], right[0], preferred_element_type=f32)
    total += jnp.dot(left[0], right[1], preferred_element_type=f32)
    return total + jnp.dot(left[1], right[0], preferred_element_type=f32)


def times_row(left, right):
    return jnp.dot(left, right, precision=highest, preferred_element_type=f32)


def split_store(target, piece, value):
    high, low = split(value)
    target[0, :, piece] = high
    target[1, :, piece] = low


def same_block(shape):
    return lax.broadcasted_iota(jnp.int32, shape, 0) // 16 == lax.broadcasted_iota(jnp.int32, shape, 1) // 16


def on_blocks(piece):
    return jnp.where(same_block((256, 256)), jnp.concatenate([piece] * 16, axis=0), 0.0)


def off_blocks(array):
    return jnp.sum(jnp.where(same_block((256, 256)), array, 0.0).reshape(16, 16, 256), axis=0)


def kernel(sizes, x_hbm, d_hbm, res_hbm, rate_hbm, skip_hbm, fwd_hbm, inv_hbm, trig_hbm,
           y_ref, z_ref, final_ref, weight_ref, chosen_ref,
           x_ref, d_ref, res_ref, rate_ref, skip_ref, fwd_ref, inv_ref, trig_ref,
           wf_ref, wb_ref, h_ref, x_hat, d_hat, ylocal, zlocal, rate_row, states, coefs, carried_ref, packs,
           out_send, out_recv, back_send, back_recv, p_send, from_dp, o_send, o_recv,
           load_sem, send_sem, recv_sem, psend_sem, precv_sem):
    nctx, ndp, rows, channels, groups, modes, scale = sizes
    half = rows // 2
    tiles = channels // 256
    me = lax.axis_index("ctx")
    mine = lax.axis_index("dp")

    barrier = pltpu.get_barrier_semaphore()

    def far_first(count):
        return nctx // 2 + jnp.where(count % 2 == 1, -((count + 1) // 2), count // 2)

    def greet(count, carried):
        step = far_first(count)
        pl.semaphore_signal(barrier, inc=1, device_id={"ctx": lax.rem(me + step, nctx)}, device_id_type=MESH)
        return carried

    if COMM:
        lax.fori_loop(0, nctx - 1, greet, 0)
        for step in range(1, ndp):
            pl.semaphore_signal(barrier, inc=1, device_id={"dp": lax.rem(mine + step, ndp)}, device_id_type=MESH)

    loads = [
        pltpu.make_async_copy(source, target, load_sem.at[number])
        for number, (source, target) in enumerate(
            [(rate_hbm, rate_ref), (res_hbm, res_ref), (x_hbm.at[0], x_ref), (d_hbm.at[0], d_ref), (trig_hbm, trig_ref),
             (fwd_hbm, fwd_ref), (inv_hbm, inv_ref), (skip_hbm, skip_ref)]
        )
    ]
    for load in loads:
        load.start()

    lanes = lax.broadcasted_iota(jnp.int32, (8, 128), 1)
    lower = lanes < 64
    lower_row = lax.broadcasted_iota(jnp.int32, (1, 128), 1) < 64
    positions = lax.broadcasted_iota(jnp.int32, (rows, 1), 0).astype(f32)
    own_group = (
        lax.broadcasted_iota(jnp.int32, (groups, channels), 1) // modes == lax.broadcasted_iota(jnp.int32, (groups, channels), 0)
    ).astype(f32)
    own_mode = (
        lax.broadcasted_iota(jnp.int32, (modes, channels), 1) % modes == lax.broadcasted_iota(jnp.int32, (modes, channels), 0)
    )

    def by_tiles(body):
        if UNROLL:
            for q in range(tiles):
                body(q, slice(256 * q, 256 * q + 256))
        else:
            def turn(q, carried):
                body(q, pl.ds(pl.multiple_of(q * 256, 256), 256))
                return carried

            lax.fori_loop(0, tiles, turn, 0)

    def pack(array, target, top):
        for pair in range(nctx // 2):
            low = array[0:8, 128 * pair : 128 * pair + 128]
            high = array[8:16, 128 * pair : 128 * pair + 128]
            target[2 * pair, top : top + 8] = jnp.where(lower, low, pltpu.roll(high, 64, 1))
            target[2 * pair + 1, top : top + 8] = jnp.where(lower, pltpu.roll(low, 64, 1), high)

    def unpack(source, top):
        lows, highs = [], []
        for pair in range(nctx // 2):
            first, second = source[2 * pair, top : top + 8], source[2 * pair + 1, top : top + 8]
            lows.append(jnp.where(lower, first, pltpu.roll(second, 64, 1)))
            highs.append(jnp.where(lower, pltpu.roll(first, 64, 1), second))
        return jnp.concatenate([jnp.concatenate(lows, axis=1), jnp.concatenate(highs, axis=1)], axis=0)

    def transposed_dot(left, right):
        return lax.dot_general(left, right, (((0,), (0,)), ((), ())), preferred_element_type=f32)

    loads[0].wait()
    rate_wide = times_row(rate_ref[...], own_group)
    rate_row[...] = jnp.sum(jnp.where(own_mode, rate_wide, 0.0), axis=0, keepdims=True)

    def end_states(q, piece):
        split_store(wb_ref, piece, jnp.exp(-rate_row[:, piece] * (rows - 1.0 - positions)))
        full = transposed_dot(wb_ref[0, :, piece], x_ref[:, piece]) + transposed_dot(wb_ref[1, :, piece], x_ref[:, piece])
        states[0, :, piece] = off_blocks(full)

    def start_states(q, piece):
        split_store(wf_ref, piece, jnp.exp(-rate_row[:, piece] * positions))
        full = transposed_dot(wf_ref[0, :, piece], d_ref[:, piece]) + transposed_dot(wf_ref[1, :, piece], d_ref[:, piece])
        states[1, :, piece] = off_blocks(full)

    loads[2].wait()
    by_tiles(end_states)
    pack(states[0], out_send, 0)
    loads[3].wait()
    by_tiles(start_states)
    pack(states[1], out_send, 8)

    def state_copy(there, kind, send, recv, slot_there):
        return pltpu.make_async_remote_copy(
            src_ref=send.at[there] if kind < 2 else send,
            dst_ref=recv.at[slot_there],
            send_sem=send_sem.at[kind, there],
            recv_sem=recv_sem.at[kind, slot_there],
            device_id={"ctx": there},
            device_id_type=MESH,
        )

    def over_peers(body):
        def turn(count, carried):
            body(lax.rem(me + far_first(nctx - 2 - count), nctx))
            return carried

        if COMM:
            lax.fori_loop(0, nctx - 1, turn, 0)

    def send_all(kind, send, recv):
        def turn(count, carried):
            state_copy(lax.rem(me + far_first(count), nctx), kind, send, recv, me).start()
            return carried

        if COMM:
            lax.fori_loop(0, nctx - 1, turn, 0)

    def await_all(kind, send, recv):
        over_peers(lambda origin: state_copy(origin, kind, send, recv, origin).wait_recv())

    def await_sent(kind, send, recv):
        over_peers(lambda origin: state_copy(origin, kind, send, recv, origin).wait_send())

    for load in loads[4:]:
        load.wait()

    def spectra(q, piece):
        step_piece = jnp.exp(-rate_row[:, piece])
        less_cos, sine = trig_ref[:, 0:1], trig_ref[:, 1:2]
        rest = 1.0 - step_piece
        near = step_piece * less_cos
        below = 1.0 / (rest * rest + 2.0 * near)
        h_ref[0:half, piece] = (rest + near) * below
        h_ref[half:rows, piece] = (-step_piece * sine) * below
        x_piece, d_piece = x_ref[:, piece], d_ref[:, piece]
        x_new = jnp.dot(fwd_ref[0], x_piece, preferred_element_type=f32) + jnp.dot(fwd_ref[1], x_piece, preferred_element_type=f32)
        d_new = jnp.dot(fwd_ref[0], d_piece, preferred_element_type=f32) + jnp.dot(fwd_ref[1], d_piece, preferred_element_type=f32)
        x_hat[:, piece] = x_new
        d_hat[:, piece] = d_new
        x_re, x_im, d_re, d_im = x_new[0:half], x_new[half:rows], d_new[0:half], d_new[half:rows]
        cross = jnp.concatenate([d_re * x_re + d_im * x_im, d_im * x_re - d_re * x_im], axis=0)
        cross_high, cross_low = split(cross)
        ones = same_block((256, 256)).astype(bf16)
        grouped = jnp.dot(cross_high, ones, preferred_element_type=f32) + jnp.dot(cross_low, ones, preferred_element_type=f32)
        grad_piece = jnp.sum(grouped * h_ref[:, piece], axis=0, keepdims=True) * (2.0 / rows)
        skip_piece = jnp.sum(x_piece.astype(f32) * d_piece.astype(f32), axis=0, keepdims=True)
        for part in range(2):
            pair = 2 * q + part
            grad_row, skip_row = grad_piece[:, 128 * part : 128 * part + 128], skip_piece[:, 128 * part : 128 * part + 128]
            out_send[2 * pair, 16:17] = jnp.where(lower_row, grad_row, pltpu.roll(skip_row, 64, 1))
            out_send[2 * pair + 1, 16:17] = jnp.where(lower_row, pltpu.roll(grad_row, 64, 1), skip_row)

    by_tiles(spectra)

    if COMM:
        pl.semaphore_wait(barrier, nctx - 1 + ndp - 1)
    send_all(0, out_send, out_recv)
    out_recv[me] = out_send[me]

    loads[1].wait()
    coefs[0] = times_row(res_ref[...], own_group) * jnp.sqrt(1.0 - jnp.exp(-2.0 * rate_wide))
    step_wide = jnp.exp(-rate_wide)
    block_wide = jnp.exp(-rate_wide * float(rows))
    inverse_wide = 1.0 / (1.0 + block_wide)
    coefs[1] = coefs[0] * step_wide
    coefs[2] = inverse_wide
    pack(block_wide, packs.at[0], 0)
    pack(inverse_wide, packs.at[1], 0)
    pack(step_wide, packs.at[2], 0)

    weight_ref[...] = jnp.sqrt(1.0 - jnp.exp(-2.0 * rate_ref[...]))
    chosen_ref[...] = (
        lax.broadcasted_iota(jnp.int32, (channels, groups), 0) // modes == lax.broadcasted_iota(jnp.int32, (channels, groups), 1)
    ).astype(bf16)

    def own_part(q, piece):
        response = times(split(h_ref[:, piece]), split(on_blocks(coefs[0, :, piece])))
        f_re, f_im = response[0:half], response[half:rows]
        x_re, x_im, d_re, d_im = x_hat[0:half, piece], x_hat[half:rows, piece], d_hat[0:half, piece], d_hat[half:rows, piece]
        skip = skip_ref[:, piece]
        y_hat = jnp.concatenate([f_re * x_re - f_im * x_im, f_re * x_im + f_im * x_re], axis=0)
        ylocal[:, piece] = times((inv_ref[0], inv_ref[1]), split(y_hat)) + skip * x_ref[:, piece].astype(f32)
        z_hat = jnp.concatenate([f_re * d_re + f_im * d_im, f_re * d_im - f_im * d_re], axis=0)
        zlocal[:, piece] = times((inv_ref[0], inv_ref[1]), split(z_hat)) + skip * d_ref[:, piece].astype(f32)

    by_tiles(own_part)

    block_own, inverse_own, step_own = packs[0, me], packs[1, me], packs[2, me]
    lane_row = lax.broadcasted_iota(jnp.int32, (128, 128), 0)
    lane_column = lax.broadcasted_iota(jnp.int32, (128, 128), 1)
    chosen = (
        (lane_row // 64 == (lane_column % 16) // 8) & ((lane_row % 64) // 16 == lane_column // 16)
    ).astype(bf16)
    right_row = lax.broadcasted_iota(jnp.int32, (8, 128), 0) == lanes % 8
    await_all(0, out_send, out_recv)
    running = jnp.zeros((8, 128), f32)
    inner = []
    for block in range(nctx):
        end = out_recv[block, 0:8]
        back_send[block, 0:8] = running
        inner.append(running + end * inverse_own)
        running = running * block_own + end
    running = jnp.zeros((8, 128), f32)
    owned = jnp.zeros((8, 128), f32)
    gradient = jnp.zeros((1, 128), f32)
    for block in range(nctx - 1, -1, -1):
        start = out_recv[block, 8:16]
        back_send[block, 8:16] = running
        running = running * block_own + start
        owned += start * inner[block]
        gradient += out_recv[block, 16:17]
    high, low = split(owned * step_own)
    summed = jnp.dot(high, chosen, preferred_element_type=f32) + jnp.dot(low, chosen, preferred_element_type=f32)
    gradient += jnp.sum(jnp.where(right_row & lower, summed, 0.0), axis=0, keepdims=True)
    p_send[...] = gradient

    def dp_copy(step, here):
        there = lax.rem(mine + step, ndp)
        slot = there if here else mine
        return pltpu.make_async_remote_copy(
            src_ref=p_send,
            dst_ref=from_dp.at[slot],
            send_sem=psend_sem.at[there],
            recv_sem=precv_sem.at[slot],
            device_id={"dp": there},
            device_id_type=MESH,
        )

    if COMM:
        for step in range(1, ndp):
            dp_copy(step, False).start()
    send_all(1, back_send, back_recv)
    back_recv[me] = back_send[me]
    from_dp[mine] = gradient
    if COMM:
        for step in range(1, ndp):
            dp_copy(step, True).wait_recv()
    gradient = from_dp[0]
    for other in range(1, ndp):
        gradient += from_dp[other]
    o_send[...] = gradient * scale
    send_all(2, o_send, o_recv)
    o_recv[me] = gradient * scale

    await_sent(0, out_send, out_recv)
    await_sent(1, back_send, back_recv)
    await_all(1, back_send, back_recv)
    carried_ref[0] = (unpack(back_recv, 0) + states[0] * coefs[2]) * coefs[1]
    carried_ref[1] = (unpack(back_recv, 8) + states[1] * coefs[2]) * coefs[1]

    def finish(q, piece):
        product = times((wf_ref[0, :, piece], wf_ref[1, :, piece]), split(on_blocks(carried_ref[0, :, piece])))
        y_ref[:, piece] = (ylocal[:, piece] + product).astype(bf16)
        product = times((wb_ref[0, :, piece], wb_ref[1, :, piece]), split(on_blocks(carried_ref[1, :, piece])))
        z_ref[:, piece] = (zlocal[:, piece] + product).astype(bf16)

    by_tiles(finish)
    await_sent(2, o_send, o_recv)
    if COMM:
        for step in range(1, ndp):
            dp_copy(step, True).wait_send()
    await_all(2, o_send, o_recv)
    final_ref[...] = o_recv[...]


def last_kernel(y_in, z_in, final_ref, weight_ref, chosen_ref, y_hbm, z_hbm, gres_hbm, gskip_hbm, gres_ref, gskip_ref, sem):
    channels = y_in.shape[1]
    modes = weight_ref.shape[0]
    copies = []

    def send(source, target):
        copies.append(pltpu.make_async_copy(source, target, sem.at[len(copies)]))
        copies[-1].start()

    send(y_in, y_hbm.at[0])
    send(z_in, z_hbm.at[0])
    lower_row = lax.broadcasted_iota(jnp.int32, (1, 128), 1) < 64
    final = []
    for pair in range(channels // 128):
        first, second = final_ref[2 * pair], final_ref[2 * pair + 1]
        gskip_ref[:, 128 * pair : 128 * pair + 128] = jnp.where(lower_row, pltpu.roll(first, 64, 1), second)
        final.append(jnp.where(lower_row, first, pltpu.roll(second, 64, 1)))
    send(gskip_ref, gskip_hbm)
    own_mode = (
        lax.broadcasted_iota(jnp.int32, (modes, channels), 1) % modes == lax.broadcasted_iota(jnp.int32, (modes, channels), 0)
    )
    high, low = split(jnp.where(own_mode, jnp.concatenate(final, axis=1), 0.0))
    chosen = chosen_ref[...]
    by_group = jnp.dot(high, chosen, preferred_element_type=f32) + jnp.dot(low, chosen, preferred_element_type=f32)
    gres_ref[...] = by_group * weight_ref[...]
    send(gres_ref, gres_hbm)
    for copy in copies:
        copy.wait()


def transform(rows):
    frequency = np.pi * (2 * np.arange(rows // 2) + 1) / rows
    angle = frequency[:, None] * np.arange(rows)[None, :]
    forward = np.concatenate([np.cos(angle), -np.sin(angle)], axis=0)
    high = forward.astype(jnp.bfloat16)
    low = (forward - high.astype(np.float64)).astype(jnp.bfloat16)
    both = np.stack([high, low])
    back = (both.transpose(0, 2, 1).astype(np.float32) * (2.0 / rows)).astype(jnp.bfloat16)
    trig = np.zeros((rows // 2, 128), np.float32)
    trig[:, 0] = 2.0 * np.sin(frequency / 2.0) ** 2
    trig[:, 1] = np.sin(frequency)
    return jnp.asarray(both), jnp.asarray(back), jnp.asarray(trig)


def shards(nctx, ndp, inputs, cotangent, residues, decay_rates, skip_gain):
    _, rows, channels = inputs.shape
    groups, modes = residues.shape
    sizes = (nctx, ndp, rows, channels, groups, modes, 1.0 / math.sqrt(rows * nctx * ndp))
    forward, back, trig = transform(rows)
    hbm = pl.BlockSpec(memory_space=pltpu.HBM)
    vmem = pl.BlockSpec(memory_space=pltpu.VMEM)
    wide = (1, rows, channels)
    parts = pl.pallas_call(
        functools.partial(kernel, sizes),
        out_shape=(
            jax.ShapeDtypeStruct((rows, channels), bf16),
            jax.ShapeDtypeStruct((rows, channels), bf16),
            jax.ShapeDtypeStruct((nctx, 1, 128), f32),
            jax.ShapeDtypeStruct((modes, groups), f32),
            jax.ShapeDtypeStruct((channels, groups), bf16),
        ),
        in_specs=[hbm] * 8,
        out_specs=(vmem,) * 5,
        scratch_shapes=[
            pltpu.VMEM((rows, channels), bf16),
            pltpu.VMEM((rows, channels), bf16),
            pltpu.VMEM((modes, groups), f32),
            pltpu.VMEM((modes, groups), f32),
            pltpu.VMEM((1, channels), f32),
            pltpu.VMEM((2, rows, rows), bf16),
            pltpu.VMEM((2, rows, rows), bf16),
            pltpu.VMEM((rows // 2, 128), f32),
            pltpu.VMEM((2, rows, channels), bf16),
            pltpu.VMEM((2, rows, channels), bf16),
            pltpu.VMEM((rows, channels), f32),
            pltpu.VMEM((rows, channels), f32),
            pltpu.VMEM((rows, channels), f32),
            pltpu.VMEM((rows, channels), f32),
            pltpu.VMEM((rows, channels), f32),
            pltpu.VMEM((1, channels), f32),
            pltpu.VMEM((2, modes, channels), f32),
            pltpu.VMEM((3, modes, channels), f32),
            pltpu.VMEM((2, modes, channels), f32),
            pltpu.VMEM((3, nctx, 8, 128), f32),
            pltpu.VMEM((nctx, 17, 128), f32),
            pltpu.VMEM((nctx, 17, 128), f32),
            pltpu.VMEM((nctx, 16, 128), f32),
            pltpu.VMEM((nctx, 16, 128), f32),
            pltpu.VMEM((1, 128), f32),
            pltpu.VMEM((ndp, 1, 128), f32),
            pltpu.VMEM((1, 128), f32),
            pltpu.VMEM((nctx, 1, 128), f32),
            pltpu.SemaphoreType.DMA((8,)),
            pltpu.SemaphoreType.DMA((3, nctx)),
            pltpu.SemaphoreType.DMA((3, nctx)),
            pltpu.SemaphoreType.DMA((ndp,)),
            pltpu.SemaphoreType.DMA((ndp,)),
        ],
        compiler_params=pltpu.CompilerParams(collective_id=0, has_side_effects=True, vmem_limit_bytes=32 * 1024 * 1024),
        name="hyena",
    )(*[pltpu.with_memory_space_constraint(a, pltpu.HBM) for a in (inputs, cotangent, residues.T, decay_rates.T, skip_gain.reshape(1, channels), forward, back, trig)])
    outputs, grad_inputs, grad_residues, grad_skip = pl.pallas_call(
        last_kernel,
        out_shape=(
            jax.ShapeDtypeStruct(wide, bf16),
            jax.ShapeDtypeStruct(wide, bf16),
            jax.ShapeDtypeStruct((modes, groups), f32),
            jax.ShapeDtypeStruct((1, channels), f32),
        ),
        in_specs=[vmem] * 5,
        out_specs=(hbm,) * 4,
        scratch_shapes=[
            pltpu.VMEM((modes, groups), f32),
            pltpu.VMEM((1, channels), f32),
            pltpu.SemaphoreType.DMA((4,)),
        ],
        compiler_params=pltpu.CompilerParams(vmem_limit_bytes=32 * 1024 * 1024),
        name="last",
    )(*parts)
    return outputs, grad_inputs, grad_residues.T, grad_skip.reshape(channels)


def solution(mesh):
    placed = (P("dp", "ctx", "tp"), P("dp", "ctx", "tp"), P("tp", None), P("tp", None), P("tp"))
    return jax.shard_map(
        functools.partial(shards, mesh.shape["ctx"], mesh.shape["dp"]),
        mesh=mesh,
        in_specs=placed,
        out_specs=(P("dp", "ctx", "tp"), P("dp", "ctx", "tp"), P("tp", None), P("tp")),
        check_vma=False,
    )
```
